32 devices in a mesh: dp: 4 (over y, core), sq: 8 (over z, x).
Axes of the slice: x: 2, y: 2, z: 4, core: 2. Of those that a mesh axis runs over, the one named last changes fastest.
Arguments:
- tokens: bfloat16 [8, 2048, 512], P('dp', 'sq'), may hold values from -6 to 6
- lengths: int32 [8, 4], P('dp'), may hold values from 1 to 2045, as said below
- key_mask: int32 [8, 2048], P('dp'), may hold values 0 or 1
- halt_steps: int32 [8, 2048], P('dp', 'sq'), may hold values from 1 to 3
- query_weight: bfloat16 [512, 512], replicated, may hold values from -0.5 to 0.5
- query_bias: bfloat16 [512], replicated, may hold values from -1.796875 to 1.796875
- key_weight: bfloat16 [512, 512], replicated, may hold values from -0.25 to 0.25
- value_weight: bfloat16 [512, 512], replicated, may hold values from -0.25 to 0.25
- value_bias: bfloat16 [512], replicated, may hold values from -1.796875 to 1.796875
- out_weight: bfloat16 [512, 512], replicated, may hold values from -1 to 1
- out_bias: bfloat16 [512], replicated, may hold values from -1.796875 to 1.796875
- first_gain: bfloat16 [512], replicated, may hold values from 0.5 to 1.5
- first_shift: bfloat16 [512], replicated, may hold values from -1.796875 to 1.796875
- second_gain: bfloat16 [512], replicated, may hold values from 0.5 to 1.5
- second_shift: bfloat16 [512], replicated, may hold values from -1.796875 to 1.796875
- up_weight: bfloat16 [512, 2048], P(None, 'sq'), may hold values from -0.25 to 0.25
- up_bias: bfloat16 [2048], P('sq'), may hold values from -3 to 3
- down_weight: bfloat16 [2048, 512], P('sq'), may hold values from -0.1875 to 0.1875
- down_bias: bfloat16 [512], replicated, may hold values from -1.796875 to 1.796875
- halt_weight: float32 [512], replicated, may hold values from -0.25 to 0.25
- halt_bias: float32 [1], replicated, may hold values from -2 to 2
- cotangent: bfloat16 [8, 2048, 512], P('dp', 'sq'), may hold values from -6 to 6
Outputs:
- acted: bfloat16 [8, 2048, 512], P('dp', 'sq')
- grad_tokens: float32 [8, 2048, 512], P('dp', 'sq')
- grad_query_weight: float32 [512, 512], replicated
- grad_query_bias: float32 [512], replicated
- grad_key_weight: float32 [512, 512], replicated
- grad_value_weight: float32 [512, 512], replicated
- grad_value_bias: float32 [512], replicated
- grad_out_weight: float32 [512, 512], replicated
- grad_out_bias: float32 [512], replicated
- grad_first_gain: float32 [512], replicated
- grad_first_shift: float32 [512], replicated
- grad_second_gain: float32 [512], replicated
- grad_second_shift: float32 [512], replicated
- grad_up_weight: float32 [512, 2048], P(None, 'sq')
- grad_up_bias: float32 [2048], P('sq')
- grad_down_weight: float32 [2048, 512], P('sq')
- grad_down_bias: float32 [512], replicated
- grad_halt_weight: float32 [512], replicated
- grad_halt_bias: float32 [1], replicated
The draws below stay inside these ranges and needn't reach their ends.
Inputs may be any that keep to these rules, and one draw needn't show every extreme that they name: Each row's 4 lengths sum to 2048; one of them is longer than 1792, the others together are shorter than 256. `key_mask`: 1 marks a position that may be attended; a position always attends itself.
All inputs are finite; a program needn't handle non-finite values. No bound on the sum of `key_mask` on one device may be relied on, other than what follows from the above.
Results may differ from the reference program's by a relative error of at most 0.019.
Values may be sent and summed in bfloat16 or wider, within the bound.
No kernel may reach another device: no remote copies, remote signals or barrier semaphores. Data moves between devices by JAX's collectives and lax.ppermute only.
A program may use at most 512 MiB of HBM per device.

```python
import math
import jax
import jax.numpy as jnp
from jax import lax

D = 512
HEADS = 8
HEAD = 64
FF = 2048
STEPS = 3
DOCS = 4
ROW_LEN = 2048
SEQ_DEV = 256
ROWS = 8


def draw_lengths(key, part):
    key = jax.random.fold_in(key, 11)
    short_key, place_key = jax.random.split(key)
    short_top = max(SEQ_DEV // (DOCS - 1), 1)
    shorts = jax.random.randint(short_key, (ROWS, DOCS - 1), 1, short_top + 1, dtype=jnp.int32)
    shorts = shorts.at[:, 0].set(1)
    shorts = shorts.at[0, :].set(1)
    longest = (ROW_LEN - jnp.sum(shorts, axis=1)).astype(jnp.int32)
    place = jax.random.randint(place_key, (ROWS, 1), 0, DOCS, dtype=jnp.int32)
    columns = jnp.arange(DOCS, dtype=jnp.int32)[None, :]
    picked = jnp.minimum(columns - (columns > place).astype(jnp.int32), DOCS - 2)
    chosen = jnp.take_along_axis(shorts, picked, axis=1)
    return jnp.where(columns == place, longest[:, None], chosen).astype(jnp.int32)


def place_ends(result, rng, smallest, largest):
    shape = result.shape
    spot = [jax.random.randint(jax.random.fold_in(rng, axis), (), 0, shape[axis]) for axis in range(len(shape))]
    result = result.at[tuple(spot)].set(smallest)
    longest = shape.index(max(shape))
    spot[longest] = (spot[longest] + 1) % shape[longest]
    return result.at[tuple(spot)].set(largest)


def shard_levels(rng, shape, cuts, least, high):
    factor_of, own = 1.0, jax.random.fold_in(rng, 6)
    for dim, parts in cuts:
        steps = jnp.exp(jax.random.uniform(jax.random.fold_in(own, dim), (parts,), jnp.float32, least / len(cuts), high / len(cuts)))
        factor_of = factor_of * jnp.repeat(steps, shape[dim] // parts).reshape([-1 if axis == dim else 1 for axis in range(len(shape))])
    return factor_of


def gaussian(key, extent, width, limit, pieces=(), kind=jnp.bfloat16):
    values = width * jax.random.normal(key, extent, jnp.float32)
    if pieces:
        values = values * shard_levels(key, extent, pieces, -0.22, 0.18)
    return jnp.clip(values, -limit, limit).astype(kind)


def setup_inputs(seed: int = 0) -> dict:
    streams_of = jax.random.split(jax.random.key(seed), 23)
    return {
        "tokens": gaussian(streams_of[0], (ROWS, ROW_LEN, D), 1.0, 6.0, ((0, 4), (1, 8))),
        "lengths": draw_lengths(jax.random.fold_in(streams_of[22], 71), 0),
        "key_mask": place_ends((jax.random.randint(streams_of[2], (ROWS, ROW_LEN), 0, 8) < 7).astype(jnp.int32), jax.random.fold_in(streams_of[2], 1), 0, 1),
        "halt_steps": place_ends(jax.random.randint(streams_of[3], (ROWS, ROW_LEN), 1, STEPS + 1), jax.random.fold_in(streams_of[3], 1), 1, STEPS).astype(jnp.int32),
        "query_weight": gaussian(streams_of[4], (D, D), (D // 4) ** -0.5, 0.5),
        "query_bias": gaussian(streams_of[5], (D,), 0.3, 1.796875),
        "key_weight": gaussian(streams_of[6], (D, D), D ** -0.5, 0.25),
        "value_weight": gaussian(streams_of[7], (D, D), D ** -0.5, 0.25),
        "value_bias": gaussian(streams_of[8], (D,), 0.3, 1.796875),
        "out_weight": gaussian(streams_of[9], (D, D), (max(D // 16, 32)) ** -0.5, 1.0),
        "out_bias": gaussian(streams_of[10], (D,), 0.3, 1.796875),
        "first_gain": jnp.clip(1.0 + 0.1 * jax.random.normal(streams_of[11], (D,), jnp.float32), 0.5, 1.5).astype(jnp.bfloat16),
        "first_shift": gaussian(streams_of[12], (D,), 0.3, 1.796875),
        "second_gain": jnp.clip(1.0 + 0.1 * jax.random.normal(streams_of[13], (D,), jnp.float32), 0.5, 1.5).astype(jnp.bfloat16),
        "second_shift": gaussian(streams_of[14], (D,), 0.3, 1.796875),
        "up_weight": gaussian(streams_of[15], (D, FF), D ** -0.5, 0.25, ((1, 8),)),
        "up_bias": gaussian(streams_of[16], (FF,), 0.5, 3.0, ((0, 8),)),
        "down_weight": gaussian(streams_of[17], (FF, D), (FF // 2) ** -0.5, 0.1875, ((0, 8),)),
        "down_bias": gaussian(streams_of[18], (D,), 0.3, 1.796875),
        "halt_weight": gaussian(streams_of[19], (D,), D ** -0.5, 0.25, (), jnp.float32),
        "halt_bias": jnp.clip(jax.random.uniform(streams_of[20], (1,), jnp.float32, -2.0, 2.0), -2.0, 2.0),
        "cotangent": gaussian(streams_of[21], (ROWS, ROW_LEN, D), 1.0, 6.0, ((0, 4), (1, 8))),
    }


@jax.custom_vjp
def low(v):
    return lax.optimization_barrier(v.astype(jnp.bfloat16)).astype(jnp.float32)

@jax.custom_vjp
def low_back(v):
    return v

def low_keep(v):
    return (low(v), None)

def low_pass(kept, grad):
    return (grad,)

def back_keep(v):
    return (v, None)

def back_low(kept, grad):
    return (low(grad),)
low.defvjp(low_keep, low_pass)
low_back.defvjp(back_keep, back_low)
LN_EPS = 1e-05
PONDER = 0.01
NEG_FILL = -1e+30
HIGHEST = lax.Precision.HIGHEST

def rounded(values_in):
    return low_back(low(values_in))

def layer_norm(inputs, norm_gain, norm_shift):
    centre = lax.optimization_barrier(jnp.mean(inputs, axis=-1, keepdims=True))
    centered = inputs - centre
    spread = lax.optimization_barrier(jnp.mean(centered * centered, axis=-1, keepdims=True))
    return centered * lax.rsqrt(spread + LN_EPS) * norm_gain + norm_shift

def matrix(left_side, right_side):
    return jnp.dot(left_side, right_side, precision=HIGHEST)

def attention(queries, key_rows, value_rows, allowed):
    block = math.gcd(512, ROW_LEN)
    blocks = ROW_LEN // block
    split_queries = queries.reshape(blocks, block, HEADS, HEAD)
    split_allowed = allowed.reshape(blocks, block, ROW_LEN)
    key_heads = key_rows.reshape(ROW_LEN, HEADS, HEAD)
    value_heads = value_rows.reshape(ROW_LEN, HEADS, HEAD)
    scale_factor = 1.0 / math.sqrt(HEAD)

    def one_block(pair):
        query_block, allow_block = pair
        raw_scores = jnp.einsum('bhe,khe->hbk', query_block, key_heads, precision=HIGHEST) * scale_factor
        scores = jnp.where(allow_block[None], low_back(raw_scores), NEG_FILL)
        row_top = lax.optimization_barrier(jnp.max(scores, axis=-1, keepdims=True))
        exponent = jnp.exp(scores - row_top)
        attn_probs = exponent / lax.optimization_barrier(jnp.sum(exponent, axis=-1, keepdims=True))
        return jnp.einsum('hbk,khe->bhe', low(attn_probs), value_heads, precision=HIGHEST)
    mixed = lax.map(jax.checkpoint(one_block), (split_queries, split_allowed))
    return mixed.reshape(ROW_LEN, HEADS * HEAD)

def row_forward(row_tokens, allowed, row_steps, params):
    query_weight, query_bias, key_weight, value_weight, value_bias, out_weight, out_bias, first_gain, first_shift, second_gain, second_shift, up_weight, up_bias, down_weight, down_bias, halt_weight, halt_bias = params
    current = row_tokens
    states = [current]
    halt_probs = []
    for step_no in range(STEPS):
        logit = jnp.dot(current, halt_weight, precision=HIGHEST) + halt_bias[0]
        halt_probs.append(jax.nn.sigmoid(logit) / STEPS)
        normed = low(layer_norm(current, first_gain, first_shift))
        queries = rounded(matrix(normed, query_weight) + query_bias)
        key_rows = rounded(matrix(normed, key_weight))
        value_rows = rounded(matrix(normed, value_weight) + value_bias)
        mixed = rounded(attention(queries, key_rows, value_rows, allowed))
        hidden = current + low_back(matrix(mixed, out_weight) + out_bias)
        normed_two = low(layer_norm(hidden, second_gain, second_shift))
        pre_act = low_back(matrix(normed_two, up_weight) + up_bias)
        activated = low(jax.nn.gelu(pre_act))
        renewed = hidden + low_back(matrix(activated, down_weight) + down_bias)
        current = jnp.where((row_steps >= step_no + 1)[:, None], renewed, current)
        states.append(current)
    remainder = jnp.ones((ROW_LEN,), jnp.float32)
    for step_no in range(STEPS):
        remainder = remainder - jnp.where(row_steps > step_no + 1, halt_probs[step_no], 0.0)
    acted = remainder[:, None] * current
    for step_no in range(STEPS):
        weight_now = jnp.where(row_steps > step_no + 1, halt_probs[step_no], 0.0)
        acted = acted + weight_now[:, None] * states[step_no + 1]
    ponder = PONDER * jnp.sum(row_steps.astype(jnp.float32) + remainder)
    return (acted, ponder)

def reference(tokens, lengths, key_mask, halt_steps, query_weight, query_bias, key_weight, value_weight, value_bias, out_weight, out_bias, first_gain, first_shift, second_gain, second_shift, up_weight, up_bias, down_weight, down_bias, halt_weight, halt_bias, cotangent):
    params = tuple((item.astype(jnp.float32) for item in (query_weight, query_bias, key_weight, value_weight, value_bias, out_weight, out_bias, first_gain, first_shift, second_gain, second_shift, up_weight, up_bias, down_weight, down_bias, halt_weight, halt_bias)))
    positions = jnp.arange(ROW_LEN, dtype=jnp.int32)

    def one_row(carry, row_data):
        row_tokens, row_lengths, row_mask, row_steps, row_cot = row_data
        doc_ends = jnp.cumsum(row_lengths.astype(jnp.int32)).astype(jnp.int32)
        doc_hits = (positions[:, None] >= doc_ends[None, :]).astype(jnp.int32)
        doc_of = lax.optimization_barrier(jnp.sum(doc_hits, axis=1)).astype(jnp.int32)
        allowed = (doc_of[:, None] == doc_of[None, :]) & ((row_mask[None, :] == 1) | (positions[:, None] == positions[None, :]))

        def forward(inputs, weights):
            return row_forward(inputs, allowed, row_steps, weights)
        (acted_row, ponder), backward = jax.vjp(forward, row_tokens.astype(jnp.float32), params)
        grad_row, grad_params = backward((row_cot.astype(jnp.float32), jnp.ones((), jnp.float32)))
        carry = tuple((total + grad for total, grad in zip(carry, grad_params)))
        return (carry, (acted_row.astype(jnp.bfloat16), grad_row))
    initial = tuple((jnp.zeros(item.shape, jnp.float32) for item in params))
    sums, (acted, grad_tokens) = lax.scan(one_row, initial, (tokens, lengths, key_mask, halt_steps, cotangent))
    return (acted, grad_tokens, sums[0], sums[1], sums[2], sums[3], sums[4], sums[5], sums[6], sums[7], sums[8], sums[9], sums[10], sums[11], sums[12], sums[13], sums[14], sums[15], sums[16])
```

```python
import functools
import math

import jax
import jax.numpy as jnp
from jax import lax
from jax.experimental import pallas as pl
from jax.experimental.pallas import tpu as pltpu
from jax.sharding import PartitionSpec as P

HEAD = 64
STEPS = 3
LN_EPS = 1e-05
PONDER = 0.01
MASKED = -1e30
TOO_LARGE = 1e30
QUAD = 256
PAIR = 128
SHIFT_LANE = 16
BIAS_Q, BIAS_V, BIAS_O, BIAS_D, GAIN_1, SHIFT_1, GAIN_2, SHIFT_2, HALT_W, HALT_B = range(10)
HALTS, ALONE = 0, 1
AXES = ("dp", "sq")
VMEM_LIMIT = 32 * 2**20
HIGHEST = lax.Precision.HIGHEST
bf16 = jnp.bfloat16
f32 = jnp.float32

NN = (((1,), (0,)), ((), ()))
NT = (((1,), (1,)), ((), ()))
TN = (((0,), (0,)), ((), ()))


def dot(left, right, dims=NN):
    return lax.dot_general(left, right, dims, preferred_element_type=f32)


def split_two(values):
    high = values.astype(bf16)
    return high, (values - high.astype(f32)).astype(bf16)


def iota(shape, dim):
    return lax.broadcasted_iota(jnp.int32, shape, dim)


def head_lanes(groups):
    row, lane = iota((QUAD, PAIR), 0), iota((QUAD, PAIR), 1)
    place = lane - SHIFT_LANE
    hit = (place >= 0) & (place < 8 * groups) & (place % 8 == row // HEAD)
    return jnp.where(hit, 1.0, 0.0).astype(bf16)


def head_rows():
    hit = iota((8, QUAD), 0) == iota((8, QUAD), 1) // HEAD
    return jnp.where(hit, 1.0, 0.0).astype(bf16)


def head_block():
    hit = iota((QUAD, QUAD), 0) // HEAD == iota((QUAD, QUAD), 1) // HEAD
    return jnp.where(hit, 1.0, 0.0).astype(bf16)


def exact_three(values):
    group = (iota((1, PAIR), 1) - SHIFT_LANE) // 8
    high = values.astype(bf16).astype(f32)
    rest = values - high
    middle = rest.astype(bf16).astype(f32)
    low = rest - middle
    return jnp.where(group == 0, high, jnp.where(group == 1, middle, low)).astype(bf16)


def rows_to_lanes(rows, groups):
    count = rows.shape[1]
    parts = [jnp.zeros((SHIFT_LANE, count), f32)] + [rows] * groups
    parts.append(jnp.zeros((PAIR - SHIFT_LANE - 8 * groups, count), f32))
    return jnp.concatenate(parts, 0).T


def pair_of(values, head):
    start = head // 2 * PAIR
    return values[:, start : start + PAIR]


def only_head(values, head):
    return jnp.where(iota((1, PAIR), 1) // HEAD == head % 2, pair_of(values, head), bf16(0))


def shift_lanes(shift, features, head, groups=1):
    place = iota((1, PAIR), 1) - SHIFT_LANE
    hit = (place >= 0) & (place < 8 * groups) & (place % 8 == head)
    return jnp.where(hit, -shift, features)


def norm_stats(values):
    centered = values - jnp.mean(values, axis=-1, keepdims=True)
    inverse = lax.rsqrt(jnp.mean(centered * centered, axis=-1, keepdims=True) + LN_EPS)
    return centered * inverse, inverse


def norm_back(grad, normal, inverse, gain):
    scaled = grad * gain
    return inverse * (
        scaled
        - jnp.mean(scaled, axis=-1, keepdims=True)
        - normal * jnp.mean(scaled * normal, axis=-1, keepdims=True)
    )


def near_kernel(
    own_ref, mate_ref, wq_ref, wk_ref, wv_ref, rows_ref, qf_ref, kf_ref, alone_ref,
    q_ref, k_ref, v_ref, mixed_ref, lse_ref, vt_ref,
):
    count = own_ref.shape[0]
    own = own_ref[...]
    bias_q, bias_v = rows_ref[BIAS_Q : BIAS_Q + 1, :], rows_ref[BIAS_V : BIAS_V + 1, :]
    q_ref[...] = (dot(own, wq_ref[...]) + bias_q).astype(bf16) * bf16(1.0 / math.sqrt(HEAD))
    for place, rows in ((0, own), (1, mate_ref[...])):
        here = pl.ds(place * count, count)
        k_ref[here, :] = dot(rows, wk_ref[...]).astype(bf16)
        v_ref[here, :] = (dot(rows, wv_ref[...]) + bias_v).astype(bf16)
    vt_ref[...] = v_ref[...].T
    high, low = split_two(q_ref[...].astype(f32) * k_ref[:count, :].astype(f32))
    shift = dot(high, head_lanes(1)).astype(bf16)
    self_score = dot(head_rows(), high, NT) + dot(head_rows(), low, NT)
    pick = jnp.where(iota((8, PAIR), 1) == iota((8, PAIR), 0) + SHIFT_LANE, 1.0, 0.0).astype(bf16)
    base = dot(pick, shift, NT)
    lse_ref[...] = jnp.zeros_like(lse_ref)

    def one_head(head, exact):
        query = jnp.concatenate(
            [only_head(q_ref[...], head), shift_lanes(shift, qf_ref[...], head)], 1
        )
        keys = jnp.concatenate([pair_of(k_ref, head), kf_ref[...]], 1)
        scores = dot(keys, query, NT)
        start = base[head : head + 1]
        if exact:
            top = jnp.maximum(jnp.max(scores, axis=0, keepdims=True), 0.0)
            scores = scores - top
            start = start + top
        probs = jnp.exp(scores)
        total = jnp.sum(probs, axis=0, keepdims=True)
        lanes = pl.ds(head * HEAD, HEAD)
        mixed = dot(vt_ref[lanes, :], probs.astype(bf16))
        alone = jnp.exp(self_score[head : head + 1] - start) * alone_ref[0:1, :]
        total = total + alone
        mixed = mixed + vt_ref[lanes, :count].astype(f32) * alone
        mixed_ref[lanes, :] = mixed / total
        lse_ref[head : head + 1, :] = start + jnp.log(total)
        return total

    most = functools.reduce(jnp.maximum, [one_head(head, False) for head in range(4)])

    @pl.when(jnp.logical_not(jnp.max(most) < TOO_LARGE))
    def _():
        for head in range(4):
            one_head(head, True)


def far_kernel(blocks, *refs):
    block_refs, refs = refs[:blocks], refs[blocks:]
    wk_ref, wv_ref, rows_ref, qf_ref, kf_ref, q_ref, near_ref, near_lse_ref = refs[:8]
    k_ref, v_ref, mixed_ref, lse_ref, vt_ref, total_ref = refs[8:]
    count = q_ref.shape[0]
    bias_v = rows_ref[BIAS_V : BIAS_V + 1, :]
    for place, block_ref in enumerate(block_refs):
        here = pl.ds(place * count, count)
        rows = block_ref[...]
        k_ref[here, :] = dot(rows, wk_ref[...]).astype(bf16)
        v_ref[here, :] = (dot(rows, wv_ref[...]) + bias_v).astype(bf16)
    vt_ref[...] = v_ref[...].T
    near_lse = near_lse_ref[...]
    base = near_lse.astype(bf16).astype(f32)
    shift = rows_to_lanes(base, 1).astype(bf16)
    lse_ref[...] = jnp.zeros_like(lse_ref)

    def one_head(head, exact):
        query = jnp.concatenate(
            [only_head(q_ref[...], head), shift_lanes(shift, qf_ref[...], head)], 1
        )
        keys = jnp.concatenate([pair_of(k_ref, head), kf_ref[...]], 1)
        scores = dot(keys, query, NT)
        start = base[head : head + 1]
        if exact:
            top = jnp.maximum(jnp.max(scores, axis=0, keepdims=True), 0.0)
            scores = scores - top
            start = start + top
        probs = jnp.exp(scores)
        total = jnp.sum(probs, axis=0, keepdims=True)
        lanes = pl.ds(head * HEAD, HEAD)
        mixed = dot(vt_ref[lanes, :], probs.astype(bf16))
        before = jnp.exp(near_lse[head : head + 1] - start)
        total = total + before
        total_ref[lanes, :] = (mixed + near_ref[lanes, :] * before) / total
        lse_ref[head : head + 1, :] = start + jnp.log(total)
        return total

    most = functools.reduce(jnp.maximum, [one_head(head, False) for head in range(4)])

    @pl.when(jnp.logical_not(jnp.max(most) < TOO_LARGE))
    def _():
        for head in range(4):
            one_head(head, True)

    mixed_ref[...] = total_ref[...].T.astype(bf16)


def back_kernel(
    with_self, blocks, q_ref, do_ref, o_ref, lse_ref, k_ref, v_ref, kf_ref, wk_ref, wv_ref, qf_ref,
    *refs,
):
    if with_self:
        part_q_ref, cols_ref = refs[:2]
        refs = refs[2:]
    dq_ref, dk_ref, dv_ref, sum_ref = refs[:4]
    da_refs = refs[4 : 4 + blocks]
    kt_ref, dqt_ref, dkf_ref, dvf_ref, daf_ref = refs[4 + blocks :]
    count = q_ref.shape[0]
    step = pl.program_id(0)
    kt_ref[...] = k_ref[...].T
    query_all, grad_all = q_ref[...], do_ref[...]
    lse_terms = exact_three(rows_to_lanes(lse_ref[...], 3))
    high, low = split_two(grad_all.astype(f32) * o_ref[...].astype(f32))
    delta_terms = exact_three(dot(high, head_lanes(3)) + dot(low, head_lanes(3)))
    for head in range(4):
        query = only_head(query_all, head)
        grad = only_head(grad_all, head)
        keys = jnp.concatenate([pair_of(k_ref, head), kf_ref[...]], 1)
        values = jnp.concatenate([pair_of(v_ref, head), kf_ref[...]], 1)
        query_wide = jnp.concatenate([query, shift_lanes(lse_terms, qf_ref[...], head, 3)], 1)
        grad_wide = jnp.concatenate([grad, shift_lanes(delta_terms, bf16(0), head, 3)], 1)
        probs = jnp.exp(dot(keys, query_wide, NT))
        back = (probs * dot(values, grad_wide, NT)).astype(bf16)
        probs = probs.astype(bf16)
        pair = pl.ds(head // 2 * PAIR, PAIR)
        if head % 2 == 0:
            dvf_ref[:, pair] = dot(probs, grad)
            dkf_ref[:, pair] = dot(back, query)
        else:
            dvf_ref[:, pair] += dot(probs, grad)
            dkf_ref[:, pair] += dot(back, query)
        lanes = pl.ds(head * HEAD, HEAD)
        dqt_ref[lanes, :] = dot(kt_ref[lanes, :], back)
    dq = dqt_ref[...].T
    if with_self:
        block = head_block()
        own_k, own_v = k_ref[:count, :].astype(f32), v_ref[:count, :].astype(f32)
        query_f, grad_f = query_all.astype(f32), grad_all.astype(f32)

        def per_head(values):
            first, second = split_two(values)
            return dot(first, block) + dot(second, block)

        spread = jnp.where(
            (iota((PAIR, QUAD), 0) >= SHIFT_LANE)
            & (iota((PAIR, QUAD), 0) < SHIFT_LANE + 24)
            & (iota((PAIR, QUAD), 0) % 8 == iota((PAIR, QUAD), 1) // HEAD),
            1.0,
            0.0,
        ).astype(bf16)
        prob = jnp.exp(per_head(query_f * own_k) - dot(lse_terms, spread)) * cols_ref[:, ALONE : ALONE + 1]
        back = prob * (per_head(grad_f * own_v) - dot(delta_terms, spread))
        dq = dq + back * own_k
        dkf_ref[:count, :] += back * query_f
        dvf_ref[:count, :] += prob * grad_f
    dq = dq * (1.0 / math.sqrt(HEAD))
    if with_self:
        dq = (dq + part_q_ref[...]).astype(bf16)
        sum_ref[0:1, :] = jnp.sum(dq.astype(f32), axis=0, keepdims=True)
    else:
        sum_ref[0:1, :] = jnp.zeros((1, QUAD), f32)
    dq_ref[...] = dq
    dk, dv = dkf_ref[...].astype(bf16), dvf_ref[...].astype(bf16)
    dk_ref[...] = dk
    dv_ref[...] = dv
    sum_ref[1:2, :] = jnp.sum(dvf_ref[...], axis=0, keepdims=True)
    part = dot(dk, wk_ref[...], NT) + dot(dv, wv_ref[...], NT)

    @pl.when(step == 0)
    def _():
        daf_ref[...] = part

    @pl.when(step > 0)
    def _():
        daf_ref[...] += part

    @pl.when(step == pl.num_programs(0) - 1)
    def _():
        for place, da_ref in enumerate(da_refs):
            da_ref[...] = daf_ref[place * count : (place + 1) * count, :].astype(bf16)


def mix_kernel(
    step_no, last, x_ref, o_ref, wo_ref, rows_ref, up_a_ref, up_b_ref, down_a_ref, down_b_ref,
    cols_ref, hidden_ref, normed_ref, act_ref, slope_ref, new_ref, *refs,
):
    if last:
        (total_ref,) = refs
    else:
        next_ref, total_ref = refs
    step = pl.program_id(0)
    width = x_ref.shape[1]

    def row(place):
        return rows_ref[place : place + 1, :]

    @pl.when(step == 0)
    def _():
        hidden = x_ref[...] + (dot(o_ref[...], wo_ref[...]) + row(BIAS_O))
        hidden_ref[...] = hidden
        normal = norm_stats(hidden)[0]
        normed_ref[:, :width] = (normal * row(GAIN_2) + row(SHIFT_2)).astype(bf16)
        one = jnp.where(iota((x_ref.shape[0], PAIR), 1) == 0, 1.0, 0.0)
        normed_ref[:, width:] = one.astype(bf16)
        total_ref[...] = hidden + row(BIAS_D)

    in_first = step < pl.num_programs(0) // 2
    before = dot(normed_ref[...], jnp.where(in_first, up_a_ref[...], up_b_ref[...]), NT)
    root = math.sqrt(2.0 / math.pi)
    square = before * before
    bent = jnp.tanh(before * (root + root * 0.044715 * square))
    half = 0.5 + 0.5 * bent
    act = (before * half).astype(bf16)
    act_ref[...] = act
    slope_ref[...] = (
        half + 0.5 * before * (1.0 - bent * bent) * (root + 3.0 * root * 0.044715 * square)
    ).astype(bf16)
    total_ref[...] += dot(act, jnp.where(in_first, down_a_ref[...], down_b_ref[...]))

    @pl.when(step == pl.num_programs(0) - 1)
    def _():
        live = cols_ref[:, HALTS : HALTS + 1] >= step_no + 1
        new = jnp.where(live, total_ref[...], x_ref[...])
        new_ref[...] = new
        if not last:
            next_ref[...] = (norm_stats(new)[0] * row(GAIN_1) + row(SHIFT_1)).astype(bf16)


def unmix_kernel(
    step_no, grad_ref, cols_ref, slope_ref, up_a_ref, up_b_ref, down_a_ref, down_b_ref,
    hidden_ref, rows_ref, wo_ref, dz_ref, du_ref, dh_ref, dy_ref, do_ref, sum_ref, total_ref,
):
    in_first = pl.program_id(0) < pl.num_programs(0) // 2
    step = pl.program_id(0)
    width = grad_ref.shape[1]

    def live_grad():
        return jnp.where(cols_ref[:, HALTS : HALTS + 1] >= step_no + 1, grad_ref[...], 0.0)

    @pl.when(step == 0)
    def _():
        dz_ref[...] = live_grad().astype(bf16)

    down = jnp.where(in_first, down_a_ref[...], down_b_ref[...])
    du = (slope_ref[...].astype(f32) * dot(dz_ref[...], down, NT)).astype(bf16)
    du_ref[...] = du
    part = dot(du, jnp.where(in_first, up_a_ref[:, :width], up_b_ref[:, :width]))

    @pl.when(step == 0)
    def _():
        total_ref[...] = part

    @pl.when(step > 0)
    def _():
        total_ref[...] += part

    @pl.when(step == pl.num_programs(0) - 1)
    def _():
        normal, inverse = norm_stats(hidden_ref[...])
        back = total_ref[...]
        gain = rows_ref[GAIN_2 : GAIN_2 + 1, :]
        dh = live_grad() + norm_back(back, normal, inverse, gain)
        dh_ref[...] = dh
        dy = dh.astype(bf16)
        dy_ref[...] = dy
        do_ref[...] = dot(dy, wo_ref[...], NT).astype(bf16)
        sum_ref[0:1, :] = jnp.sum(dz_ref[...].astype(f32), axis=0, keepdims=True)
        sum_ref[1:2, :] = jnp.sum(dy.astype(f32), axis=0, keepdims=True)
        sum_ref[2:3, :] = jnp.sum(back * normal, axis=0, keepdims=True)
        sum_ref[3:4, :] = jnp.sum(back, axis=0, keepdims=True)


def join_kernel(
    step_no, received, dq_ref, wq_ref, near_ref, x_ref, rows_ref, grad_ref, cols_ref, dh_ref,
    halt_ref, cot_ref, *refs,
):
    parts, (new_ref, sum_ref) = refs[:received], refs[received:]
    back = dot(dq_ref[...], wq_ref[...], NT) + near_ref[...].astype(f32)
    for part in parts:
        back = back + part[...].astype(f32)
    values = x_ref[...]
    normal, inverse = norm_stats(values)
    slope = halt_ref[:, step_no : step_no + 1]
    passed = jnp.where(cols_ref[:, HALTS : HALTS + 1] >= step_no + 1, 0.0, grad_ref[...])
    new = (
        passed
        + dh_ref[...]
        + norm_back(back, normal, inverse, rows_ref[GAIN_1 : GAIN_1 + 1, :])
        + slope * rows_ref[HALT_W : HALT_W + 1, :]
    )
    if step_no > 0:
        weight = halt_ref[:, STEPS + step_no - 1 : STEPS + step_no]
        new = new + weight * cot_ref[...].astype(f32)
    new_ref[...] = new
    sums = [back * normal, back, slope * values]

    @pl.when(pl.program_id(0) == 0)
    def _():
        sum_ref[...] = jnp.zeros_like(sum_ref)

    for place, item in enumerate(sums):
        sum_ref[place : place + 1, :] += jnp.sum(item, axis=0, keepdims=True)


def halt_kernel(*refs):
    state_refs = refs[: STEPS + 1]
    rows_ref, cols_ref, cot_ref, acted_ref, grad_ref, halt_ref, sum_ref = refs[STEPS + 1 :]
    states = [ref[...] for ref in state_refs]
    cot = cot_ref[...].astype(f32)
    halts = cols_ref[:, HALTS : HALTS + 1]
    halt_row = rows_ref[HALT_W : HALT_W + 1, :]
    halt_bias = rows_ref[HALT_B : HALT_B + 1, 0:1]
    final_dot = jnp.sum(cot * states[STEPS], axis=-1, keepdims=True)
    remainder = jnp.ones_like(halts)
    acted = jnp.zeros_like(states[0])
    slopes, weights = [], []
    for step in range(STEPS):
        logit = jnp.sum(states[step] * halt_row, axis=-1, keepdims=True) + halt_bias
        prob = (1.0 / (1.0 + jnp.exp(-logit))) / STEPS
        early = halts > step + 1
        weight = jnp.where(early, prob, 0.0)
        weights.append(weight)
        remainder = remainder - weight
        acted = acted + weight * states[step + 1]
        step_dot = jnp.sum(cot * states[step + 1], axis=-1, keepdims=True)
        slope = (step_dot - final_dot - PONDER) * prob * (1.0 - STEPS * prob)
        slopes.append(jnp.where(early, slope, 0.0))
    acted_ref[...] = (acted + remainder * states[STEPS]).astype(bf16)
    grad_ref[...] = (remainder + weights[STEPS - 1]) * cot
    lane = iota((halts.shape[0], PAIR), 1)
    table = jnp.zeros((halts.shape[0], PAIR), f32)
    for place, column in enumerate(slopes + weights):
        table = jnp.where(lane == place, column, table)
    halt_ref[...] = table

    @pl.when(pl.program_id(0) == 0)
    def _():
        sum_ref[...] = jnp.zeros_like(sum_ref)

    sum_ref[0:1, :] += jnp.sum(jnp.where(lane < STEPS, table, 0.0), axis=0, keepdims=True)


def masks_kernel(
    middle, mine_ref, theirs_ref, my_lengths_ref, their_lengths_ref, halts_a_ref, halts_b_ref,
    qf_ref, near_ref, far_ref, cols_ref, alone_ref, row_ref,
):
    seq_here = halts_a_ref.shape[1]
    count = 2 * seq_here
    docs = my_lengths_ref.shape[1]
    d_at, s_at = lax.axis_index("dp"), lax.axis_index("sq")
    top = 2 * middle
    parity, upper, core, chip = s_at % 2, s_at // top, d_at % 2, s_at % top // 2
    same = core == upper
    both = jnp.where(same, mine_ref[...], theirs_ref[...])
    row_ref[...] = jnp.broadcast_to(
        jnp.where(parity == 0, both[0:1, :], both[1:2, :]), row_ref.shape
    )
    ends, total = [], jnp.int32(0)
    for doc in range(docs):
        length = jnp.where(same, my_lengths_ref[parity, doc], their_lengths_ref[parity, doc])
        total = total + length
        ends.append(total)

    def at_block(core_at, chip_at):
        start = (core_at * middle + chip_at) * count
        block = row_ref[0:1, pl.ds(pl.multiple_of(start, count), count)]
        turned = jnp.concatenate([block[:, seq_here:], block[:, :seq_here]], 1)
        offset = iota((1, count), 1) + parity * seq_here
        place = start + jnp.where(offset >= count, offset - count, offset)
        doc_at = jnp.zeros((1, count), jnp.int32)
        for end in ends:
            doc_at = doc_at + jnp.where(place >= end, 1, 0)
        return doc_at, jnp.where(parity == 0, block, turned)

    kind = iota((PAIR, 1), 0)

    def key_features(core_at, chip_at):
        doc_at, open_at = at_block(core_at, chip_at)
        closed = (kind == doc_at) | ((kind == 8) & (open_at == 0))
        ones = jnp.where(kind >= SHIFT_LANE, 1.0, 0.0)
        return jnp.where(closed, MASKED, jnp.broadcast_to(ones, closed.shape)).T.astype(bf16)

    doc_at, open_at = at_block(core, chip)
    wanted = ((kind < docs) & (kind != doc_at)) | (kind == 8)
    qf_ref[...] = jnp.where(wanted, 1.0, 0.0).T.astype(bf16)
    for place, core_at in enumerate((core, 1 - core)):
        near_ref[pl.ds(place * count, count), :] = key_features(core_at, chip)
    place = 0
    for offset in range(1, middle):
        for core_at in (core, 1 - core):
            far_ref[pl.ds(place * count, count), :] = key_features(core_at, chip ^ offset)
            place += 1
    halts = jnp.concatenate([halts_a_ref[...], halts_b_ref[...]], 1).astype(f32)
    alone = jnp.where(open_at == 0, 1.0, 0.0)
    alone_ref[...] = jnp.broadcast_to(alone, alone_ref.shape)
    table = jnp.where(kind == HALTS, halts, jnp.where(kind == ALONE, alone, 0.0))
    cols_ref[...] = table.T


def hidden_grads_kernel(steps, *refs):
    act_refs, dz_refs, du_refs, normed_refs = (refs[i * steps : (i + 1) * steps] for i in range(4))
    up_ref, down_ref = refs[4 * steps :]
    up_ref[...] = sum(
        dot(du[...], normed[...], TN) for du, normed in zip(du_refs, normed_refs)
    ).astype(bf16)
    down_ref[...] = sum(dot(act[...], dz[...], TN) for act, dz in zip(act_refs, dz_refs)).astype(
        bf16
    )


def pack_kernel(bits, *refs):
    sources, results = refs[: len(refs) // 3 * 2], refs[len(refs) // 3 * 2 :]
    blocks = 2 ** len(bits)
    rows = sources[0].shape[0] // blocks
    width = sources[0].shape[1]
    own = own_block(bits)
    for block in range(blocks):
        start = pl.multiple_of((own ^ block) * rows, rows)
        for place, source in enumerate(sources):
            lanes = pl.ds(place % 2 * width, width)
            results[place // 2][pl.ds(block * rows, rows), lanes] = source[
                pl.ds(start, rows), :
            ].astype(bf16)


def unpack_kernel(bits, *refs):
    sources, results = refs[: len(refs) // 3], refs[len(refs) // 3 :]
    blocks = 2 ** len(bits)
    rows = sources[0].shape[0] // blocks
    width = sources[0].shape[1] // 2
    own = own_block(bits)
    for block in range(blocks):
        start = pl.multiple_of((own ^ block) * rows, rows)
        for place, result in enumerate(results):
            lanes = pl.ds(place % 2 * width, width)
            result[pl.ds(block * rows, rows), :] = sources[place // 2][
                pl.ds(start, rows), lanes
            ].astype(f32)


def own_block(bits):
    own = jnp.int32(0)
    for d_bit, s_bit in bits:
        at = lax.axis_index("dp") & d_bit if d_bit else lax.axis_index("sq") & s_bit
        own = own * 2 + jnp.where(at != 0, 1, 0)
    return own


def whole(shape):
    return pl.BlockSpec(shape, lambda i: (0,) * len(shape))


def lanes_of(rows, width=QUAD):
    return pl.BlockSpec((rows, width), lambda i: (0, i))


def rows_of(rows, width):
    return pl.BlockSpec((rows, width), lambda i: (i, 0))


def shaped(shape, dtype):
    return jax.ShapeDtypeStruct(shape, dtype)


def params(flops, moved, exps=0):
    return dict(
        compiler_params=pltpu.CompilerParams(vmem_limit_bytes=VMEM_LIMIT),
        cost_estimate=pl.CostEstimate(
            flops=int(flops), bytes_accessed=int(moved), transcendentals=int(exps)
        ),
    )


def attend_near(own, mate, wq, wk, wv, rows, qf, kf, alone):
    count, width = own.shape
    quads = width // QUAD
    keys = 2 * count
    return pl.pallas_call(
        near_kernel,
        grid=(quads,),
        in_specs=[
            whole((count, width)), whole((count, width)),
            lanes_of(width), lanes_of(width), lanes_of(width), lanes_of(rows.shape[0]),
            whole((count, PAIR)), whole((keys, PAIR)), whole((8, count)),
        ],
        out_specs=[
            lanes_of(count), lanes_of(keys), lanes_of(keys), rows_of(QUAD, count),
            rows_of(8, count),
        ],
        out_shape=[
            shaped((count, width), bf16), shaped((keys, width), bf16), shaped((keys, width), bf16),
            shaped((width, count), f32), shaped((8 * quads, count), f32),
        ],
        scratch_shapes=[pltpu.VMEM((QUAD, keys), bf16)],
        name="attend_near",
        **params(8 * count * keys * width * 2, 10 * count * width * 2, count * keys * 8),
    )(own, mate, wq, wk, wv, rows, qf, kf, alone)


def attend_far(blocks, wk, wv, rows, qf, kf, queries, near_mixed, near_lse):
    count, width = queries.shape
    quads = width // QUAD
    keys = len(blocks) * count
    return pl.pallas_call(
        functools.partial(far_kernel, len(blocks)),
        grid=(quads,),
        in_specs=[whole((count, width))] * len(blocks)
        + [
            lanes_of(width), lanes_of(width), lanes_of(rows.shape[0]),
            whole((count, PAIR)), whole((keys, PAIR)), lanes_of(count), rows_of(QUAD, count),
            rows_of(8, count),
        ],
        out_specs=[lanes_of(keys), lanes_of(keys), lanes_of(count), rows_of(8, count)],
        out_shape=[
            shaped((keys, width), bf16), shaped((keys, width), bf16), shaped((count, width), bf16),
            shaped((8 * quads, count), f32),
        ],
        scratch_shapes=[pltpu.VMEM((QUAD, keys), bf16), pltpu.VMEM((QUAD, count), f32)],
        name="attend_far",
        **params(8 * count * keys * width * 2, 10 * count * width * 2, count * keys * 8),
    )(*blocks, wk, wv, rows, qf, kf, queries, near_mixed, near_lse)


def attend_back(queries, grad_mixed, mixed, lse, keys_in, values_in, kf, wk, wv, qf, partial, cols):
    count, width = queries.shape
    quads = width // QUAD
    keys = keys_in.shape[0]
    blocks = keys // count
    with_self = cols is not None
    extra = [partial, cols] if with_self else []
    extra_specs = [lanes_of(count), whole((count, PAIR))] if with_self else []
    return pl.pallas_call(
        functools.partial(back_kernel, with_self, blocks),
        grid=(quads,),
        in_specs=[
            lanes_of(count), lanes_of(count), lanes_of(count), rows_of(8, count), lanes_of(keys),
            lanes_of(keys), whole((keys, PAIR)), lanes_of(width), lanes_of(width),
            whole((count, PAIR)),
        ]
        + extra_specs,
        out_specs=[lanes_of(count), lanes_of(keys), lanes_of(keys), lanes_of(8)]
        + [whole((count, width))] * blocks,
        out_shape=[
            shaped((count, width), bf16 if with_self else f32), shaped((keys, width), bf16),
            shaped((keys, width), bf16), shaped((8, width), f32),
        ]
        + [shaped((count, width), bf16)] * blocks,
        scratch_shapes=[
            pltpu.VMEM((QUAD, keys), bf16), pltpu.VMEM((QUAD, count), f32),
            pltpu.VMEM((keys, QUAD), f32), pltpu.VMEM((keys, QUAD), f32),
            pltpu.VMEM((keys, width), f32),
        ],
        name="back_near" if with_self else "back_far",
        **params(20 * count * keys * width * 2, 20 * count * width * 2, count * keys * 8),
    )(queries, grad_mixed, mixed, lse, keys_in, values_in, kf, wk, wv, qf, *extra)


def halves_of(rows, width, steps):
    half = steps // 2
    return [
        pl.BlockSpec((rows, width), lambda i: (jnp.minimum(i, half - 1), 0)),
        pl.BlockSpec((rows, width), lambda i: (jnp.maximum(i - half, 0), 0)),
    ]


def mix(step_no, x, mixed, wo, rows, ups, downs, cols, last):
    count, width = x.shape
    hidden = 2 * ups[0].shape[0]
    chunk = min(512, hidden // 2)
    steps = hidden // chunk
    square = whole((count, width))
    wide = width + PAIR
    out_specs = [
        square, whole((count, wide)), lanes_of(count, chunk), lanes_of(count, chunk), square,
    ]
    out_shape = [
        shaped((count, width), f32), shaped((count, wide), bf16), shaped((count, hidden), bf16),
        shaped((count, hidden), bf16), shaped((count, width), f32),
    ]
    if not last:
        out_specs.append(square)
        out_shape.append(shaped((count, width), bf16))
    return pl.pallas_call(
        functools.partial(mix_kernel, step_no, last),
        grid=(hidden // chunk,),
        in_specs=[
            square, square, whole((width, width)), whole(rows.shape),
            *halves_of(chunk, wide, steps), *halves_of(chunk, width, steps),
            whole((count, PAIR)),
        ],
        out_specs=out_specs,
        out_shape=out_shape,
        scratch_shapes=[pltpu.VMEM((count, width), f32)],
        name="mix",
        **params(4 * count * width * hidden, 16 * count * width + 8 * width * hidden),
    )(x, mixed, wo, rows, *ups, *downs, cols)


def unmix(step_no, grad, cols, slope, ups, downs, hidden_state, rows, wo):
    count, width = grad.shape
    hidden = 2 * ups[0].shape[0]
    chunk = min(512, hidden // 2)
    steps = hidden // chunk
    square = whole((count, width))
    return pl.pallas_call(
        functools.partial(unmix_kernel, step_no),
        grid=(hidden // chunk,),
        in_specs=[
            square, whole((count, PAIR)), lanes_of(count, chunk),
            *halves_of(chunk, width + PAIR, steps), *halves_of(chunk, width, steps), square,
            whole(rows.shape), whole((width, width)),
        ],
        out_specs=[
            square, lanes_of(count, chunk), square, square, square, whole((8, width)),
        ],
        out_shape=[
            shaped((count, width), bf16), shaped((count, hidden), bf16), shaped((count, width), f32),
            shaped((count, width), bf16), shaped((count, width), bf16), shaped((8, width), f32),
        ],
        scratch_shapes=[pltpu.VMEM((count, width), f32)],
        name="unmix",
        **params(4 * count * width * hidden, 16 * count * width + 8 * width * hidden),
    )(grad, cols, slope, *ups, *downs, hidden_state, rows, wo)


def join(step_no, dq, wq, near, x, rows, grad, cols, dh, halt_table, cot, parts):
    count, width = x.shape
    piece = min(128, count)
    part, table = rows_of(piece, width), rows_of(piece, PAIR)
    return pl.pallas_call(
        functools.partial(join_kernel, step_no, len(parts)),
        grid=(count // piece,),
        in_specs=[
            part, whole((width, width)), part, part, whole(rows.shape), part, table, part, table,
            part,
        ]
        + [part] * len(parts),
        out_specs=[part, whole((8, width))],
        out_shape=[shaped((count, width), f32), shaped((8, width), f32)],
        name="join",
        **params(2 * count * width * width, 24 * count * width),
    )(dq, wq, near, x, rows, grad, cols, dh, halt_table, cot, *parts)


def halting(states, rows, cols, cot):
    count, width = cot.shape
    piece = min(128, count)
    part, table = rows_of(piece, width), rows_of(piece, PAIR)
    return pl.pallas_call(
        halt_kernel,
        grid=(count // piece,),
        in_specs=[part] * len(states) + [whole(rows.shape), table, part],
        out_specs=[part, part, table, whole((8, PAIR))],
        out_shape=[
            shaped((count, width), bf16), shaped((count, width), f32), shaped((count, PAIR), f32),
            shaped((8, PAIR), f32),
        ],
        name="halting",
        **params(20 * count * width, 24 * count * width),
    )(*states, rows, cols, cot)


def masks(middle, mine, theirs, my_lengths, their_lengths, halts_a, halts_b):
    count = 2 * halts_a.shape[1]
    far = max(2 * (middle - 1), 1) * count
    here = pl.BlockSpec(memory_space=pltpu.VMEM)
    scalars = pl.BlockSpec(memory_space=pltpu.SMEM)
    return pl.pallas_call(
        functools.partial(masks_kernel, middle),
        in_specs=[here, here, scalars, scalars, here, here],
        out_specs=[here] * 5,
        out_shape=[
            shaped((count, PAIR), bf16), shaped((2 * count, PAIR), bf16), shaped((far, PAIR), bf16),
            shaped((count, PAIR), f32), shaped((8, count), f32),
        ],
        scratch_shapes=[pltpu.VMEM((8, mine.shape[1]), jnp.int32)],
        name="masks",
        **params(10 * count * PAIR, 16 * count * PAIR),
    )(mine, theirs, my_lengths, their_lengths, halts_a, halts_b)


def hidden_grads(acts, dzs, dus, normeds):
    count, hidden = acts[0].shape
    width, wide = dzs[0].shape[1], normeds[0].shape[1]
    chunk = min(256, hidden)
    tall = lanes_of(count, chunk)
    steps = len(acts)
    return pl.pallas_call(
        functools.partial(hidden_grads_kernel, steps),
        grid=(hidden // chunk,),
        in_specs=[tall] * steps
        + [whole((count, width))] * steps
        + [tall] * steps
        + [whole((count, wide))] * steps,
        out_specs=[rows_of(chunk, wide), rows_of(chunk, width)],
        out_shape=[shaped((hidden, wide), bf16), shaped((hidden, width), bf16)],
        name="hidden_grads",
        **params(4 * steps * count * width * hidden, 4 * steps * count * hidden),
    )(*acts, *dzs, *dus, *normeds)


def pack(bits, sources):
    rows, width = sources[0].shape
    here = pl.BlockSpec(memory_space=pltpu.VMEM)
    return pl.pallas_call(
        functools.partial(pack_kernel, bits),
        in_specs=[here] * len(sources),
        out_specs=[here] * (len(sources) // 2),
        out_shape=[shaped((rows, 2 * width), bf16)] * (len(sources) // 2),
        name="pack",
        **params(0, 6 * rows * width * len(sources)),
    )(*sources)


def unpack(bits, sources):
    rows, width = sources[0].shape
    here = pl.BlockSpec(memory_space=pltpu.VMEM)
    return pl.pallas_call(
        functools.partial(unpack_kernel, bits),
        in_specs=[here] * len(sources),
        out_specs=[here] * (2 * len(sources)),
        out_shape=[shaped((rows, width // 2), f32)] * (2 * len(sources)),
        name="unpack",
        **params(0, 6 * rows * width * len(sources)),
    )(*sources)


def make_per_device(dp_size, sq_size):
    middle = sq_size // 4
    top = sq_size // 2

    def permute(value, move):
        pairs = []
        for d in range(dp_size):
            for s in range(sq_size):
                to_d, to_s = move(d, s)
                pairs.append((d * sq_size + s, to_d * sq_size + to_s))
        return lax.ppermute(value, AXES, pairs)

    def swap(value, d_bits, s_bits):
        return permute(value, lambda d, s: (d ^ d_bits, s ^ s_bits))

    def regroup(flip):
        def move(d, s):
            upper, core = s // top, d % 2
            return d - core + upper, (core * top + s % top) ^ flip

        return move

    def bits_of(size):
        return [1 << place for place in range(size.bit_length() - 1)]

    dp_bits, sq_bits = bits_of(dp_size), bits_of(sq_size)
    bit_names = [(bit, 0) for bit in dp_bits] + [(0, bit) for bit in sq_bits[::-1]]

    def with_bits(value):
        return value.reshape((2,) * len(bit_names) + (-1,) + value.shape[1:])

    class Gather:
        def __init__(self, piece, order):
            self.piece, self.order, self.names = piece, list(order), []

        def start(self):
            if self.order:
                self.sent = [swap(self.piece, *self.order[0])]
            return self.sent if self.order else []

        def finish(self, arrived):
            if self.order:
                name = self.order.pop(0)
                place = sum(bit_names.index(item) < bit_names.index(name) for item in self.names)
                self.names = sorted(self.names + [name], key=bit_names.index)
                self.piece = jnp.stack([self.piece, arrived[0]], place)

        def step(self, *others):
            self.finish([after(item, *others) for item in self.start()])

    class Scatter:
        def __init__(self, total, order):
            self.piece, self.order, self.names = with_bits(total), list(order), list(bit_names)

        def start(self):
            if not self.order:
                return []
            axis = self.names.index(self.order[0])
            self.kept = lax.index_in_dim(self.piece, 0, axis, False)
            return [swap(lax.index_in_dim(self.piece, 1, axis, False), *self.order[0])]

        def finish(self, arrived):
            if self.order:
                self.names.remove(self.order.pop(0))
                self.piece = self.kept + arrived[0]

    class Everywhere:
        def __init__(self, total, order):
            self.work, self.order = Scatter(total, order), list(order)

        def start(self):
            if isinstance(self.work, Scatter) and not self.work.order:
                self.work = Gather(self.work.piece, self.order[::-1])
            return self.work.start()

        def finish(self, arrived):
            self.work.finish(arrived)
            self.piece = self.work.piece

    class Small:
        def __init__(self, total, order):
            self.piece, self.order = total, list(order)

        def start(self):
            return [swap(self.piece, *self.order[0])] if self.order else []

        def finish(self, arrived):
            if self.order:
                self.order.pop(0)
                self.piece = self.piece + arrived[0]

    def together(chains):
        sent = [chain.start() for chain in chains]
        flat = [item for items in sent for item in items]
        if flat:
            flat = list(lax.optimization_barrier(tuple(flat)))
        for chain, items in zip(chains, sent):
            chain.finish([flat.pop(0) for _ in items])

    def own_part(shard):
        rows = shard.shape[0] // dp_size
        return lax.dynamic_slice_in_dim(shard, lax.axis_index("dp") * rows, rows, 0)

    def gather_dp(piece):
        for bit in dp_bits:
            other = swap(piece, bit, 0)
            lower = (lax.axis_index("dp") & bit) == 0
            piece = jnp.concatenate(
                [jnp.where(lower, piece, other), jnp.where(lower, other, piece)], 0
            )
        return piece

    def turn(total):
        shape = total.shape
        total = with_bits(total)
        for axis, (d_bit, s_bit) in enumerate(bit_names):
            own = ((lax.axis_index("dp") & d_bit) | (lax.axis_index("sq") & s_bit)) != 0
            total = jnp.where(own, jnp.flip(total, axis), total)
        return total.reshape(shape)

    def after(value, *others):
        return lax.optimization_barrier((value,) + others)[0]

    def per_device(
        tokens, lengths, key_mask, halt_steps, query_weight, query_bias, key_weight, value_weight,
        value_bias, out_weight, out_bias, first_gain, first_shift, second_gain, second_shift,
        up_weight, up_bias, down_weight, down_bias, halt_weight, halt_bias, cotangent,
    ):
        seq_here, width = tokens.shape[1:]
        parity = lax.axis_index("sq") % 2

        def spread(value):
            own = lax.dynamic_index_in_dim(value, parity, 0, False)
            other = lax.dynamic_index_in_dim(value, 1 - parity, 0, False)
            return permute(own, regroup(0)), permute(other, regroup(1))

        def unspread(value):
            own = permute(value[:seq_here], regroup(0))
            other = permute(value[seq_here:], regroup(1))
            first = jnp.where(parity == 0, own, other)
            second = jnp.where(parity == 0, other, own)
            return jnp.stack([first, second], 0)

        tokens_here = spread(tokens)
        far_bits, core_bit, other_dp, side = sq_bits[::-1][:-1], (1, 0), dp_bits[1:], (0, 1)
        z_order = [(0, bit) for bit in far_bits]
        y_order = [(bit, 0) for bit in other_dp]
        up_wide = jnp.concatenate(
            [up_weight.T, jnp.pad(up_bias[:, None], ((0, 0), (0, PAIR - 1)))], 1
        )
        gathers = [
            Gather(own_part(up_wide), z_order + [side] + y_order),
            Gather(own_part(down_weight), z_order + y_order + [side]),
        ]

        def gather_step(*others):
            sent = [gather.start() for gather in gathers]
            for gather, items in zip(gathers, sent):
                gather.finish([after(item, *others) for item in items])

        halts = spread(halt_steps[:, None, :])
        query_feats, near_feats, far_feats, cols, alone_row = masks(
            middle, key_mask, swap(key_mask, 1, 0), lengths, swap(lengths, 1, 0), *halts
        )
        tokens_here = [after(item, query_feats) for item in tokens_here]
        x = jnp.concatenate(tokens_here, 0).astype(f32)
        rows = jnp.stack(
            [
                item.astype(f32)
                for item in (
                    query_bias, value_bias, out_bias, down_bias, first_gain, first_shift,
                    second_gain, second_shift, halt_weight, jnp.broadcast_to(halt_bias, (width,)),
                )
            ]
            + [jnp.zeros((width,), f32)] * 6
        )
        centered = x - jnp.mean(x, axis=-1, keepdims=True)
        inverse = lax.rsqrt(jnp.mean(centered * centered, axis=-1, keepdims=True) + LN_EPS)
        gain_one, shift_one = first_gain.astype(f32), first_shift.astype(f32)
        normed = (centered * inverse * gain_one + shift_one).astype(bf16)

        gather_step(normed)

        states, kept = [x], []
        for step in range(STEPS):
            x = states[-1]
            arrived = [swap(normed, 0, offset * 2) for offset in range(1, middle)]
            mate = swap(normed, 1, 0)
            if step == 0:
                gather_step(mate)
            queries, keys_near, values_near, near_mixed, near_lse = attend_near(
                normed, mate, query_weight, key_weight, value_weight, rows, query_feats,
                near_feats, alone_row,
            )
            if step == 0:
                gather_step(near_lse)
            far = []
            for block in arrived:
                block = after(block, near_lse)
                far += [block, swap(block, 1, 0)]
            keys_far, values_far, mixed, lse = attend_far(
                far, key_weight, value_weight, rows, query_feats, far_feats, queries, near_mixed,
                near_lse,
            )
            if step == 0:
                gather_step(lse)
                while gathers[0].order:
                    gather_step()
                halves = []
                for gather, weight in zip(gathers, (up_wide, down_weight)):
                    half = gather.piece.reshape(-1, weight.shape[1])
                    halves.append((half, swap(half, *core_bit)))
                up_rows, down_rows = halves
                cot = jnp.concatenate(spread(after(cotangent, lse)), 0)
            out = mix(
                step, x, mixed, out_weight, rows, up_rows, down_rows, cols, step == STEPS - 1
            )
            hidden, normed_two, act, slope, new = out[:5]
            kept.append(
                (normed, mate, far, queries, keys_near, values_near, keys_far, values_far, mixed,
                 lse, hidden, normed_two, act, slope)
            )
            states.append(new)
            if step < STEPS - 1:
                normed = out[5]

        acted, grad, halt_table, halt_sums = halting(states, rows, cols, cot)
        acted_out = unspread(acted)
        total = {}

        def add(name, value):
            total[name] = total[name] + value if name in total else value

        add("halt_bias", jnp.sum(halt_sums[0]))
        hidden_parts = []
        for step in reversed(range(STEPS)):
            (normed, mate, far, queries, keys_near, values_near, keys_far, values_far, mixed, lse,
             hidden, normed_two, act, slope) = kept[step]
            dz, du, dh, dy, grad_mixed, sums = unmix(
                step, grad, cols, slope, up_rows, down_rows, hidden, rows, out_weight
            )
            hidden_parts.append((act, dz, du, normed_two))
            add("down_bias", sums[0])
            add("out_bias", sums[1])
            add("gain_two", sums[2])
            add("shift_two", sums[3])
            add("out", dot(mixed, dy, TN))
            if step == 0:
                up_part, down_part = hidden_grads(*zip(*hidden_parts))
                grad_mixed = after(grad_mixed, up_part)
                scatter_order = [core_bit] + y_order + [side] + z_order[::-1]
                other_order = [core_bit, side] + y_order + z_order[::-1]
                hidden_sums = [Scatter(up_part, scatter_order), Scatter(down_part, other_order)]
                together(hidden_sums)
            part_q, dk_far, dv_far, far_sums, *da_far = attend_back(
                queries, grad_mixed, mixed, lse, keys_far, values_far, far_feats, key_weight,
                value_weight, query_feats, None, None,
            )
            sent = []
            for offset in range(1, middle):
                same, crossed = da_far[2 * offset - 2 : 2 * offset]
                sent += [swap(same, 0, offset * 2), swap(crossed, 1, offset * 2)]
            for place, block in enumerate(far):
                here = slice(place * seq_here * 2, (place + 1) * seq_here * 2)
                add("key", dot(block, dk_far[here], TN))
                add("value", dot(block, dv_far[here], TN))
            held = [part_q, total["key"], total["value"], total["out"]]
            if step == 0:
                held += [item.piece for item in hidden_sums]
            part_q, total["key"], total["value"], total["out"], *pieces = (
                lax.optimization_barrier(tuple(held))
            )
            if step == 0:
                for item, piece in zip(hidden_sums, pieces):
                    item.piece = piece
                hidden_sent = [item.start() for item in hidden_sums]
            dq, dk_near, dv_near, near_sums, da_own, da_mate = attend_back(
                queries, grad_mixed, mixed, lse, keys_near, values_near, near_feats, key_weight,
                value_weight, query_feats, part_q, cols,
            )
            add("query_bias", near_sums[0])
            add("value_bias", near_sums[1] + far_sums[1])
            da_mate, *sent = lax.optimization_barrier((da_mate, *sent))
            arrived = swap(da_mate, 1, 0)
            for place, block in enumerate((normed, mate)):
                here = slice(place * seq_here * 2, (place + 1) * seq_here * 2)
                add("key", dot(block, dk_near[here], TN))
                add("value", dot(block, dv_near[here], TN))
            add("query", dot(normed, dq, TN))
            if step > 0:
                dq, total["query"], total["key"], total["value"] = lax.optimization_barrier(
                    (dq, total["query"], total["key"], total["value"])
                )
            grad, join_sums = join(
                step, dq, query_weight, da_own, states[step], rows, grad, cols, dh, halt_table,
                cot, sent + [arrived],
            )
            add("gain_one", join_sums[0])
            add("shift_one", join_sums[1])
            add("halt", join_sums[2])

        squares = [total["query"], total["key"], total["value"], total["out"]]
        by_kernel = width % (16 * 2 ** len(bit_names)) == 0
        if by_kernel:
            squares = pack(bit_names, squares)
        else:
            squares = [
                turn(jnp.concatenate(squares[place : place + 2], 1).astype(bf16))
                for place in (0, 2)
            ]
        sums = [Everywhere(squares[0], scatter_order), Everywhere(squares[1], other_order)]
        names = (
            "query_bias", "value_bias", "out_bias", "gain_one", "shift_one", "gain_two",
            "shift_two", "down_bias", "halt",
        )
        small = jnp.concatenate(
            [total[name] for name in names] + [jnp.full((PAIR,), total["halt_bias"])]
        )
        for item, items in zip(hidden_sums, hidden_sent):
            item.finish(items)
        together(sums + hidden_sums)
        small = Small(small, bit_names)
        together(sums + hidden_sums + [small])
        grad_tokens = unspread(grad.astype(bf16)).astype(f32)
        while sums[0].work.order or isinstance(sums[0].work, Scatter):
            together(sums + hidden_sums + [small])
        up_sum, down_sum = gather_dp(hidden_sums[0].piece), gather_dp(hidden_sums[1].piece)
        small = small.piece
        squares = [item.piece.reshape(width, 2 * width) for item in sums]
        if by_kernel:
            grad_q, grad_k, grad_v, grad_o = unpack(bit_names, squares)
        else:
            grad_q, grad_k, grad_v, grad_o = (
                turn(item)[:, place * width : (place + 1) * width].astype(f32)
                for item in squares
                for place in range(2)
            )
        vectors = {name: small[i * width : (i + 1) * width] for i, name in enumerate(names)}
        return (
            acted_out,
            grad_tokens,
            grad_q,
            vectors["query_bias"],
            grad_k,
            grad_v,
            vectors["value_bias"],
            grad_o,
            vectors["out_bias"],
            vectors["gain_one"],
            vectors["shift_one"],
            vectors["gain_two"],
            vectors["shift_two"],
            up_sum[:, :width].T.astype(f32),
            up_sum[:, width].astype(f32),
            down_sum.astype(f32),
            vectors["down_bias"],
            vectors["halt"],
            small[len(names) * width : len(names) * width + 1],
        )

    return per_device


def solution(mesh):
    shared = P()
    rows = P("dp", "sq", None)
    return jax.shard_map(
        make_per_device(mesh.shape["dp"], mesh.shape["sq"]),
        mesh=mesh,
        in_specs=(rows, P("dp", None), P("dp", None), P("dp", "sq"))
        + (shared,) * 11
        + (P(None, "sq"), P("sq"), P("sq", None), shared, shared, shared, rows),
        out_specs=(rows, rows)
        + (shared,) * 11
        + (P(None, "sq"), P("sq"), P("sq", None), shared, shared, shared),
        check_vma=False,
    )
```

```python
import functools
import math

import jax
import jax.numpy as jnp
from jax import lax
from jax.experimental import pallas as pl
from jax.experimental.pallas import tpu as pltpu
from jax.sharding import PartitionSpec as P

HEAD = 64
STEPS = 3
LN_EPS = 1e-05
PONDER = 0.01
MASKED = -1e30
TOO_LARGE = 1e30
QUAD = 256
PAIR = 128
SHIFT_LANE = 16
BIAS_Q, BIAS_V, BIAS_O, BIAS_D, GAIN_1, SHIFT_1, GAIN_2, SHIFT_2, HALT_W, HALT_B = range(10)
HALTS, ALONE = 0, 1
AXES = ("dp", "sq")
VMEM_LIMIT = 20 * 2**20
HIGHEST = lax.Precision.HIGHEST
bf16 = jnp.bfloat16
f32 = jnp.float32

NN = (((1,), (0,)), ((), ()))
NT = (((1,), (1,)), ((), ()))
TN = (((0,), (0,)), ((), ()))


def dot(left, right, dims=NN):
    return lax.dot_general(left, right, dims, preferred_element_type=f32)


def split_two(values):
    high = values.astype(bf16)
    return high, (values - high.astype(f32)).astype(bf16)


def iota(shape, dim):
    return lax.broadcasted_iota(jnp.int32, shape, dim)


def head_lanes(groups):
    row, lane = iota((QUAD, PAIR), 0), iota((QUAD, PAIR), 1)
    place = lane - SHIFT_LANE
    hit = (place >= 0) & (place < 8 * groups) & (place % 8 == row // HEAD)
    return jnp.where(hit, 1.0, 0.0).astype(bf16)


def head_rows():
    hit = iota((8, QUAD), 0) == iota((8, QUAD), 1) // HEAD
    return jnp.where(hit, 1.0, 0.0).astype(bf16)


def head_block():
    hit = iota((QUAD, QUAD), 0) // HEAD == iota((QUAD, QUAD), 1) // HEAD
    return jnp.where(hit, 1.0, 0.0).astype(bf16)


def exact_three(values):
    group = (iota((1, PAIR), 1) - SHIFT_LANE) // 8
    high = values.astype(bf16).astype(f32)
    rest = values - high
    middle = rest.astype(bf16).astype(f32)
    low = rest - middle
    return jnp.where(group == 0, high, jnp.where(group == 1, middle, low)).astype(bf16)


def rows_to_lanes(rows, groups):
    count = rows.shape[1]
    parts = [jnp.zeros((SHIFT_LANE, count), f32)] + [rows] * groups
    parts.append(jnp.zeros((PAIR - SHIFT_LANE - 8 * groups, count), f32))
    return jnp.concatenate(parts, 0).T


def pair_of(values, head):
    start = head // 2 * PAIR
    return values[:, start : start + PAIR]


def only_head(values, head):
    return jnp.where(iota((1, PAIR), 1) // HEAD == head % 2, pair_of(values, head), bf16(0))


def shift_lanes(shift, features, head, groups=1):
    place = iota((1, PAIR), 1) - SHIFT_LANE
    hit = (place >= 0) & (place < 8 * groups) & (place % 8 == head)
    return jnp.where(hit, -shift, features)


def norm_stats(values):
    centered = values - jnp.mean(values, axis=-1, keepdims=True)
    inverse = lax.rsqrt(jnp.mean(centered * centered, axis=-1, keepdims=True) + LN_EPS)
    return centered * inverse, inverse


def norm_back(grad, normal, inverse, gain):
    scaled = grad * gain
    return inverse * (
        scaled
        - jnp.mean(scaled, axis=-1, keepdims=True)
        - normal * jnp.mean(scaled * normal, axis=-1, keepdims=True)
    )


def near_kernel(
    own_ref, mate_ref, wq_ref, wk_ref, wv_ref, rows_ref, qf_ref, kf_ref, alone_ref,
    q_ref, k_ref, v_ref, mixed_ref, lse_ref, vt_ref,
):
    count = own_ref.shape[0]
    own = own_ref[...]
    bias_q, bias_v = rows_ref[BIAS_Q : BIAS_Q + 1, :], rows_ref[BIAS_V : BIAS_V + 1, :]
    q_ref[...] = (dot(own, wq_ref[...]) + bias_q).astype(bf16) * bf16(1.0 / math.sqrt(HEAD))
    for place, rows in ((0, own), (1, mate_ref[...])):
        here = pl.ds(place * count, count)
        k_ref[here, :] = dot(rows, wk_ref[...]).astype(bf16)
        v_ref[here, :] = (dot(rows, wv_ref[...]) + bias_v).astype(bf16)
    vt_ref[...] = v_ref[...].T
    high, low = split_two(q_ref[...].astype(f32) * k_ref[:count, :].astype(f32))
    shift = dot(high, head_lanes(1)).astype(bf16)
    self_score = dot(head_rows(), high, NT) + dot(head_rows(), low, NT)
    pick = jnp.where(iota((8, PAIR), 1) == iota((8, PAIR), 0) + SHIFT_LANE, 1.0, 0.0).astype(bf16)
    base = dot(pick, shift, NT)
    lse_ref[...] = jnp.zeros_like(lse_ref)

    def one_head(head, exact):
        query = jnp.concatenate(
            [only_head(q_ref[...], head), shift_lanes(shift, qf_ref[...], head)], 1
        )
        keys = jnp.concatenate([pair_of(k_ref, head), kf_ref[...]], 1)
        scores = dot(keys, query, NT)
        start = base[head : head + 1]
        if exact:
            top = jnp.maximum(jnp.max(scores, axis=0, keepdims=True), 0.0)
            scores = scores - top
            start = start + top
        probs = jnp.exp(scores)
        total = jnp.sum(probs, axis=0, keepdims=True)
        lanes = pl.ds(head * HEAD, HEAD)
        mixed = dot(vt_ref[lanes, :], probs.astype(bf16))
        alone = jnp.exp(self_score[head : head + 1] - start) * alone_ref[0:1, :]
        total = total + alone
        mixed = mixed + vt_ref[lanes, :count].astype(f32) * alone
        mixed_ref[lanes, :] = mixed / total
        lse_ref[head : head + 1, :] = start + jnp.log(total)
        return total

    most = functools.reduce(jnp.maximum, [one_head(head, False) for head in range(4)])

    @pl.when(jnp.logical_not(jnp.max(most) < TOO_LARGE))
    def _():
        for head in range(4):
            one_head(head, True)


def far_kernel(blocks, *refs):
    block_refs, refs = refs[:blocks], refs[blocks:]
    wk_ref, wv_ref, rows_ref, qf_ref, kf_ref, q_ref, near_ref, near_lse_ref = refs[:8]
    k_ref, v_ref, mixed_ref, lse_ref, vt_ref, total_ref = refs[8:]
    count = q_ref.shape[0]
    bias_v = rows_ref[BIAS_V : BIAS_V + 1, :]
    for place, block_ref in enumerate(block_refs):
        here = pl.ds(place * count, count)
        rows = block_ref[...]
        k_ref[here, :] = dot(rows, wk_ref[...]).astype(bf16)
        v_ref[here, :] = (dot(rows, wv_ref[...]) + bias_v).astype(bf16)
    vt_ref[...] = v_ref[...].T
    near_lse = near_lse_ref[...]
    base = near_lse.astype(bf16).astype(f32)
    shift = rows_to_lanes(base, 1).astype(bf16)
    lse_ref[...] = jnp.zeros_like(lse_ref)

    def one_head(head, exact):
        query = jnp.concatenate(
            [only_head(q_ref[...], head), shift_lanes(shift, qf_ref[...], head)], 1
        )
        keys = jnp.concatenate([pair_of(k_ref, head), kf_ref[...]], 1)
        scores = dot(keys, query, NT)
        start = base[head : head + 1]
        if exact:
            top = jnp.maximum(jnp.max(scores, axis=0, keepdims=True), 0.0)
            scores = scores - top
            start = start + top
        probs = jnp.exp(scores)
        total = jnp.sum(probs, axis=0, keepdims=True)
        lanes = pl.ds(head * HEAD, HEAD)
        mixed = dot(vt_ref[lanes, :], probs.astype(bf16))
        before = jnp.exp(near_lse[head : head + 1] - start)
        total = total + before
        total_ref[lanes, :] = (mixed + near_ref[lanes, :] * before) / total
        lse_ref[head : head + 1, :] = start + jnp.log(total)
        return total

    most = functools.reduce(jnp.maximum, [one_head(head, False) for head in range(4)])

    @pl.when(jnp.logical_not(jnp.max(most) < TOO_LARGE))
    def _():
        for head in range(4):
            one_head(head, True)

    mixed_ref[...] = total_ref[...].T.astype(bf16)


def back_kernel(
    with_self, blocks, q_ref, do_ref, o_ref, lse_ref, k_ref, v_ref, kf_ref, wk_ref, wv_ref, qf_ref,
    *refs,
):
    if with_self:
        part_q_ref, cols_ref = refs[:2]
        refs = refs[2:]
    dq_ref, dk_ref, dv_ref, sum_ref = refs[:4]
    da_refs = refs[4 : 4 + blocks]
    kt_ref, dqt_ref, dkf_ref, dvf_ref, daf_ref = refs[4 + blocks :]
    count = q_ref.shape[0]
    step = pl.program_id(0)
    kt_ref[...] = k_ref[...].T
    query_all, grad_all = q_ref[...], do_ref[...]
    lse_terms = exact_three(rows_to_lanes(lse_ref[...], 3))
    high, low = split_two(grad_all.astype(f32) * o_ref[...].astype(f32))
    delta_terms = exact_three(dot(high, head_lanes(3)) + dot(low, head_lanes(3)))
    for head in range(4):
        query = only_head(query_all, head)
        grad = only_head(grad_all, head)
        keys = jnp.concatenate([pair_of(k_ref, head), kf_ref[...]], 1)
        values = jnp.concatenate([pair_of(v_ref, head), kf_ref[...]], 1)
        query_wide = jnp.concatenate([query, shift_lanes(lse_terms, qf_ref[...], head, 3)], 1)
        grad_wide = jnp.concatenate([grad, shift_lanes(delta_terms, bf16(0), head, 3)], 1)
        probs = jnp.exp(dot(keys, query_wide, NT))
        back = (probs * dot(values, grad_wide, NT)).astype(bf16)
        probs = probs.astype(bf16)
        pair = pl.ds(head // 2 * PAIR, PAIR)
        if head % 2 == 0:
            dvf_ref[:, pair] = dot(probs, grad)
            dkf_ref[:, pair] = dot(back, query)
        else:
            dvf_ref[:, pair] += dot(probs, grad)
            dkf_ref[:, pair] += dot(back, query)
        lanes = pl.ds(head * HEAD, HEAD)
        dqt_ref[lanes, :] = dot(kt_ref[lanes, :], back)
    dq = dqt_ref[...].T
    if with_self:
        block = head_block()
        own_k, own_v = k_ref[:count, :].astype(f32), v_ref[:count, :].astype(f32)
        query_f, grad_f = query_all.astype(f32), grad_all.astype(f32)

        def per_head(values):
            first, second = split_two(values)
            return dot(first, block) + dot(second, block)

        spread = jnp.where(
            (iota((PAIR, QUAD), 0) >= SHIFT_LANE)
            & (iota((PAIR, QUAD), 0) < SHIFT_LANE + 24)
            & (iota((PAIR, QUAD), 0) % 8 == iota((PAIR, QUAD), 1) // HEAD),
            1.0,
            0.0,
        ).astype(bf16)
        prob = jnp.exp(per_head(query_f * own_k) - dot(lse_terms, spread)) * cols_ref[:, ALONE : ALONE + 1]
        back = prob * (per_head(grad_f * own_v) - dot(delta_terms, spread))
        dq = dq + back * own_k
        dkf_ref[:count, :] += back * query_f
        dvf_ref[:count, :] += prob * grad_f
    dq = dq * (1.0 / math.sqrt(HEAD))
    if with_self:
        dq = (dq + part_q_ref[...]).astype(bf16)
        sum_ref[0:1, :] = jnp.sum(dq.astype(f32), axis=0, keepdims=True)
    else:
        sum_ref[0:1, :] = jnp.zeros((1, QUAD), f32)
    dq_ref[...] = dq
    dk, dv = dkf_ref[...].astype(bf16), dvf_ref[...].astype(bf16)
    dk_ref[...] = dk
    dv_ref[...] = dv
    sum_ref[1:2, :] = jnp.sum(dvf_ref[...], axis=0, keepdims=True)
    part = dot(dk, wk_ref[...], NT) + dot(dv, wv_ref[...], NT)

    @pl.when(step == 0)
    def _():
        daf_ref[...] = part

    @pl.when(step > 0)
    def _():
        daf_ref[...] += part

    @pl.when(step == pl.num_programs(0) - 1)
    def _():
        for place, da_ref in enumerate(da_refs):
            da_ref[...] = daf_ref[place * count : (place + 1) * count, :].astype(bf16)


def mix_kernel(
    step_no, last, x_ref, o_ref, wo_ref, rows_ref, up_a_ref, up_b_ref, down_a_ref, down_b_ref,
    cols_ref, hidden_ref, normed_ref, act_ref, slope_ref, new_ref, *refs,
):
    if last:
        (total_ref,) = refs
    else:
        next_ref, total_ref = refs
    step = pl.program_id(0)
    width = x_ref.shape[1]

    def row(place):
        return rows_ref[place : place + 1, :]

    @pl.when(step == 0)
    def _():
        hidden = x_ref[...] + (dot(o_ref[...], wo_ref[...]) + row(BIAS_O))
        hidden_ref[...] = hidden
        normal = norm_stats(hidden)[0]
        normed_ref[:, :width] = (normal * row(GAIN_2) + row(SHIFT_2)).astype(bf16)
        one = jnp.where(iota((x_ref.shape[0], PAIR), 1) == 0, 1.0, 0.0)
        normed_ref[:, width:] = one.astype(bf16)
        total_ref[...] = hidden + row(BIAS_D)

    in_first = step < pl.num_programs(0) // 2
    before = dot(normed_ref[...], jnp.where(in_first, up_a_ref[...], up_b_ref[...]), NT)
    root = math.sqrt(2.0 / math.pi)
    square = before * before
    bent = jnp.tanh(before * (root + root * 0.044715 * square))
    half = 0.5 + 0.5 * bent
    act = (before * half).astype(bf16)
    act_ref[...] = act
    slope_ref[...] = (
        half + 0.5 * before * (1.0 - bent * bent) * (root + 3.0 * root * 0.044715 * square)
    ).astype(bf16)
    total_ref[...] += dot(act, jnp.where(in_first, down_a_ref[...], down_b_ref[...]))

    @pl.when(step == pl.num_programs(0) - 1)
    def _():
        live = cols_ref[:, HALTS : HALTS + 1] >= step_no + 1
        new = jnp.where(live, total_ref[...], x_ref[...])
        new_ref[...] = new
        if not last:
            next_ref[...] = (norm_stats(new)[0] * row(GAIN_1) + row(SHIFT_1)).astype(bf16)


def unmix_kernel(
    step_no, grad_ref, cols_ref, slope_ref, up_a_ref, up_b_ref, down_a_ref, down_b_ref,
    hidden_ref, rows_ref, wo_ref, dz_ref, du_ref, dh_ref, dy_ref, do_ref, sum_ref, total_ref,
):
    in_first = pl.program_id(0) < pl.num_programs(0) // 2
    step = pl.program_id(0)
    width = grad_ref.shape[1]

    def live_grad():
        return jnp.where(cols_ref[:, HALTS : HALTS + 1] >= step_no + 1, grad_ref[...], 0.0)

    @pl.when(step == 0)
    def _():
        dz_ref[...] = live_grad().astype(bf16)

    down = jnp.where(in_first, down_a_ref[...], down_b_ref[...])
    du = (slope_ref[...].astype(f32) * dot(dz_ref[...], down, NT)).astype(bf16)
    du_ref[...] = du
    part = dot(du, jnp.where(in_first, up_a_ref[:, :width], up_b_ref[:, :width]))

    @pl.when(step == 0)
    def _():
        total_ref[...] = part

    @pl.when(step > 0)
    def _():
        total_ref[...] += part

    @pl.when(step == pl.num_programs(0) - 1)
    def _():
        normal, inverse = norm_stats(hidden_ref[...])
        back = total_ref[...]
        gain = rows_ref[GAIN_2 : GAIN_2 + 1, :]
        dh = live_grad() + norm_back(back, normal, inverse, gain)
        dh_ref[...] = dh
        dy = dh.astype(bf16)
        dy_ref[...] = dy
        do_ref[...] = dot(dy, wo_ref[...], NT).astype(bf16)
        sum_ref[0:1, :] = jnp.sum(dz_ref[...].astype(f32), axis=0, keepdims=True)
        sum_ref[1:2, :] = jnp.sum(dy.astype(f32), axis=0, keepdims=True)
        sum_ref[2:3, :] = jnp.sum(back * normal, axis=0, keepdims=True)
        sum_ref[3:4, :] = jnp.sum(back, axis=0, keepdims=True)


def half_of(first_ref, second_ref):
    in_first = pl.program_id(0) < pl.num_programs(0) // 2
    return jnp.where(in_first, first_ref[...], second_ref[...])


def join_kernel(
    step_no, received, dq_ref, wq_ref, near_ref, x_ref, rows_ref, grad_ref, cols_ref, dh_ref,
    halt_ref, cot_a_ref, cot_b_ref, *refs,
):
    parts, (new_ref, sum_ref) = refs[:received], refs[received:]
    back = dot(dq_ref[...], wq_ref[...], NT) + near_ref[...].astype(f32)
    for part in parts:
        back = back + part[...].astype(f32)
    values = x_ref[...]
    normal, inverse = norm_stats(values)
    slope = halt_ref[:, step_no : step_no + 1]
    passed = jnp.where(cols_ref[:, HALTS : HALTS + 1] >= step_no + 1, 0.0, grad_ref[...])
    new = (
        passed
        + dh_ref[...]
        + norm_back(back, normal, inverse, rows_ref[GAIN_1 : GAIN_1 + 1, :])
        + slope * rows_ref[HALT_W : HALT_W + 1, :]
    )
    if step_no > 0:
        weight = halt_ref[:, STEPS + step_no - 1 : STEPS + step_no]
        new = new + weight * half_of(cot_a_ref, cot_b_ref).astype(f32)
    new_ref[...] = new
    sums = [back * normal, back, slope * values]

    @pl.when(pl.program_id(0) == 0)
    def _():
        sum_ref[...] = jnp.zeros_like(sum_ref)

    for place, item in enumerate(sums):
        sum_ref[place : place + 1, :] += jnp.sum(item, axis=0, keepdims=True)


def halt_kernel(*refs):
    state_refs = refs[: STEPS + 1]
    rows_ref, cols_ref, cot_a_ref, cot_b_ref, acted_ref, grad_ref, halt_ref, sum_ref = refs[
        STEPS + 1 :
    ]
    states = [ref[...] for ref in state_refs]
    cot = half_of(cot_a_ref, cot_b_ref).astype(f32)
    halts = cols_ref[:, HALTS : HALTS + 1]
    halt_row = rows_ref[HALT_W : HALT_W + 1, :]
    halt_bias = rows_ref[HALT_B : HALT_B + 1, 0:1]
    final_dot = jnp.sum(cot * states[STEPS], axis=-1, keepdims=True)
    remainder = jnp.ones_like(halts)
    acted = jnp.zeros_like(states[0])
    slopes, weights = [], []
    for step in range(STEPS):
        logit = jnp.sum(states[step] * halt_row, axis=-1, keepdims=True) + halt_bias
        prob = (1.0 / (1.0 + jnp.exp(-logit))) / STEPS
        early = halts > step + 1
        weight = jnp.where(early, prob, 0.0)
        weights.append(weight)
        remainder = remainder - weight
        acted = acted + weight * states[step + 1]
        step_dot = jnp.sum(cot * states[step + 1], axis=-1, keepdims=True)
        slope = (step_dot - final_dot - PONDER) * prob * (1.0 - STEPS * prob)
        slopes.append(jnp.where(early, slope, 0.0))
    acted_ref[...] = (acted + remainder * states[STEPS]).astype(bf16)
    grad_ref[...] = (remainder + weights[STEPS - 1]) * cot
    lane = iota((halts.shape[0], PAIR), 1)
    table = jnp.zeros((halts.shape[0], PAIR), f32)
    for place, column in enumerate(slopes + weights):
        table = jnp.where(lane == place, column, table)
    halt_ref[...] = table

    @pl.when(pl.program_id(0) == 0)
    def _():
        sum_ref[...] = jnp.zeros_like(sum_ref)

    sum_ref[0:1, :] += jnp.sum(jnp.where(lane < STEPS, table, 0.0), axis=0, keepdims=True)


def outset_kernel(
    tokens_ref, mask_ref, halts_ref, cot_ref, lengths_ref, own_ref, other_ref, cot_own_ref,
    cot_other_ref,
):
    seq_here, width = tokens_ref.shape[1:]
    parity = lax.axis_index("sq") % 2
    lane = iota((1, width), 1)

    def row_of(ref, row):
        return jnp.where(row == 0, ref[0:1, :], ref[1:2, :]).astype(f32)

    for row, out_ref, cot_out_ref in (
        (parity, own_ref, cot_own_ref), (1 - parity, other_ref, cot_other_ref)
    ):
        cot_out_ref[...] = cot_ref[row]
        out_ref[:seq_here, :] = tokens_ref[row]
        mask = row_of(mask_ref, row)
        parts = [mask[:, at : at + width] for at in range(0, mask.shape[1], width)]
        halts = row_of(halts_ref, row)
        if seq_here < width:
            halts = jnp.concatenate([halts, jnp.zeros((1, width - seq_here), f32)], 1)
        parts.append(halts)
        for part in (lambda value: value // 16, lambda value: value % 16):
            entry = jnp.zeros((1, width), jnp.int32)
            for doc in range(lengths_ref.shape[1]):
                entry = jnp.where(lane == doc, part(lengths_ref[row, doc]), entry)
            parts.append(entry.astype(f32))
        parts.append(jnp.zeros((out_ref.shape[0] - seq_here - len(parts), width), f32))
        out_ref[seq_here:, :] = jnp.concatenate(parts, 0).astype(bf16)


def begin_kernel(
    middle, docs, row_len, a_ref, b_ref, rows_ref, x_ref, normed_ref, qf_ref, near_ref, far_ref,
    cols_ref, alone_ref, row_ref,
):
    count, width = x_ref.shape
    seq_here = count // 2
    d_at, s_at = lax.axis_index("dp"), lax.axis_index("sq")
    top = 2 * middle
    parity, core, chip = s_at % 2, d_at % 2, s_at % top // 2
    for place, ref in enumerate((a_ref, b_ref)):
        here = pl.ds(place * seq_here, seq_here)
        values = ref[:seq_here, :].astype(f32)
        x_ref[here, :] = values
        normed_ref[here, :] = (
            norm_stats(values)[0] * rows_ref[GAIN_1 : GAIN_1 + 1, :]
            + rows_ref[SHIFT_1 : SHIFT_1 + 1, :]
        ).astype(bf16)
    info = a_ref[seq_here:, :].astype(f32)
    mask_rows = row_len // width
    for at in range(mask_rows):
        row_ref[:, at * width : (at + 1) * width] = jnp.broadcast_to(
            info[at : at + 1, :], (row_ref.shape[0], width)
        )
    lengths = info[mask_rows + 1 : mask_rows + 2, :] * 16.0 + info[mask_rows + 2 : mask_rows + 3, :]
    lane = iota((1, width), 1)
    ends = [
        jnp.sum(jnp.where(lane <= doc, lengths, 0.0), axis=1, keepdims=True)
        for doc in range(docs)
    ]

    def at_block(core_at, chip_at):
        start = (core_at * middle + chip_at) * count
        block = row_ref[0:1, pl.ds(pl.multiple_of(start, count), count)]
        turned = jnp.concatenate([block[:, seq_here:], block[:, :seq_here]], 1)
        offset = iota((1, count), 1) + parity * seq_here
        place = (start + jnp.where(offset >= count, offset - count, offset)).astype(f32)
        doc_at = jnp.zeros((1, count), jnp.int32)
        for end in ends:
            doc_at = doc_at + jnp.where(place >= end, 1, 0)
        return doc_at, jnp.where(parity == 0, block, turned)

    kind = iota((PAIR, 1), 0)

    def key_features(core_at, chip_at):
        doc_at, open_at = at_block(core_at, chip_at)
        closed = (kind == doc_at) | ((kind == 8) & (open_at == 0))
        ones = jnp.where(kind >= SHIFT_LANE, 1.0, 0.0)
        return jnp.where(closed, MASKED, jnp.broadcast_to(ones, closed.shape)).T.astype(bf16)

    doc_at, open_at = at_block(core, chip)
    wanted = ((kind < docs) & (kind != doc_at)) | (kind == 8)
    qf_ref[...] = jnp.where(wanted, 1.0, 0.0).T.astype(bf16)
    for place, core_at in enumerate((core, 1 - core)):
        near_ref[pl.ds(place * count, count), :] = key_features(core_at, chip)
    place = 0
    for offset in range(1, middle):
        for core_at in (core, 1 - core):
            far_ref[pl.ds(place * count, count), :] = key_features(core_at, chip ^ offset)
            place += 1
    halts = jnp.concatenate(
        [
            ref[seq_here:, :].astype(f32)[mask_rows : mask_rows + 1, :seq_here]
            for ref in (a_ref, b_ref)
        ],
        1,
    )
    alone = jnp.where(open_at == 0, 1.0, 0.0)
    alone_ref[...] = jnp.broadcast_to(alone, alone_ref.shape)
    table = jnp.where(kind == HALTS, halts, jnp.where(kind == ALONE, alone, 0.0))
    cols_ref[...] = table.T


def small_kernel(unmix_refs, near_refs, far_refs, join_refs, halt_ref, out_ref):
    def row(refs, place):
        return sum(ref[place : place + 1, :] for ref in refs)

    out_ref[...] = jnp.zeros_like(out_ref)
    entries = (
        row(near_refs, 0), row(near_refs, 1) + row(far_refs, 1), row(unmix_refs, 1),
        row(join_refs, 0), row(join_refs, 1), row(unmix_refs, 2), row(unmix_refs, 3),
        row(unmix_refs, 0), row(join_refs, 2),
    )
    for place, entry in enumerate(entries):
        out_ref[place : place + 1, :] = entry
    bias = jnp.sum(halt_ref[0:1, :], axis=1, keepdims=True)
    out_ref[len(entries) : len(entries) + 1, :] = jnp.broadcast_to(bias, (1, out_ref.shape[1]))


def hidden_grads_kernel(steps, *refs):
    act_refs, dz_refs, du_refs, normed_refs = (refs[i * steps : (i + 1) * steps] for i in range(4))
    out_ref = refs[4 * steps]
    wide = normed_refs[0].shape[1]
    out_ref[:, :wide] = sum(
        dot(du[...], normed[...], TN) for du, normed in zip(du_refs, normed_refs)
    ).astype(bf16)
    out_ref[:, wide:] = sum(
        dot(act[...], dz[...], TN) for act, dz in zip(act_refs, dz_refs)
    ).astype(bf16)


def pack_kernel(bits, *refs):
    sources, results = refs[: len(refs) // 3 * 2], refs[len(refs) // 3 * 2 :]
    blocks = 2 ** len(bits)
    rows = sources[0].shape[0] // blocks
    width = sources[0].shape[1]
    own = own_block(bits)
    for block in range(blocks):
        start = pl.multiple_of((own ^ block) * rows, rows)
        for place, source in enumerate(sources):
            lanes = pl.ds(place % 2 * width, width)
            results[place // 2][pl.ds(block * rows, rows), lanes] = source[
                pl.ds(start, rows), :
            ].astype(bf16)


def unpack_kernel(bits, *refs):
    sources, results = refs[: len(refs) // 3], refs[len(refs) // 3 :]
    blocks = 2 ** len(bits)
    rows = sources[0].shape[0] // blocks
    width = sources[0].shape[1] // 2
    own = own_block(bits)
    for block in range(blocks):
        start = pl.multiple_of((own ^ block) * rows, rows)
        for place, result in enumerate(results):
            lanes = pl.ds(place % 2 * width, width)
            result[pl.ds(block * rows, rows), :] = sources[place // 2][
                pl.ds(start, rows), lanes
            ].astype(f32)


def hidden_out_kernel(dp_bits, source_ref, up_ref, bias_ref, down_ref, wide_ref, order_ref):
    width = down_ref.shape[1]
    blocks = 2 ** len(dp_bits)
    rows = source_ref.shape[0] // blocks
    own = own_block([(bit, 0) for bit in dp_bits])
    wide_ref[...] = source_ref[...].astype(f32)
    for block in range(blocks):
        place = sum(
            (1 << at) for at, bit in enumerate(dp_bits[::-1]) if block & bit
        )
        start = pl.multiple_of((own ^ place) * rows, rows)
        order_ref[pl.ds(block * rows, rows), :] = wide_ref[pl.ds(start, rows), :]
    up_ref[...] = order_ref[:, :width].T
    bias_ref[...] = jnp.broadcast_to(order_ref[:, width : width + PAIR].T[0:1, :], bias_ref.shape)
    down_ref[...] = order_ref[:, width + PAIR :]


def own_block(bits):
    own = jnp.int32(0)
    for d_bit, s_bit in bits:
        at = lax.axis_index("dp") & d_bit if d_bit else lax.axis_index("sq") & s_bit
        own = own * 2 + jnp.where(at != 0, 1, 0)
    return own


def whole(shape):
    return pl.BlockSpec(shape, lambda i: (0,) * len(shape))


def lanes_of(rows, width=QUAD):
    return pl.BlockSpec((rows, width), lambda i: (0, i))


def rows_of(rows, width):
    return pl.BlockSpec((rows, width), lambda i: (i, 0))


def shaped(shape, dtype):
    return jax.ShapeDtypeStruct(shape, dtype)


def in_hbm(value):
    return pltpu.with_memory_space_constraint(value, pltpu.HBM)


def params(flops, moved, exps=0):
    return dict(
        compiler_params=pltpu.CompilerParams(vmem_limit_bytes=VMEM_LIMIT),
        cost_estimate=pl.CostEstimate(
            flops=int(flops), bytes_accessed=int(moved), transcendentals=int(exps)
        ),
    )


def attend_near(own, mate, wq, wk, wv, rows, qf, kf, alone):
    count, width = own.shape
    quads = width // QUAD
    keys = 2 * count
    return pl.pallas_call(
        near_kernel,
        grid=(quads,),
        in_specs=[
            whole((count, width)), whole((count, width)),
            lanes_of(width), lanes_of(width), lanes_of(width), lanes_of(rows.shape[0]),
            whole((count, PAIR)), whole((keys, PAIR)), whole((8, count)),
        ],
        out_specs=[
            lanes_of(count), lanes_of(keys), lanes_of(keys), rows_of(QUAD, count),
            rows_of(8, count),
        ],
        out_shape=[
            shaped((count, width), bf16), shaped((keys, width), bf16), shaped((keys, width), bf16),
            shaped((width, count), f32), shaped((8 * quads, count), f32),
        ],
        scratch_shapes=[pltpu.VMEM((QUAD, keys), bf16)],
        name="attend_near",
        **params(8 * count * keys * width * 2, 10 * count * width * 2, count * keys * 8),
    )(own, mate, wq, wk, wv, rows, qf, kf, alone)


def attend_far(blocks, wk, wv, rows, qf, kf, queries, near_mixed, near_lse):
    count, width = queries.shape
    quads = width // QUAD
    keys = len(blocks) * count
    return pl.pallas_call(
        functools.partial(far_kernel, len(blocks)),
        grid=(quads,),
        in_specs=[whole((count, width))] * len(blocks)
        + [
            lanes_of(width), lanes_of(width), lanes_of(rows.shape[0]),
            whole((count, PAIR)), whole((keys, PAIR)), lanes_of(count), rows_of(QUAD, count),
            rows_of(8, count),
        ],
        out_specs=[lanes_of(keys), lanes_of(keys), lanes_of(count), rows_of(8, count)],
        out_shape=[
            shaped((keys, width), bf16), shaped((keys, width), bf16), shaped((count, width), bf16),
            shaped((8 * quads, count), f32),
        ],
        scratch_shapes=[pltpu.VMEM((QUAD, keys), bf16), pltpu.VMEM((QUAD, count), f32)],
        name="attend_far",
        **params(8 * count * keys * width * 2, 10 * count * width * 2, count * keys * 8),
    )(*blocks, wk, wv, rows, qf, kf, queries, near_mixed, near_lse)


def attend_back(queries, grad_mixed, mixed, lse, keys_in, values_in, kf, wk, wv, qf, partial, cols):
    count, width = queries.shape
    quads = width // QUAD
    keys = keys_in.shape[0]
    blocks = keys // count
    with_self = cols is not None
    extra = [partial, cols] if with_self else []
    extra_specs = [lanes_of(count), whole((count, PAIR))] if with_self else []
    return pl.pallas_call(
        functools.partial(back_kernel, with_self, blocks),
        grid=(quads,),
        in_specs=[
            lanes_of(count), lanes_of(count), lanes_of(count), rows_of(8, count), lanes_of(keys),
            lanes_of(keys), whole((keys, PAIR)), lanes_of(width), lanes_of(width),
            whole((count, PAIR)),
        ]
        + extra_specs,
        out_specs=[lanes_of(count), lanes_of(keys), lanes_of(keys), lanes_of(8)]
        + [whole((count, width))] * blocks,
        out_shape=[
            shaped((count, width), bf16 if with_self else f32), shaped((keys, width), bf16),
            shaped((keys, width), bf16), shaped((8, width), f32),
        ]
        + [shaped((count, width), bf16)] * blocks,
        scratch_shapes=[
            pltpu.VMEM((QUAD, keys), bf16), pltpu.VMEM((QUAD, count), f32),
            pltpu.VMEM((keys, QUAD), f32), pltpu.VMEM((keys, QUAD), f32),
            pltpu.VMEM((keys, width), f32),
        ],
        name="back_near" if with_self else "back_far",
        **params(20 * count * keys * width * 2, 20 * count * width * 2, count * keys * 8),
    )(queries, grad_mixed, mixed, lse, keys_in, values_in, kf, wk, wv, qf, *extra)


def halves_of(rows, width, steps):
    half = steps // 2
    return [
        pl.BlockSpec((rows, width), lambda i: (jnp.minimum(i, half - 1), 0)),
        pl.BlockSpec((rows, width), lambda i: (jnp.maximum(i - half, 0), 0)),
    ]


def mix(step_no, x, mixed, wo, rows, ups, downs, cols, last):
    count, width = x.shape
    hidden = 2 * ups[0].shape[0]
    chunk = min(512, hidden // 2)
    steps = hidden // chunk
    square = whole((count, width))
    wide = width + PAIR
    out_specs = [
        square, whole((count, wide)), lanes_of(count, chunk), lanes_of(count, chunk), square,
    ]
    out_shape = [
        shaped((count, width), f32), shaped((count, wide), bf16), shaped((count, hidden), bf16),
        shaped((count, hidden), bf16), shaped((count, width), f32),
    ]
    if not last:
        out_specs.append(square)
        out_shape.append(shaped((count, width), bf16))
    return pl.pallas_call(
        functools.partial(mix_kernel, step_no, last),
        grid=(hidden // chunk,),
        in_specs=[
            square, square, whole((width, width)), whole(rows.shape),
            *halves_of(chunk, wide, steps), *halves_of(chunk, width, steps),
            whole((count, PAIR)),
        ],
        out_specs=out_specs,
        out_shape=out_shape,
        scratch_shapes=[pltpu.VMEM((count, width), f32)],
        name="mix",
        **params(4 * count * width * hidden, 16 * count * width + 8 * width * hidden),
    )(x, mixed, wo, rows, *ups, *downs, cols)


def unmix(step_no, grad, cols, slope, ups, downs, hidden_state, rows, wo):
    count, width = grad.shape
    hidden = 2 * ups[0].shape[0]
    chunk = min(512, hidden // 2)
    steps = hidden // chunk
    square = whole((count, width))
    return pl.pallas_call(
        functools.partial(unmix_kernel, step_no),
        grid=(hidden // chunk,),
        in_specs=[
            square, whole((count, PAIR)), lanes_of(count, chunk),
            *halves_of(chunk, width + PAIR, steps), *halves_of(chunk, width, steps), square,
            whole(rows.shape), whole((width, width)),
        ],
        out_specs=[
            square, lanes_of(count, chunk), square, square, square, whole((8, width)),
        ],
        out_shape=[
            shaped((count, width), bf16), shaped((count, hidden), bf16), shaped((count, width), f32),
            shaped((count, width), bf16), shaped((count, width), bf16), shaped((8, width), f32),
        ],
        scratch_shapes=[pltpu.VMEM((count, width), f32)],
        name="unmix",
        **params(4 * count * width * hidden, 16 * count * width + 8 * width * hidden),
    )(grad, cols, slope, *ups, *downs, hidden_state, rows, wo)


def join(step_no, dq, wq, near, x, rows, grad, cols, dh, halt_table, cot, parts):
    count, width = x.shape
    piece = min(128, count // 2)
    part, table = rows_of(piece, width), rows_of(piece, PAIR)
    return pl.pallas_call(
        functools.partial(join_kernel, step_no, len(parts)),
        grid=(count // piece,),
        in_specs=[
            part, whole((width, width)), part, part, whole(rows.shape), part, table, part, table,
            *halves_of(piece, width, count // piece),
        ]
        + [part] * len(parts),
        out_specs=[part, whole((8, width))],
        out_shape=[shaped((count, width), f32), shaped((8, width), f32)],
        name="join",
        **params(2 * count * width * width, 24 * count * width),
    )(dq, wq, near, x, rows, grad, cols, dh, halt_table, *cot, *parts)


def halting(states, rows, cols, cot):
    count, width = states[0].shape
    piece = min(128, count // 2)
    part, table = rows_of(piece, width), rows_of(piece, PAIR)
    return pl.pallas_call(
        halt_kernel,
        grid=(count // piece,),
        in_specs=[part] * len(states) + [whole(rows.shape), table, *halves_of(piece, width, count // piece)],
        out_specs=[part, part, table, whole((8, PAIR))],
        out_shape=[
            shaped((count, width), bf16), shaped((count, width), f32), shaped((count, PAIR), f32),
            shaped((8, PAIR), f32),
        ],
        name="halting",
        **params(20 * count * width, 24 * count * width),
    )(*states, rows, cols, *cot)


def outset(tokens, mask, halts, cot, lengths):
    seq_here, width = tokens.shape[1:]
    here = pl.BlockSpec(memory_space=pltpu.VMEM)
    extra = -(-(mask.shape[1] // width + 3) // 16) * 16
    block = shaped((seq_here + extra, width), bf16)
    return pl.pallas_call(
        outset_kernel,
        in_specs=[here] * 4 + [pl.BlockSpec(memory_space=pltpu.SMEM)],
        out_specs=[here] * 4,
        out_shape=[block] * 2 + [shaped((seq_here, width), bf16)] * 2,
        name="outset",
        **params(0, 8 * seq_here * width),
    )(*map(in_hbm, (tokens, mask, halts, cot)), lengths)


def begin(middle, docs, row_len, blocks, rows, seq_here):
    width = blocks[0].shape[1]
    count = 2 * seq_here
    far = max(2 * (middle - 1), 1) * count
    here = pl.BlockSpec(memory_space=pltpu.VMEM)
    return pl.pallas_call(
        functools.partial(begin_kernel, middle, docs, row_len),
        in_specs=[here] * 3,
        out_specs=[here] * 7,
        out_shape=[
            shaped((count, width), f32), shaped((count, width), bf16),
            shaped((count, PAIR), bf16), shaped((2 * count, PAIR), bf16), shaped((far, PAIR), bf16),
            shaped((count, PAIR), f32), shaped((8, count), f32),
        ],
        scratch_shapes=[pltpu.VMEM((8, row_len), f32)],
        name="begin",
        **params(10 * count * width, 16 * count * width),
    )(*blocks, rows)


def small_sums(unmix_sums, near_sums, far_sums, join_sums, halt_sums):
    steps, width = len(unmix_sums), unmix_sums[0].shape[1]
    here = pl.BlockSpec(memory_space=pltpu.VMEM)

    def body(*refs):
        groups = [refs[at * steps : (at + 1) * steps] for at in range(4)]
        small_kernel(*groups, *refs[4 * steps :])

    return pl.pallas_call(
        body,
        in_specs=[here] * (4 * steps + 1),
        out_specs=here,
        out_shape=shaped((16, width), f32),
        name="small_sums",
        **params(0, 64 * width),
    )(*unmix_sums, *near_sums, *far_sums, *join_sums, halt_sums)


def hidden_grads(acts, dzs, dus, normeds):
    count, hidden = acts[0].shape
    width, wide = dzs[0].shape[1], normeds[0].shape[1]
    chunk = min(256, hidden)
    tall = lanes_of(count, chunk)
    steps = len(acts)
    return pl.pallas_call(
        functools.partial(hidden_grads_kernel, steps),
        grid=(hidden // chunk,),
        in_specs=[tall] * steps
        + [whole((count, width))] * steps
        + [tall] * steps
        + [whole((count, wide))] * steps,
        out_specs=rows_of(chunk, wide + width),
        out_shape=shaped((hidden, wide + width), bf16),
        name="hidden_grads",
        **params(4 * steps * count * width * hidden, 4 * steps * count * hidden),
    )(*map(in_hbm, acts), *dzs, *map(in_hbm, dus), *normeds)


def pack(bits, sources):
    rows, width = sources[0].shape
    here = pl.BlockSpec(memory_space=pltpu.VMEM)
    return pl.pallas_call(
        functools.partial(pack_kernel, bits),
        in_specs=[here] * len(sources),
        out_specs=[here] * (len(sources) // 2),
        out_shape=[shaped((rows, 2 * width), bf16)] * (len(sources) // 2),
        name="pack",
        **params(0, 6 * rows * width * len(sources)),
    )(*sources)


def unpack(bits, sources):
    rows, width = sources[0].shape
    here = pl.BlockSpec(memory_space=pltpu.VMEM)
    return pl.pallas_call(
        functools.partial(unpack_kernel, bits),
        in_specs=[here] * len(sources),
        out_specs=[here] * (2 * len(sources)),
        out_shape=[shaped((rows, width // 2), f32)] * (2 * len(sources)),
        name="unpack",
        **params(0, 6 * rows * width * len(sources)),
    )(*sources)


def hidden_out(dp_bits, source, width):
    rows = source.shape[0]
    here = pl.BlockSpec(memory_space=pltpu.VMEM)
    return pl.pallas_call(
        functools.partial(hidden_out_kernel, dp_bits),
        in_specs=[here],
        out_specs=[here] * 3,
        out_shape=[shaped((width, rows), f32), shaped((8, rows), f32), shaped((rows, width), f32)],
        scratch_shapes=[pltpu.VMEM(source.shape, f32), pltpu.VMEM(source.shape, f32)],
        name="hidden_out",
        **params(0, 6 * rows * source.shape[1]),
    )(source)


def make_per_device(dp_size, sq_size):
    middle = sq_size // 4
    top = sq_size // 2

    def permute(value, move):
        pairs = []
        for d in range(dp_size):
            for s in range(sq_size):
                to_d, to_s = move(d, s)
                pairs.append((d * sq_size + s, to_d * sq_size + to_s))
        return lax.ppermute(value, AXES, pairs)

    def swap(value, d_bits, s_bits):
        return permute(value, lambda d, s: (d ^ d_bits, s ^ s_bits))

    def regroup(flip):
        def move(d, s):
            upper, core = s // top, d % 2
            return d - core + upper, (core * top + s % top) ^ flip

        return move

    def bits_of(size):
        return [1 << place for place in range(size.bit_length() - 1)]

    dp_bits, sq_bits = bits_of(dp_size), bits_of(sq_size)
    bit_names = [(bit, 0) for bit in dp_bits] + [(0, bit) for bit in sq_bits[::-1]]

    def with_bits(value, names=bit_names):
        return value.reshape((2,) * len(names) + (-1,) + value.shape[len(value.shape) - 1 :])

    def offsets_of(group):
        result = []
        for code in range(1, 2 ** len(group)):
            digits = [code >> (len(group) - 1 - at) & 1 for at in range(len(group))]
            move = [0, 0]
            for digit, (d_bit, s_bit) in zip(digits, group):
                move[0] |= d_bit * digit
                move[1] |= s_bit * digit
            result.append((tuple(move), digits))
        return result

    class Gather:
        def __init__(self, piece, order, axes=()):
            self.piece, self.order, self.axes = piece, list(order), list(axes)

        def start(self):
            return [swap(self.piece, *move) for move, _ in offsets_of(self.order[0])]

        def finish(self, arrived):
            group = self.order.pop(0)
            first = bit_names.index(group[0])
            place = sum(bit_names.index(axis[0]) < first for axis in self.axes)
            self.axes.insert(place, group)
            self.piece = jnp.stack([self.piece] + list(arrived), place)

    class Scatter:
        def __init__(self, total, order, names=bit_names):
            self.piece, self.order, self.names = with_bits(total, names), list(order), list(names)

        def start(self):
            group = self.order[0]
            sent = []
            for move, digits in [(None, [0] * len(group))] + offsets_of(group):
                part = self.piece
                taken = sorted(zip(group, digits), key=lambda item: -self.names.index(item[0]))
                for name, digit in taken:
                    part = lax.index_in_dim(part, digit, self.names.index(name), False)
                if move is None:
                    self.kept = part
                else:
                    sent.append(swap(part, *move))
            return sent

        def finish(self, arrived):
            for name in self.order.pop(0):
                self.names.remove(name)
            self.piece = self.kept
            for item in arrived:
                self.piece = self.piece + item

    class Small:
        def __init__(self, total, order):
            self.piece, self.order = total, list(order)

        def start(self):
            return [swap(self.piece, *move) for move, _ in offsets_of(self.order[0])]

        def finish(self, arrived):
            self.order.pop(0)
            for item in arrived:
                self.piece = self.piece + item

    def together(chains, others=()):
        chains = [chain for chain in chains if chain.order]
        sent = [chain.start() for chain in chains]
        flat = [item for items in sent for item in items] + list(others)
        if flat:
            flat = list(lax.optimization_barrier(tuple(flat)))
        for chain, items in zip(chains, sent):
            chain.finish([flat.pop(0) for _ in items])
        return flat

    def own_part(shard):
        rows = shard.shape[0] // dp_size
        return lax.dynamic_slice_in_dim(shard, lax.axis_index("dp") * rows, rows, 0)

    def turn(total):
        shape = total.shape
        total = with_bits(total)
        for axis, (d_bit, s_bit) in enumerate(bit_names):
            own = ((lax.axis_index("dp") & d_bit) | (lax.axis_index("sq") & s_bit)) != 0
            total = jnp.where(own, jnp.flip(total, axis), total)
        return total.reshape(shape)

    def after(value, *others):
        return lax.optimization_barrier((value,) + others)[0]

    def per_device(
        tokens, lengths, key_mask, halt_steps, query_weight, query_bias, key_weight, value_weight,
        value_bias, out_weight, out_bias, first_gain, first_shift, second_gain, second_shift,
        up_weight, up_bias, down_weight, down_bias, halt_weight, halt_bias, cotangent,
    ):
        seq_here, width = tokens.shape[1:]
        parity = lax.axis_index("sq") % 2

        def send_back(value):
            return [
                permute(value[:seq_here], regroup(0)), permute(value[seq_here:], regroup(1))
            ]

        def unspread(own, other):
            first = jnp.where(parity == 0, own, other)
            second = jnp.where(parity == 0, other, own)
            return jnp.stack([first, second], 0)

        *leaving, cot_own, cot_other = outset(tokens, key_mask, halt_steps, cotangent, lengths)
        tokens_here = [permute(block, regroup(flip)) for flip, block in enumerate(leaving)]
        core_bit, side = (1, 0), (0, 1)
        z_bits = tuple((0, bit) for bit in sq_bits[::-1][:-1])
        y_order = [((bit, 0),) for bit in dp_bits[1:]]
        z_order = [(bit,) for bit in z_bits]
        up_wide = jnp.concatenate(
            [up_weight.T, jnp.pad(up_bias[:, None], ((0, 0), (0, PAIR - 1)))], 1
        )
        gathers = [
            Gather(own_part(up_wide), z_order + [(side,)] + y_order),
            Gather(own_part(down_weight), z_order + y_order + [(side,)]),
        ]

        def gather_step(*others):
            sent = [gather.start() for gather in gathers]
            for gather, items in zip(gathers, sent):
                gather.finish([after(item, *others) for item in items])

        def gathered():
            return [gather.piece for gather in gathers]

        rows = jnp.stack(
            [
                item.astype(f32)
                for item in (
                    query_bias, value_bias, out_bias, down_bias, first_gain, first_shift,
                    second_gain, second_shift, halt_weight, jnp.broadcast_to(halt_bias, (width,)),
                )
            ]
            + [jnp.zeros((width,), f32)] * 6
        )
        gather_step()
        tokens_here = [after(item, *gathered()) for item in tokens_here]
        x, normed, query_feats, near_feats, far_feats, cols, alone_row = begin(
            middle, lengths.shape[1], key_mask.shape[1], tokens_here, rows, seq_here
        )

        states, kept = [x], []
        for step in range(STEPS):
            x = states[-1]
            arrived = [swap(normed, 0, offset * 2) for offset in range(1, middle)]
            mate = swap(normed, 1, 0)
            if step == 0:
                gather_step(normed)
                mate = after(mate, *gathered())
            queries, keys_near, values_near, near_mixed, near_lse = attend_near(
                normed, mate, query_weight, key_weight, value_weight, rows, query_feats,
                near_feats, alone_row,
            )
            if step == 0:
                gather_step(near_lse)
                arrived = [after(block, *gathered()) for block in arrived]
            far = []
            for block in arrived:
                block = after(block, near_lse)
                far += [block, swap(block, 1, 0)]
            if step == 1:
                cot = [
                    permute(after(block, far[0]), regroup(flip))
                    for flip, block in enumerate((cot_own, cot_other))
                ]
            keys_far, values_far, mixed, lse = attend_far(
                far, key_weight, value_weight, rows, query_feats, far_feats, queries, near_mixed,
                near_lse,
            )
            if step == 0:
                gather_step(lse)
                while gathers[0].order:
                    gather_step()
                halves = []
                for gather, weight in zip(gathers, (up_wide, down_weight)):
                    half = gather.piece.reshape(-1, weight.shape[1])
                    halves.append((half, swap(half, *core_bit)))
                up_rows, down_rows = halves
            out = mix(
                step, x, mixed, out_weight, rows, up_rows, down_rows, cols, step == STEPS - 1
            )
            hidden, normed_two, act, slope, new = out[:5]
            kept.append(
                (normed, mate, far, queries, keys_near, values_near, keys_far, values_far, mixed,
                 lse, hidden, normed_two, act, slope)
            )
            states.append(new)
            if step < STEPS - 1:
                normed = out[5]
            if step == 1:
                normed, *cot = lax.optimization_barrier((normed, *cot))

        acted, grad, halt_table, halt_sums = halting(states, rows, cols, cot)
        acted_sent = send_back(acted)
        total = {}

        def add(name, value):
            total[name] = total[name] + value if name in total else value

        small_parts = ([], [], [], [])
        hidden_parts = []
        for step in reversed(range(STEPS)):
            (normed, mate, far, queries, keys_near, values_near, keys_far, values_far, mixed, lse,
             hidden, normed_two, act, slope) = kept[step]
            dz, du, dh, dy, grad_mixed, sums = unmix(
                step, grad, cols, slope, up_rows, down_rows, hidden, rows, out_weight
            )
            hidden_parts.append((act, dz, du, normed_two))
            small_parts[0].append(sums)
            add("out", dot(mixed, dy, TN))
            if step == 0:
                hidden_part = hidden_grads(*zip(*hidden_parts))
                grad_mixed = after(grad_mixed, hidden_part)
                hidden_sum = Scatter(hidden_part, [(core_bit,)])
                together([hidden_sum])
                names, wide = hidden_sum.names, normed_two.shape[1]
                hidden_sums = [
                    Scatter(hidden_sum.piece[..., :wide], y_order + [(side,)], names),
                    Scatter(hidden_sum.piece[..., wide:], [(side,)] + y_order, names),
                ]
            part_q, dk_far, dv_far, far_sums, *da_far = attend_back(
                queries, grad_mixed, mixed, lse, keys_far, values_far, far_feats, key_weight,
                value_weight, query_feats, None, None,
            )
            if step == STEPS - 1:
                *da_far, acted_own, acted_other = lax.optimization_barrier(
                    (*da_far, *acted_sent)
                )
                acted_sent = [acted_own, acted_other]
            crossed = [swap(part, 1, 0) for part in da_far[1::2]]
            for place, block in enumerate(far):
                here = slice(place * seq_here * 2, (place + 1) * seq_here * 2)
                add("key", dot(block, dk_far[here], TN))
                add("value", dot(block, dv_far[here], TN))
            total["key"], total["value"], *crossed = lax.optimization_barrier(
                (total["key"], total["value"], *crossed)
            )
            summed = [part + other for part, other in zip(da_far[0::2], crossed)]
            sent = [swap(part, 0, (at + 1) * 2) for at, part in enumerate(summed)]
            held = [part_q, total["out"], *summed]
            if step == 0:
                held += [item.piece for item in hidden_sums]
            part_q, total["out"], *pieces = lax.optimization_barrier(tuple(held))
            pieces = pieces[len(summed) :]
            if step == 0:
                for item, piece in zip(hidden_sums, pieces):
                    item.piece = piece
                hidden_sent = [item.start()[0] for item in hidden_sums]
            dq, dk_near, dv_near, near_sums, da_own, da_mate = attend_back(
                queries, grad_mixed, mixed, lse, keys_near, values_near, near_feats, key_weight,
                value_weight, query_feats, part_q, cols,
            )
            small_parts[1].append(near_sums)
            small_parts[2].append(far_sums)
            if step == 0:
                da_mate, *hidden_sent = lax.optimization_barrier((da_mate, *hidden_sent))
            da_mate, *sent = lax.optimization_barrier((da_mate, *sent))
            arrived = swap(da_mate, 1, 0)
            for place, block in enumerate((normed, mate)):
                here = slice(place * seq_here * 2, (place + 1) * seq_here * 2)
                add("key", dot(block, dk_near[here], TN))
                add("value", dot(block, dv_near[here], TN))
            add("query", dot(normed, dq, TN))
            if step > 0:
                dq, total["query"], total["key"], total["value"] = lax.optimization_barrier(
                    (dq, total["query"], total["key"], total["value"])
                )
            grad, join_sums = join(
                step, dq, query_weight, da_own, states[step], rows, grad, cols, dh, halt_table,
                cot, sent + [arrived],
            )
            small_parts[3].append(join_sums)

        squares = [total["query"], total["key"], total["value"], total["out"]]
        by_kernel = width % (16 * 2 ** len(bit_names)) == 0
        if by_kernel:
            squares = pack(bit_names, squares)
        else:
            squares = [
                turn(jnp.concatenate(squares[place : place + 2], 1).astype(bf16))
                for place in (0, 2)
            ]
        names = (
            "query_bias", "value_bias", "out_bias", "gain_one", "shift_one", "gain_two",
            "shift_two", "down_bias", "halt",
        )
        small = small_sums(*small_parts, halt_sums).reshape(-1)
        for item, arrived in zip(hidden_sums, hidden_sent):
            item.finish([arrived])
        sums = [
            Scatter(squares[0], [(core_bit,)] + y_order + [(side,)]),
            Scatter(squares[1], [(core_bit,), (side,)] + y_order),
        ]
        (grad,) = together(sums + hidden_sums, [grad])
        while hidden_sums[0].order:
            together(hidden_sums)
        hidden_all = Scatter(
            jnp.concatenate([item.piece for item in hidden_sums], -1), [z_bits], z_bits
        )
        small = Small(small, [(core_bit,)] + y_order + [(side,), z_bits])
        grad_sent = together(sums + [hidden_all, small], send_back(grad.astype(bf16)))
        grad_tokens = unspread(*grad_sent).astype(f32)
        hidden_all = Gather(hidden_all.piece, y_order[::-1] + [(core_bit,)])
        while sums[0].order:
            together(sums + [hidden_all, small])
        both = Scatter(
            jnp.concatenate([item.piece for item in sums], -1), [z_bits], z_bits
        )
        together([both, hidden_all, small])
        both = Gather(both.piece, [z_bits])
        together([both, hidden_all, small])
        sums = [
            Gather(
                both.piece[..., place * 2 * width : (place + 1) * 2 * width],
                order[::-1] + [(core_bit,)],
                [z_bits],
            )
            for place, order in enumerate((y_order + [(side,)], [(side,)] + y_order))
        ]
        while sums[0].order:
            together(sums + [hidden_all, small])
        while hidden_all.order or small.order:
            together([hidden_all, small])
        small = small.piece
        up_out, up_bias_out, down_out = hidden_out(
            dp_bits, hidden_all.piece.reshape(-1, hidden_part.shape[1]), width
        )
        squares = [item.piece.reshape(width, 2 * width) for item in sums]
        if by_kernel:
            grad_q, grad_k, grad_v, grad_o = unpack(bit_names, squares)
        else:
            grad_q, grad_k, grad_v, grad_o = (
                turn(item)[:, place * width : (place + 1) * width].astype(f32)
                for item in squares
                for place in range(2)
            )
        vectors = {name: small[i * width : (i + 1) * width] for i, name in enumerate(names)}
        return (
            unspread(*acted_sent),
            grad_tokens,
            grad_q,
            vectors["query_bias"],
            grad_k,
            grad_v,
            vectors["value_bias"],
            grad_o,
            vectors["out_bias"],
            vectors["gain_one"],
            vectors["shift_one"],
            vectors["gain_two"],
            vectors["shift_two"],
            up_out,
            up_bias_out[0],
            down_out,
            vectors["down_bias"],
            vectors["halt"],
            small[len(names) * width : len(names) * width + 1],
        )

    return per_device


def solution(mesh):
    shared = P()
    rows = P("dp", "sq", None)
    return jax.shard_map(
        make_per_device(mesh.shape["dp"], mesh.shape["sq"]),
        mesh=mesh,
        in_specs=(rows, P("dp", None), P("dp", None), P("dp", "sq"))
        + (shared,) * 11
        + (P(None, "sq"), P("sq"), P("sq", None), shared, shared, shared, rows),
        out_specs=(rows, rows)
        + (shared,) * 11
        + (P(None, "sq"), P("sq"), P("sq", None), shared, shared, shared),
        check_vma=False,
    )
```

```python
import functools
import math

import jax
import jax.numpy as jnp
from jax import lax
from jax.experimental import pallas as pl
from jax.experimental.pallas import tpu as pltpu
from jax.sharding import PartitionSpec as P

HEAD = 64
STEPS = 3
LN_EPS = 1e-05
PONDER = 0.01
MASKED = -1e30
TOO_LARGE = 1e30
QUAD = 256
PAIR = 128
SHIFT_LANE = 16
BIAS_Q, BIAS_V, BIAS_O, BIAS_D, GAIN_1, SHIFT_1, GAIN_2, SHIFT_2, HALT_W, HALT_B = range(10)
HALTS, ALONE = 0, 1
AXES = ("dp", "sq")
VMEM_LIMIT = 20 * 2**20
HIGHEST = lax.Precision.HIGHEST
bf16 = jnp.bfloat16
f32 = jnp.float32

NN = (((1,), (0,)), ((), ()))
NT = (((1,), (1,)), ((), ()))
TN = (((0,), (0,)), ((), ()))


def dot(left, right, dims=NN):
    return lax.dot_general(left, right, dims, preferred_element_type=f32)


def split_two(values):
    high = values.astype(bf16)
    return high, (values - high.astype(f32)).astype(bf16)


def iota(shape, dim):
    return lax.broadcasted_iota(jnp.int32, shape, dim)


def head_lanes(groups):
    row, lane = iota((QUAD, PAIR), 0), iota((QUAD, PAIR), 1)
    place = lane - SHIFT_LANE
    hit = (place >= 0) & (place < 8 * groups) & (place % 8 == row // HEAD)
    return jnp.where(hit, 1.0, 0.0).astype(bf16)


def head_rows():
    hit = iota((8, QUAD), 0) == iota((8, QUAD), 1) // HEAD
    return jnp.where(hit, 1.0, 0.0).astype(bf16)


def head_block():
    hit = iota((QUAD, QUAD), 0) // HEAD == iota((QUAD, QUAD), 1) // HEAD
    return jnp.where(hit, 1.0, 0.0).astype(bf16)


def exact_three(values):
    group = (iota((1, PAIR), 1) - SHIFT_LANE) // 8
    high = values.astype(bf16).astype(f32)
    rest = values - high
    middle = rest.astype(bf16).astype(f32)
    low = rest - middle
    return jnp.where(group == 0, high, jnp.where(group == 1, middle, low)).astype(bf16)


def rows_to_lanes(rows, groups):
    count = rows.shape[1]
    parts = [jnp.zeros((SHIFT_LANE, count), f32)] + [rows] * groups
    parts.append(jnp.zeros((PAIR - SHIFT_LANE - 8 * groups, count), f32))
    return jnp.concatenate(parts, 0).T


def pair_of(values, head):
    start = head // 2 * PAIR
    return values[:, start : start + PAIR]


def only_head(values, head):
    return jnp.where(iota((1, PAIR), 1) // HEAD == head % 2, pair_of(values, head), bf16(0))


def shift_lanes(shift, features, head, groups=1):
    place = iota((1, PAIR), 1) - SHIFT_LANE
    hit = (place >= 0) & (place < 8 * groups) & (place % 8 == head)
    return jnp.where(hit, -shift, features)


def norm_stats(values):
    centered = values - jnp.mean(values, axis=-1, keepdims=True)
    inverse = lax.rsqrt(jnp.mean(centered * centered, axis=-1, keepdims=True) + LN_EPS)
    return centered * inverse, inverse


def norm_back(grad, normal, inverse, gain):
    scaled = grad * gain
    return inverse * (
        scaled
        - jnp.mean(scaled, axis=-1, keepdims=True)
        - normal * jnp.mean(scaled * normal, axis=-1, keepdims=True)
    )


def near_kernel(
    own_ref, mate_ref, wq_ref, wk_ref, wv_ref, rows_ref, qf_ref, kf_ref, alone_ref,
    q_ref, k_ref, v_ref, mixed_ref, lse_ref, rows_in_ref, vt_ref,
):
    count = own_ref.shape[0]
    own = own_ref[...]

    @pl.when(pl.program_id(0) == 0)
    def _():
        rows_in_ref[:count, :] = own
        rows_in_ref[count:, :] = mate_ref[...]

    bias_q, bias_v = rows_ref[BIAS_Q : BIAS_Q + 1, :], rows_ref[BIAS_V : BIAS_V + 1, :]
    q_ref[...] = (dot(own, wq_ref[...]) + bias_q).astype(bf16) * bf16(1.0 / math.sqrt(HEAD))
    for place, rows in ((0, own), (1, mate_ref[...])):
        here = pl.ds(place * count, count)
        k_ref[here, :] = dot(rows, wk_ref[...]).astype(bf16)
        v_ref[here, :] = (dot(rows, wv_ref[...]) + bias_v).astype(bf16)
    vt_ref[...] = v_ref[...].T
    high, low = split_two(q_ref[...].astype(f32) * k_ref[:count, :].astype(f32))
    shift = dot(high, head_lanes(1)).astype(bf16)
    self_score = dot(head_rows(), high, NT) + dot(head_rows(), low, NT)
    pick = jnp.where(iota((8, PAIR), 1) == iota((8, PAIR), 0) + SHIFT_LANE, 1.0, 0.0).astype(bf16)
    base = dot(pick, shift, NT)
    lse_ref[...] = jnp.zeros_like(lse_ref)

    def one_head(head, exact):
        query = jnp.concatenate(
            [only_head(q_ref[...], head), shift_lanes(shift, qf_ref[...], head)], 1
        )
        keys = jnp.concatenate([pair_of(k_ref, head), kf_ref[...]], 1)
        scores = dot(keys, query, NT)
        start = base[head : head + 1]
        if exact:
            top = jnp.maximum(jnp.max(scores, axis=0, keepdims=True), 0.0)
            scores = scores - top
            start = start + top
        probs = jnp.exp(scores)
        total = jnp.sum(probs, axis=0, keepdims=True)
        lanes = pl.ds(head * HEAD, HEAD)
        mixed = dot(vt_ref[lanes, :], probs.astype(bf16))
        alone = jnp.exp(self_score[head : head + 1] - start) * alone_ref[0:1, :]
        total = total + alone
        mixed = mixed + vt_ref[lanes, :count].astype(f32) * alone
        mixed_ref[lanes, :] = mixed / total
        lse_ref[head : head + 1, :] = start + jnp.log(total)
        return total

    most = functools.reduce(jnp.maximum, [one_head(head, False) for head in range(4)])

    @pl.when(jnp.logical_not(jnp.max(most) < TOO_LARGE))
    def _():
        for head in range(4):
            one_head(head, True)


def far_kernel(blocks, *refs):
    block_refs, refs = refs[:blocks], refs[blocks:]
    wk_ref, wv_ref, rows_ref, qf_ref, kf_ref, q_ref, near_ref, near_lse_ref = refs[:8]
    k_ref, v_ref, mixed_ref, lse_ref, rows_in_ref, vt_ref, total_ref = refs[8:]
    count = q_ref.shape[0]

    @pl.when(pl.program_id(0) == 0)
    def _():
        for place, block_ref in enumerate(block_refs):
            rows_in_ref[pl.ds(place * count, count), :] = block_ref[...]

    bias_v = rows_ref[BIAS_V : BIAS_V + 1, :]
    for place, block_ref in enumerate(block_refs):
        here = pl.ds(place * count, count)
        rows = block_ref[...]
        k_ref[here, :] = dot(rows, wk_ref[...]).astype(bf16)
        v_ref[here, :] = (dot(rows, wv_ref[...]) + bias_v).astype(bf16)
    vt_ref[...] = v_ref[...].T
    near_lse = near_lse_ref[...]
    base = near_lse.astype(bf16).astype(f32)
    shift = rows_to_lanes(base, 1).astype(bf16)
    lse_ref[...] = jnp.zeros_like(lse_ref)

    def one_head(head, exact):
        query = jnp.concatenate(
            [only_head(q_ref[...], head), shift_lanes(shift, qf_ref[...], head)], 1
        )
        keys = jnp.concatenate([pair_of(k_ref, head), kf_ref[...]], 1)
        scores = dot(keys, query, NT)
        start = base[head : head + 1]
        if exact:
            top = jnp.maximum(jnp.max(scores, axis=0, keepdims=True), 0.0)
            scores = scores - top
            start = start + top
        probs = jnp.exp(scores)
        total = jnp.sum(probs, axis=0, keepdims=True)
        lanes = pl.ds(head * HEAD, HEAD)
        mixed = dot(vt_ref[lanes, :], probs.astype(bf16))
        before = jnp.exp(near_lse[head : head + 1] - start)
        total = total + before
        total_ref[lanes, :] = (mixed + near_ref[lanes, :] * before) / total
        lse_ref[head : head + 1, :] = start + jnp.log(total)
        return total

    most = functools.reduce(jnp.maximum, [one_head(head, False) for head in range(4)])

    @pl.when(jnp.logical_not(jnp.max(most) < TOO_LARGE))
    def _():
        for head in range(4):
            one_head(head, True)

    mixed_ref[...] = total_ref[...].T.astype(bf16)


def back_kernel(
    with_self, blocks, q_ref, do_ref, o_ref, lse_ref, k_ref, v_ref, kf_ref, wk_ref, wv_ref, qf_ref,
    *refs,
):
    if with_self:
        part_q_ref, cols_ref = refs[:2]
        refs = refs[2:]
    dq_ref, dk_ref, dv_ref, sum_ref = refs[:4]
    da_refs = refs[4 : 4 + blocks]
    kt_ref, dqt_ref, dkf_ref, dvf_ref, daf_ref = refs[4 + blocks :]
    count = q_ref.shape[0]
    step = pl.program_id(0)
    kt_ref[...] = k_ref[...].T
    query_all, grad_all = q_ref[...], do_ref[...]
    lse_terms = exact_three(rows_to_lanes(lse_ref[...], 3))
    high, low = split_two(grad_all.astype(f32) * o_ref[...].astype(f32))
    delta_terms = exact_three(dot(high, head_lanes(3)) + dot(low, head_lanes(3)))
    for head in range(4):
        query = only_head(query_all, head)
        grad = only_head(grad_all, head)
        keys = jnp.concatenate([pair_of(k_ref, head), kf_ref[...]], 1)
        values = jnp.concatenate([pair_of(v_ref, head), kf_ref[...]], 1)
        query_wide = jnp.concatenate([query, shift_lanes(lse_terms, qf_ref[...], head, 3)], 1)
        grad_wide = jnp.concatenate([grad, shift_lanes(delta_terms, bf16(0), head, 3)], 1)
        probs = jnp.exp(dot(keys, query_wide, NT))
        back = (probs * dot(values, grad_wide, NT)).astype(bf16)
        probs = probs.astype(bf16)
        pair = pl.ds(head // 2 * PAIR, PAIR)
        if head % 2 == 0:
            dvf_ref[:, pair] = dot(probs, grad)
            dkf_ref[:, pair] = dot(back, query)
        else:
            dvf_ref[:, pair] += dot(probs, grad)
            dkf_ref[:, pair] += dot(back, query)
        lanes = pl.ds(head * HEAD, HEAD)
        dqt_ref[lanes, :] = dot(kt_ref[lanes, :], back)
    dq = dqt_ref[...].T
    if with_self:
        block = head_block()
        own_k, own_v = k_ref[:count, :].astype(f32), v_ref[:count, :].astype(f32)
        query_f, grad_f = query_all.astype(f32), grad_all.astype(f32)

        def per_head(values):
            first, second = split_two(values)
            return dot(first, block) + dot(second, block)

        spread = jnp.where(
            (iota((PAIR, QUAD), 0) >= SHIFT_LANE)
            & (iota((PAIR, QUAD), 0) < SHIFT_LANE + 24)
            & (iota((PAIR, QUAD), 0) % 8 == iota((PAIR, QUAD), 1) // HEAD),
            1.0,
            0.0,
        ).astype(bf16)
        prob = jnp.exp(per_head(query_f * own_k) - dot(lse_terms, spread)) * cols_ref[:, ALONE : ALONE + 1]
        back = prob * (per_head(grad_f * own_v) - dot(delta_terms, spread))
        dq = dq + back * own_k
        dkf_ref[:count, :] += back * query_f
        dvf_ref[:count, :] += prob * grad_f
    dq = dq * (1.0 / math.sqrt(HEAD))
    if with_self:
        dq = (dq + part_q_ref[...]).astype(bf16)
        sum_ref[0:1, :] = jnp.sum(dq.astype(f32), axis=0, keepdims=True)
    else:
        sum_ref[0:1, :] = jnp.zeros((1, QUAD), f32)
    dq_ref[...] = dq
    dk, dv = dkf_ref[...].astype(bf16), dvf_ref[...].astype(bf16)
    dk_ref[...] = dk
    dv_ref[...] = dv
    sum_ref[1:2, :] = jnp.sum(dvf_ref[...], axis=0, keepdims=True)
    part = dot(dk, wk_ref[...], NT) + dot(dv, wv_ref[...], NT)

    @pl.when(step == 0)
    def _():
        daf_ref[...] = part

    @pl.when(step > 0)
    def _():
        daf_ref[...] += part

    @pl.when(step == pl.num_programs(0) - 1)
    def _():
        for place, da_ref in enumerate(da_refs):
            da_ref[...] = daf_ref[place * count : (place + 1) * count, :].astype(bf16)


def mix_kernel(
    step_no, last, x_ref, o_ref, wo_ref, rows_ref, up_a_ref, up_b_ref, down_a_ref, down_b_ref,
    cols_ref, hidden_ref, normed_ref, act_ref, slope_ref, new_ref, *refs,
):
    if last:
        (total_ref,) = refs
    else:
        next_ref, total_ref = refs
    step = pl.program_id(0)
    width = x_ref.shape[1]

    def row(place):
        return rows_ref[place : place + 1, :]

    @pl.when(step == 0)
    def _():
        hidden = x_ref[...] + (dot(o_ref[...], wo_ref[...]) + row(BIAS_O))
        hidden_ref[...] = hidden
        normal = norm_stats(hidden)[0]
        normed_ref[:, :width] = (normal * row(GAIN_2) + row(SHIFT_2)).astype(bf16)
        one = jnp.where(iota((x_ref.shape[0], PAIR), 1) == 0, 1.0, 0.0)
        normed_ref[:, width:] = one.astype(bf16)
        total_ref[...] = hidden + row(BIAS_D)

    in_first = step < pl.num_programs(0) // 2
    before = dot(normed_ref[...], jnp.where(in_first, up_a_ref[...], up_b_ref[...]), NT)
    root = math.sqrt(2.0 / math.pi)
    square = before * before
    bent = jnp.tanh(before * (root + root * 0.044715 * square))
    half = 0.5 + 0.5 * bent
    exact = before * half
    act = exact.astype(bf16)
    act_ref[...] = act
    slope_ref[...] = (
        half + exact * (1.0 - half) * (2.0 * root + 6.0 * root * 0.044715 * square)
    ).astype(bf16)
    total_ref[...] += dot(act, jnp.where(in_first, down_a_ref[...], down_b_ref[...]))

    @pl.when(step == pl.num_programs(0) - 1)
    def _():
        live = cols_ref[:, HALTS : HALTS + 1] >= step_no + 1
        new = jnp.where(live, total_ref[...], x_ref[...])
        new_ref[...] = new
        if not last:
            next_ref[...] = (norm_stats(new)[0] * row(GAIN_1) + row(SHIFT_1)).astype(bf16)


def unmix_kernel(
    step_no, grad_ref, cols_ref, slope_ref, up_a_ref, up_b_ref, down_a_ref, down_b_ref,
    hidden_ref, rows_ref, wo_ref, dz_ref, du_ref, dh_ref, dy_ref, do_ref, sum_ref, total_ref,
):
    in_first = pl.program_id(0) < pl.num_programs(0) // 2
    step = pl.program_id(0)
    width = grad_ref.shape[1]

    def live_grad():
        return jnp.where(cols_ref[:, HALTS : HALTS + 1] >= step_no + 1, grad_ref[...], 0.0)

    @pl.when(step == 0)
    def _():
        dz_ref[...] = live_grad().astype(bf16)

    down = jnp.where(in_first, down_a_ref[...], down_b_ref[...])
    du = (slope_ref[...].astype(f32) * dot(dz_ref[...], down, NT)).astype(bf16)
    du_ref[...] = du
    part = dot(du, jnp.where(in_first, up_a_ref[:, :width], up_b_ref[:, :width]))

    @pl.when(step == 0)
    def _():
        total_ref[...] = part

    @pl.when(step > 0)
    def _():
        total_ref[...] += part

    @pl.when(step == pl.num_programs(0) - 1)
    def _():
        normal, inverse = norm_stats(hidden_ref[...])
        back = total_ref[...]
        gain = rows_ref[GAIN_2 : GAIN_2 + 1, :]
        dh = live_grad() + norm_back(back, normal, inverse, gain)
        dh_ref[...] = dh
        dy = dh.astype(bf16)
        dy_ref[...] = dy
        do_ref[...] = dot(dy, wo_ref[...], NT).astype(bf16)
        sum_ref[0:1, :] = jnp.sum(dz_ref[...].astype(f32), axis=0, keepdims=True)
        sum_ref[1:2, :] = jnp.sum(dy.astype(f32), axis=0, keepdims=True)
        sum_ref[2:3, :] = jnp.sum(back * normal, axis=0, keepdims=True)
        sum_ref[3:4, :] = jnp.sum(back, axis=0, keepdims=True)


def half_of(first_ref, second_ref):
    in_first = pl.program_id(0) < pl.num_programs(0) // 2
    return jnp.where(in_first, first_ref[...], second_ref[...])


def join_kernel(
    step_no, received, dq_ref, wq_ref, near_ref, x_ref, rows_ref, grad_ref, cols_ref, dh_ref,
    halt_ref, cot_a_ref, cot_b_ref, *refs,
):
    parts, (new_ref, sum_ref) = refs[:received], refs[received:]
    back = dot(dq_ref[...], wq_ref[...], NT) + near_ref[...].astype(f32)
    for part in parts:
        back = back + part[...].astype(f32)
    values = x_ref[...]
    normal, inverse = norm_stats(values)
    slope = halt_ref[:, step_no : step_no + 1]
    passed = jnp.where(cols_ref[:, HALTS : HALTS + 1] >= step_no + 1, 0.0, grad_ref[...])
    new = (
        passed
        + dh_ref[...]
        + norm_back(back, normal, inverse, rows_ref[GAIN_1 : GAIN_1 + 1, :])
        + slope * rows_ref[HALT_W : HALT_W + 1, :]
    )
    if step_no > 0:
        weight = halt_ref[:, STEPS + step_no - 1 : STEPS + step_no]
        new = new + weight * half_of(cot_a_ref, cot_b_ref).astype(f32)
    new_ref[...] = new
    sums = [back * normal, back, slope * values]

    @pl.when(pl.program_id(0) == 0)
    def _():
        sum_ref[...] = jnp.zeros_like(sum_ref)

    for place, item in enumerate(sums):
        sum_ref[place : place + 1, :] += jnp.sum(item, axis=0, keepdims=True)


def halt_kernel(*refs):
    state_refs = refs[: STEPS + 1]
    rows_ref, cols_ref, cot_a_ref, cot_b_ref, acted_ref, grad_ref, halt_ref, sum_ref = refs[
        STEPS + 1 :
    ]
    states = [ref[...] for ref in state_refs]
    cot = half_of(cot_a_ref, cot_b_ref).astype(f32)
    halts = cols_ref[:, HALTS : HALTS + 1]
    halt_row = rows_ref[HALT_W : HALT_W + 1, :]
    halt_bias = rows_ref[HALT_B : HALT_B + 1, 0:1]
    final_dot = jnp.sum(cot * states[STEPS], axis=-1, keepdims=True)
    remainder = jnp.ones_like(halts)
    acted = jnp.zeros_like(states[0])
    slopes, weights = [], []
    for step in range(STEPS):
        logit = jnp.sum(states[step] * halt_row, axis=-1, keepdims=True) + halt_bias
        prob = (1.0 / (1.0 + jnp.exp(-logit))) / STEPS
        early = halts > step + 1
        weight = jnp.where(early, prob, 0.0)
        weights.append(weight)
        remainder = remainder - weight
        acted = acted + weight * states[step + 1]
        step_dot = jnp.sum(cot * states[step + 1], axis=-1, keepdims=True)
        slope = (step_dot - final_dot - PONDER) * prob * (1.0 - STEPS * prob)
        slopes.append(jnp.where(early, slope, 0.0))
    acted_ref[...] = (acted + remainder * states[STEPS]).astype(bf16)
    grad_ref[...] = (remainder + weights[STEPS - 1]) * cot
    lane = iota((halts.shape[0], PAIR), 1)
    table = jnp.zeros((halts.shape[0], PAIR), f32)
    for place, column in enumerate(slopes + weights):
        table = jnp.where(lane == place, column, table)
    halt_ref[...] = table

    @pl.when(pl.program_id(0) == 0)
    def _():
        sum_ref[...] = jnp.zeros_like(sum_ref)

    sum_ref[0:1, :] += jnp.sum(jnp.where(lane < STEPS, table, 0.0), axis=0, keepdims=True)


def outset_kernel(
    tokens_ref, mask_ref, halts_ref, cot_ref, lengths_ref, own_ref, other_ref, cot_own_ref,
    cot_other_ref,
):
    seq_here, width = tokens_ref.shape[1:]
    parity = lax.axis_index("sq") % 2
    lane = iota((1, width), 1)

    def row_of(ref, row):
        return jnp.where(row == 0, ref[0:1, :], ref[1:2, :]).astype(f32)

    for row, out_ref, cot_out_ref in (
        (parity, own_ref, cot_own_ref), (1 - parity, other_ref, cot_other_ref)
    ):
        cot_out_ref[...] = cot_ref[row]
        out_ref[:seq_here, :] = tokens_ref[row]
        mask = row_of(mask_ref, row)
        parts = [mask[:, at : at + width] for at in range(0, mask.shape[1], width)]
        halts = row_of(halts_ref, row)
        if seq_here < width:
            halts = jnp.concatenate([halts, jnp.zeros((1, width - seq_here), f32)], 1)
        parts.append(halts)
        for part in (lambda value: value // 16, lambda value: value % 16):
            entry = jnp.zeros((1, width), jnp.int32)
            for doc in range(lengths_ref.shape[1]):
                entry = jnp.where(lane == doc, part(lengths_ref[row, doc]), entry)
            parts.append(entry.astype(f32))
        parts.append(jnp.zeros((out_ref.shape[0] - seq_here - len(parts), width), f32))
        out_ref[seq_here:, :] = jnp.concatenate(parts, 0).astype(bf16)


def begin_kernel(
    middle, docs, row_len, a_ref, b_ref, rows_ref, x_ref, normed_ref, qf_ref, near_ref, far_ref,
    cols_ref, alone_ref, row_ref,
):
    count, width = x_ref.shape
    seq_here = count // 2
    d_at, s_at = lax.axis_index("dp"), lax.axis_index("sq")
    top = 2 * middle
    parity, core, chip = s_at % 2, d_at % 2, s_at % top // 2
    for place, ref in enumerate((a_ref, b_ref)):
        here = pl.ds(place * seq_here, seq_here)
        values = ref[:seq_here, :].astype(f32)
        x_ref[here, :] = values
        normed_ref[here, :] = (
            norm_stats(values)[0] * rows_ref[GAIN_1 : GAIN_1 + 1, :]
            + rows_ref[SHIFT_1 : SHIFT_1 + 1, :]
        ).astype(bf16)
    info = a_ref[seq_here:, :].astype(f32)
    mask_rows = row_len // width
    for at in range(mask_rows):
        row_ref[:, at * width : (at + 1) * width] = jnp.broadcast_to(
            info[at : at + 1, :], (row_ref.shape[0], width)
        )
    lengths = info[mask_rows + 1 : mask_rows + 2, :] * 16.0 + info[mask_rows + 2 : mask_rows + 3, :]
    lane = iota((1, width), 1)
    ends = [
        jnp.sum(jnp.where(lane <= doc, lengths, 0.0), axis=1, keepdims=True)
        for doc in range(docs)
    ]

    def at_block(core_at, chip_at):
        start = (core_at * middle + chip_at) * count
        block = row_ref[0:1, pl.ds(pl.multiple_of(start, count), count)]
        turned = jnp.concatenate([block[:, seq_here:], block[:, :seq_here]], 1)
        offset = iota((1, count), 1) + parity * seq_here
        place = (start + jnp.where(offset >= count, offset - count, offset)).astype(f32)
        doc_at = jnp.zeros((1, count), jnp.int32)
        for end in ends:
            doc_at = doc_at + jnp.where(place >= end, 1, 0)
        return doc_at, jnp.where(parity == 0, block, turned)

    kind = iota((PAIR, 1), 0)

    def key_features(core_at, chip_at):
        doc_at, open_at = at_block(core_at, chip_at)
        closed = (kind == doc_at) | ((kind == 8) & (open_at == 0))
        ones = jnp.where(kind >= SHIFT_LANE, 1.0, 0.0)
        return jnp.where(closed, MASKED, jnp.broadcast_to(ones, closed.shape)).T.astype(bf16)

    doc_at, open_at = at_block(core, chip)
    wanted = ((kind < docs) & (kind != doc_at)) | (kind == 8)
    qf_ref[...] = jnp.where(wanted, 1.0, 0.0).T.astype(bf16)
    for place, core_at in enumerate((core, 1 - core)):
        near_ref[pl.ds(place * count, count), :] = key_features(core_at, chip)
    place = 0
    for offset in range(1, middle):
        for core_at in (core, 1 - core):
            far_ref[pl.ds(place * count, count), :] = key_features(core_at, chip ^ offset)
            place += 1
    halts = jnp.concatenate(
        [
            ref[seq_here:, :].astype(f32)[mask_rows : mask_rows + 1, :seq_here]
            for ref in (a_ref, b_ref)
        ],
        1,
    )
    alone = jnp.where(open_at == 0, 1.0, 0.0)
    alone_ref[...] = jnp.broadcast_to(alone, alone_ref.shape)
    table = jnp.where(kind == HALTS, halts, jnp.where(kind == ALONE, alone, 0.0))
    cols_ref[...] = table.T


def small_kernel(unmix_refs, near_refs, far_refs, join_refs, halt_ref, out_ref):
    def row(refs, place):
        return sum(ref[place : place + 1, :] for ref in refs)

    out_ref[...] = jnp.zeros_like(out_ref)
    entries = (
        row(near_refs, 0), row(near_refs, 1) + row(far_refs, 1), row(unmix_refs, 1),
        row(join_refs, 0), row(join_refs, 1), row(unmix_refs, 2), row(unmix_refs, 3),
        row(unmix_refs, 0), row(join_refs, 2),
    )
    for place, entry in enumerate(entries):
        out_ref[place : place + 1, :] = entry
    bias = jnp.sum(halt_ref[0:1, :], axis=1, keepdims=True)
    out_ref[len(entries) : len(entries) + 1, :] = jnp.broadcast_to(bias, (1, out_ref.shape[1]))


def hidden_grads_kernel(steps, *refs):
    act_refs, dz_refs, du_refs, normed_refs = (refs[i * steps : (i + 1) * steps] for i in range(4))
    out_ref = refs[4 * steps]
    wide = normed_refs[0].shape[1]
    out_ref[:, :wide] = sum(
        dot(du[...], normed[...], TN) for du, normed in zip(du_refs, normed_refs)
    ).astype(bf16)
    out_ref[:, wide:] = sum(
        dot(act[...], dz[...], TN) for act, dz in zip(act_refs, dz_refs)
    ).astype(bf16)


def pack_kernel(bits, *refs):
    sources, results = refs[: len(refs) // 3 * 2], refs[len(refs) // 3 * 2 :]
    blocks = 2 ** len(bits)
    rows = sources[0].shape[0] // blocks
    width = sources[0].shape[1]
    own = own_block(bits)
    for block in range(blocks):
        start = pl.multiple_of((own ^ block) * rows, rows)
        for place, source in enumerate(sources):
            lanes = pl.ds(place % 2 * width, width)
            results[place // 2][pl.ds(block * rows, rows), lanes] = source[
                pl.ds(start, rows), :
            ].astype(bf16)


def unpack_kernel(bits, *refs):
    sources, results = refs[: len(refs) // 3], refs[len(refs) // 3 :]
    blocks = 2 ** len(bits)
    rows = sources[0].shape[0] // blocks
    width = sources[0].shape[1] // 2
    own = own_block(bits)
    for block in range(blocks):
        start = pl.multiple_of((own ^ block) * rows, rows)
        for place, result in enumerate(results):
            lanes = pl.ds(place % 2 * width, width)
            result[pl.ds(block * rows, rows), :] = sources[place // 2][
                pl.ds(start, rows), lanes
            ].astype(f32)


def hidden_out_kernel(dp_bits, source_ref, up_ref, bias_ref, down_ref, wide_ref, order_ref):
    width = down_ref.shape[1]
    blocks = 2 ** len(dp_bits)
    rows = source_ref.shape[0] // blocks
    own = own_block([(bit, 0) for bit in dp_bits])
    wide_ref[...] = source_ref[...].astype(f32)
    for block in range(blocks):
        place = sum(
            (1 << at) for at, bit in enumerate(dp_bits[::-1]) if block & bit
        )
        start = pl.multiple_of((own ^ place) * rows, rows)
        order_ref[pl.ds(block * rows, rows), :] = wide_ref[pl.ds(start, rows), :]
    up_ref[...] = order_ref[:, :width].T
    bias_ref[...] = jnp.broadcast_to(order_ref[:, width : width + PAIR].T[0:1, :], bias_ref.shape)
    down_ref[...] = order_ref[:, width + PAIR :]


def own_block(bits):
    own = jnp.int32(0)
    for d_bit, s_bit in bits:
        at = lax.axis_index("dp") & d_bit if d_bit else lax.axis_index("sq") & s_bit
        own = own * 2 + jnp.where(at != 0, 1, 0)
    return own


def whole(shape):
    return pl.BlockSpec(shape, lambda i: (0,) * len(shape))


def lanes_of(rows, width=QUAD):
    return pl.BlockSpec((rows, width), lambda i: (0, i))


def rows_of(rows, width):
    return pl.BlockSpec((rows, width), lambda i: (i, 0))


def shaped(shape, dtype):
    return jax.ShapeDtypeStruct(shape, dtype)


def in_hbm(value):
    return pltpu.with_memory_space_constraint(value, pltpu.HBM)


def params(flops, moved, exps=0):
    return dict(
        compiler_params=pltpu.CompilerParams(vmem_limit_bytes=VMEM_LIMIT),
        cost_estimate=pl.CostEstimate(
            flops=int(flops), bytes_accessed=int(moved), transcendentals=int(exps)
        ),
    )


def attend_near(own, mate, wq, wk, wv, rows, qf, kf, alone):
    count, width = own.shape
    quads = width // QUAD
    keys = 2 * count
    return pl.pallas_call(
        near_kernel,
        grid=(quads,),
        in_specs=[
            whole((count, width)), whole((count, width)),
            lanes_of(width), lanes_of(width), lanes_of(width), lanes_of(rows.shape[0]),
            whole((count, PAIR)), whole((keys, PAIR)), whole((8, count)),
        ],
        out_specs=[
            lanes_of(count), lanes_of(keys), lanes_of(keys), rows_of(QUAD, count),
            rows_of(8, count), whole((keys, width)),
        ],
        out_shape=[
            shaped((count, width), bf16), shaped((keys, width), bf16), shaped((keys, width), bf16),
            shaped((width, count), f32), shaped((8 * quads, count), f32),
            shaped((keys, width), bf16),
        ],
        scratch_shapes=[pltpu.VMEM((QUAD, keys), bf16)],
        name="attend_near",
        **params(8 * count * keys * width * 2, 10 * count * width * 2, count * keys * 8),
    )(own, mate, wq, wk, wv, rows, qf, kf, alone)


def attend_far(blocks, wk, wv, rows, qf, kf, queries, near_mixed, near_lse):
    count, width = queries.shape
    quads = width // QUAD
    keys = len(blocks) * count
    return pl.pallas_call(
        functools.partial(far_kernel, len(blocks)),
        grid=(quads,),
        in_specs=[whole((count, width))] * len(blocks)
        + [
            lanes_of(width), lanes_of(width), lanes_of(rows.shape[0]),
            whole((count, PAIR)), whole((keys, PAIR)), lanes_of(count), rows_of(QUAD, count),
            rows_of(8, count),
        ],
        out_specs=[
            lanes_of(keys), lanes_of(keys), lanes_of(count), rows_of(8, count), whole((keys, width)),
        ],
        out_shape=[
            shaped((keys, width), bf16), shaped((keys, width), bf16), shaped((count, width), bf16),
            shaped((8 * quads, count), f32), shaped((keys, width), bf16),
        ],
        scratch_shapes=[pltpu.VMEM((QUAD, keys), bf16), pltpu.VMEM((QUAD, count), f32)],
        name="attend_far",
        **params(8 * count * keys * width * 2, 10 * count * width * 2, count * keys * 8),
    )(*blocks, wk, wv, rows, qf, kf, queries, near_mixed, near_lse)


def attend_back(queries, grad_mixed, mixed, lse, keys_in, values_in, kf, wk, wv, qf, partial, cols):
    count, width = queries.shape
    quads = width // QUAD
    keys = keys_in.shape[0]
    blocks = keys // count
    with_self = cols is not None
    extra = [partial, cols] if with_self else []
    extra_specs = [lanes_of(count), whole((count, PAIR))] if with_self else []
    return pl.pallas_call(
        functools.partial(back_kernel, with_self, blocks),
        grid=(quads,),
        in_specs=[
            lanes_of(count), lanes_of(count), lanes_of(count), rows_of(8, count), lanes_of(keys),
            lanes_of(keys), whole((keys, PAIR)), lanes_of(width), lanes_of(width),
            whole((count, PAIR)),
        ]
        + extra_specs,
        out_specs=[lanes_of(count), lanes_of(keys), lanes_of(keys), lanes_of(8)]
        + [whole((count, width))] * blocks,
        out_shape=[
            shaped((count, width), bf16 if with_self else f32), shaped((keys, width), bf16),
            shaped((keys, width), bf16), shaped((8, width), f32),
        ]
        + [shaped((count, width), bf16)] * blocks,
        scratch_shapes=[
            pltpu.VMEM((QUAD, keys), bf16), pltpu.VMEM((QUAD, count), f32),
            pltpu.VMEM((keys, QUAD), f32), pltpu.VMEM((keys, QUAD), f32),
            pltpu.VMEM((keys, width), f32),
        ],
        name="back_near" if with_self else "back_far",
        **params(20 * count * keys * width * 2, 20 * count * width * 2, count * keys * 8),
    )(queries, grad_mixed, mixed, lse, keys_in, values_in, kf, wk, wv, qf, *extra)


def halves_of(rows, width, steps):
    half = steps // 2
    return [
        pl.BlockSpec((rows, width), lambda i: (jnp.minimum(i, half - 1), 0)),
        pl.BlockSpec((rows, width), lambda i: (jnp.maximum(i - half, 0), 0)),
    ]


def mix(step_no, x, mixed, wo, rows, ups, downs, cols, last):
    count, width = x.shape
    hidden = 2 * ups[0].shape[0]
    chunk = min(1024, hidden // 2)
    steps = hidden // chunk
    square = whole((count, width))
    wide = width + PAIR
    out_specs = [
        square, whole((count, wide)), lanes_of(count, chunk), lanes_of(count, chunk), square,
    ]
    out_shape = [
        shaped((count, width), f32), shaped((count, wide), bf16), shaped((count, hidden), bf16),
        shaped((count, hidden), bf16), shaped((count, width), f32),
    ]
    if not last:
        out_specs.append(square)
        out_shape.append(shaped((count, width), bf16))
    return pl.pallas_call(
        functools.partial(mix_kernel, step_no, last),
        grid=(hidden // chunk,),
        in_specs=[
            square, square, whole((width, width)), whole(rows.shape),
            *halves_of(chunk, wide, steps), *halves_of(chunk, width, steps),
            whole((count, PAIR)),
        ],
        out_specs=out_specs,
        out_shape=out_shape,
        scratch_shapes=[pltpu.VMEM((count, width), f32)],
        name="mix",
        **params(4 * count * width * hidden, 16 * count * width + 8 * width * hidden),
    )(x, mixed, wo, rows, *ups, *downs, cols)


def unmix(step_no, grad, cols, slope, ups, downs, hidden_state, rows, wo):
    count, width = grad.shape
    hidden = 2 * ups[0].shape[0]
    chunk = min(1024, hidden // 2)
    steps = hidden // chunk
    square = whole((count, width))
    return pl.pallas_call(
        functools.partial(unmix_kernel, step_no),
        grid=(hidden // chunk,),
        in_specs=[
            square, whole((count, PAIR)), lanes_of(count, chunk),
            *halves_of(chunk, width + PAIR, steps), *halves_of(chunk, width, steps), square,
            whole(rows.shape), whole((width, width)),
        ],
        out_specs=[
            square, lanes_of(count, chunk), square, square, square, whole((8, width)),
        ],
        out_shape=[
            shaped((count, width), bf16), shaped((count, hidden), bf16), shaped((count, width), f32),
            shaped((count, width), bf16), shaped((count, width), bf16), shaped((8, width), f32),
        ],
        scratch_shapes=[pltpu.VMEM((count, width), f32)],
        name="unmix",
        **params(4 * count * width * hidden, 16 * count * width + 8 * width * hidden),
    )(grad, cols, slope, *ups, *downs, hidden_state, rows, wo)


def join(step_no, dq, wq, near, x, rows, grad, cols, dh, halt_table, cot, parts):
    count, width = x.shape
    piece = min(128, count // 2)
    part, table = rows_of(piece, width), rows_of(piece, PAIR)
    return pl.pallas_call(
        functools.partial(join_kernel, step_no, len(parts)),
        grid=(count // piece,),
        in_specs=[
            part, whole((width, width)), part, part, whole(rows.shape), part, table, part, table,
            *halves_of(piece, width, count // piece),
        ]
        + [part] * len(parts),
        out_specs=[part, whole((8, width))],
        out_shape=[shaped((count, width), f32), shaped((8, width), f32)],
        name="join",
        **params(2 * count * width * width, 24 * count * width),
    )(dq, wq, near, x, rows, grad, cols, dh, halt_table, *cot, *parts)


def halting(states, rows, cols, cot):
    count, width = states[0].shape
    piece = min(128, count // 2)
    part, table = rows_of(piece, width), rows_of(piece, PAIR)
    return pl.pallas_call(
        halt_kernel,
        grid=(count // piece,),
        in_specs=[part] * len(states) + [whole(rows.shape), table, *halves_of(piece, width, count // piece)],
        out_specs=[part, part, table, whole((8, PAIR))],
        out_shape=[
            shaped((count, width), bf16), shaped((count, width), f32), shaped((count, PAIR), f32),
            shaped((8, PAIR), f32),
        ],
        name="halting",
        **params(20 * count * width, 24 * count * width),
    )(*states, rows, cols, *cot)


def outset(tokens, mask, halts, cot, lengths):
    seq_here, width = tokens.shape[1:]
    here = pl.BlockSpec(memory_space=pltpu.VMEM)
    extra = -(-(mask.shape[1] // width + 3) // 16) * 16
    block = shaped((seq_here + extra, width), bf16)
    return pl.pallas_call(
        outset_kernel,
        in_specs=[here] * 4 + [pl.BlockSpec(memory_space=pltpu.SMEM)],
        out_specs=[here] * 4,
        out_shape=[block] * 2 + [shaped((seq_here, width), bf16)] * 2,
        name="outset",
        **params(0, 8 * seq_here * width),
    )(*map(in_hbm, (tokens, mask, halts, cot)), lengths)


def begin(middle, docs, row_len, blocks, rows, seq_here):
    width = blocks[0].shape[1]
    count = 2 * seq_here
    far = max(2 * (middle - 1), 1) * count
    here = pl.BlockSpec(memory_space=pltpu.VMEM)
    return pl.pallas_call(
        functools.partial(begin_kernel, middle, docs, row_len),
        in_specs=[here] * 3,
        out_specs=[here] * 7,
        out_shape=[
            shaped((count, width), f32), shaped((count, width), bf16),
            shaped((count, PAIR), bf16), shaped((2 * count, PAIR), bf16), shaped((far, PAIR), bf16),
            shaped((count, PAIR), f32), shaped((8, count), f32),
        ],
        scratch_shapes=[pltpu.VMEM((8, row_len), f32)],
        name="begin",
        **params(10 * count * width, 16 * count * width),
    )(*blocks, rows)


def small_sums(unmix_sums, near_sums, far_sums, join_sums, halt_sums):
    steps, width = len(unmix_sums), unmix_sums[0].shape[1]
    here = pl.BlockSpec(memory_space=pltpu.VMEM)

    def body(*refs):
        groups = [refs[at * steps : (at + 1) * steps] for at in range(4)]
        small_kernel(*groups, *refs[4 * steps :])

    return pl.pallas_call(
        body,
        in_specs=[here] * (4 * steps + 1),
        out_specs=here,
        out_shape=shaped((16, width), f32),
        name="small_sums",
        **params(0, 64 * width),
    )(*unmix_sums, *near_sums, *far_sums, *join_sums, halt_sums)


def hidden_grads(acts, dzs, dus, normeds):
    count, hidden = acts[0].shape
    width, wide = dzs[0].shape[1], normeds[0].shape[1]
    chunk = min(256, hidden)
    tall = lanes_of(count, chunk)
    steps = len(acts)
    return pl.pallas_call(
        functools.partial(hidden_grads_kernel, steps),
        grid=(hidden // chunk,),
        in_specs=[tall] * steps
        + [whole((count, width))] * steps
        + [tall] * steps
        + [whole((count, wide))] * steps,
        out_specs=rows_of(chunk, wide + width),
        out_shape=shaped((hidden, wide + width), bf16),
        name="hidden_grads",
        **params(4 * steps * count * width * hidden, 4 * steps * count * hidden),
    )(*map(in_hbm, acts), *dzs, *map(in_hbm, dus), *normeds)


def pack(bits, sources):
    rows, width = sources[0].shape
    here = pl.BlockSpec(memory_space=pltpu.VMEM)
    return pl.pallas_call(
        functools.partial(pack_kernel, bits),
        in_specs=[here] * len(sources),
        out_specs=[here] * (len(sources) // 2),
        out_shape=[shaped((rows, 2 * width), bf16)] * (len(sources) // 2),
        name="pack",
        **params(0, 6 * rows * width * len(sources)),
    )(*sources)


def unpack(bits, sources):
    rows, width = sources[0].shape
    here = pl.BlockSpec(memory_space=pltpu.VMEM)
    return pl.pallas_call(
        functools.partial(unpack_kernel, bits),
        in_specs=[here] * len(sources),
        out_specs=[here] * (2 * len(sources)),
        out_shape=[shaped((rows, width // 2), f32)] * (2 * len(sources)),
        name="unpack",
        **params(0, 6 * rows * width * len(sources)),
    )(*sources)


def hidden_out(dp_bits, source, width):
    rows = source.shape[0]
    here = pl.BlockSpec(memory_space=pltpu.VMEM)
    return pl.pallas_call(
        functools.partial(hidden_out_kernel, dp_bits),
        in_specs=[here],
        out_specs=[here] * 3,
        out_shape=[shaped((width, rows), f32), shaped((8, rows), f32), shaped((rows, width), f32)],
        scratch_shapes=[pltpu.VMEM(source.shape, f32), pltpu.VMEM(source.shape, f32)],
        name="hidden_out",
        **params(0, 6 * rows * source.shape[1]),
    )(source)


def make_per_device(dp_size, sq_size):
    middle = sq_size // 4
    top = sq_size // 2

    def permute(value, move):
        pairs = []
        for d in range(dp_size):
            for s in range(sq_size):
                to_d, to_s = move(d, s)
                pairs.append((d * sq_size + s, to_d * sq_size + to_s))
        return lax.ppermute(value, AXES, pairs)

    def swap(value, d_bits, s_bits):
        return permute(value, lambda d, s: (d ^ d_bits, s ^ s_bits))

    def regroup(flip):
        def move(d, s):
            upper, core = s // top, d % 2
            return d - core + upper, (core * top + s % top) ^ flip

        return move

    def bits_of(size):
        return [1 << place for place in range(size.bit_length() - 1)]

    dp_bits, sq_bits = bits_of(dp_size), bits_of(sq_size)
    bit_names = [(bit, 0) for bit in dp_bits] + [(0, bit) for bit in sq_bits[::-1]]

    def with_bits(value, names=bit_names):
        return value.reshape((2,) * len(names) + (-1,) + value.shape[len(value.shape) - 1 :])

    def offsets_of(group):
        result = []
        for code in range(1, 2 ** len(group)):
            digits = [code >> (len(group) - 1 - at) & 1 for at in range(len(group))]
            move = [0, 0]
            for digit, (d_bit, s_bit) in zip(digits, group):
                move[0] |= d_bit * digit
                move[1] |= s_bit * digit
            result.append((tuple(move), digits))
        return result

    class Gather:
        def __init__(self, piece, order, axes=()):
            self.piece, self.order, self.axes = piece, list(order), list(axes)

        def start(self):
            return [swap(self.piece, *move) for move, _ in offsets_of(self.order[0])]

        def finish(self, arrived):
            group = self.order.pop(0)
            first = bit_names.index(group[0])
            place = sum(bit_names.index(axis[0]) < first for axis in self.axes)
            self.axes.insert(place, group)
            self.piece = jnp.stack([self.piece] + list(arrived), place)

    class Scatter:
        def __init__(self, total, order, names=bit_names):
            self.piece, self.order, self.names = with_bits(total, names), list(order), list(names)

        def start(self):
            group = self.order[0]
            sent = []
            for move, digits in [(None, [0] * len(group))] + offsets_of(group):
                part = self.piece
                taken = sorted(zip(group, digits), key=lambda item: -self.names.index(item[0]))
                for name, digit in taken:
                    part = lax.index_in_dim(part, digit, self.names.index(name), False)
                if move is None:
                    self.kept = part
                else:
                    sent.append(swap(part, *move))
            return sent

        def finish(self, arrived):
            for name in self.order.pop(0):
                self.names.remove(name)
            self.piece = self.kept
            for item in arrived:
                self.piece = self.piece + item

    class Small:
        def __init__(self, total, order):
            self.piece, self.order = total, list(order)

        def start(self):
            return [swap(self.piece, *move) for move, _ in offsets_of(self.order[0])]

        def finish(self, arrived):
            self.order.pop(0)
            for item in arrived:
                self.piece = self.piece + item

    def together(chains, others=()):
        chains = [chain for chain in chains if chain.order]
        sent = [chain.start() for chain in chains]
        flat = [item for items in sent for item in items] + list(others)
        if flat:
            flat = list(lax.optimization_barrier(tuple(flat)))
        for chain, items in zip(chains, sent):
            chain.finish([flat.pop(0) for _ in items])
        return flat

    def own_part(shard):
        rows = shard.shape[0] // dp_size
        return lax.dynamic_slice_in_dim(shard, lax.axis_index("dp") * rows, rows, 0)

    def turn(total):
        shape = total.shape
        total = with_bits(total)
        for axis, (d_bit, s_bit) in enumerate(bit_names):
            own = ((lax.axis_index("dp") & d_bit) | (lax.axis_index("sq") & s_bit)) != 0
            total = jnp.where(own, jnp.flip(total, axis), total)
        return total.reshape(shape)

    def after(value, *others):
        return lax.optimization_barrier((value,) + others)[0]

    def per_device(
        tokens, lengths, key_mask, halt_steps, query_weight, query_bias, key_weight, value_weight,
        value_bias, out_weight, out_bias, first_gain, first_shift, second_gain, second_shift,
        up_weight, up_bias, down_weight, down_bias, halt_weight, halt_bias, cotangent,
    ):
        seq_here, width = tokens.shape[1:]
        parity = lax.axis_index("sq") % 2

        def send_back(value):
            return [
                permute(value[:seq_here], regroup(0)), permute(value[seq_here:], regroup(1))
            ]

        def unspread(own, other):
            first = jnp.where(parity == 0, own, other)
            second = jnp.where(parity == 0, other, own)
            return jnp.stack([first, second], 0)

        *leaving, cot_own, cot_other = outset(tokens, key_mask, halt_steps, cotangent, lengths)
        tokens_here = [permute(block, regroup(flip)) for flip, block in enumerate(leaving)]
        core_bit, side = (1, 0), (0, 1)
        z_bits = tuple((0, bit) for bit in sq_bits[::-1][:-1])
        y_order = [((bit, 0),) for bit in dp_bits[1:]]
        z_order = [(bit,) for bit in z_bits]
        up_wide = jnp.concatenate(
            [up_weight.T, jnp.pad(up_bias[:, None], ((0, 0), (0, PAIR - 1)))], 1
        )
        gathers = [
            Gather(own_part(up_wide), z_order + [(side,)] + y_order),
            Gather(own_part(down_weight), z_order + y_order + [(side,)]),
        ]

        def gather_step(*others):
            sent = [gather.start() for gather in gathers]
            for gather, items in zip(gathers, sent):
                gather.finish([after(item, *others) for item in items])

        def gathered():
            return [gather.piece for gather in gathers]

        rows = jnp.stack(
            [
                item.astype(f32)
                for item in (
                    query_bias, value_bias, out_bias, down_bias, first_gain, first_shift,
                    second_gain, second_shift, halt_weight, jnp.broadcast_to(halt_bias, (width,)),
                )
            ]
            + [jnp.zeros((width,), f32)] * 6
        )
        gather_step()
        tokens_here = [after(item, *gathered()) for item in tokens_here]
        x, normed, query_feats, near_feats, far_feats, cols, alone_row = begin(
            middle, lengths.shape[1], key_mask.shape[1], tokens_here, rows, seq_here
        )

        states, kept = [x], []
        for step in range(STEPS):
            x = states[-1]
            arrived = [swap(normed, 0, offset * 2) for offset in range(1, middle)]
            mate = swap(normed, 1, 0)
            if step == 0:
                gather_step(normed)
                mate = after(mate, *gathered())
            queries, keys_near, values_near, near_mixed, near_lse, near_in = attend_near(
                normed, mate, query_weight, key_weight, value_weight, rows, query_feats,
                near_feats, alone_row,
            )
            if step == 0:
                gather_step(near_lse)
                arrived = [after(block, *gathered()) for block in arrived]
            far = []
            for block in arrived:
                block = after(block, near_lse)
                far += [block, swap(block, 1, 0)]
            if step == 1:
                cot = [
                    permute(after(block, far[0]), regroup(flip))
                    for flip, block in enumerate((cot_own, cot_other))
                ]
            keys_far, values_far, mixed, lse, far_in = attend_far(
                far, key_weight, value_weight, rows, query_feats, far_feats, queries, near_mixed,
                near_lse,
            )
            if step == 0:
                gather_step(lse)
                while gathers[0].order:
                    gather_step()
                halves = []
                for gather, weight in zip(gathers, (up_wide, down_weight)):
                    half = gather.piece.reshape(-1, weight.shape[1])
                    halves.append((half, swap(half, *core_bit)))
                up_rows, down_rows = halves
            out = mix(
                step, x, mixed, out_weight, rows, up_rows, down_rows, cols, step == STEPS - 1
            )
            hidden, normed_two, act, slope, new = out[:5]
            kept.append(
                (near_in, far_in, queries, keys_near, values_near, keys_far, values_far, mixed,
                 lse, hidden, normed_two, act, slope)
            )
            states.append(new)
            if step < STEPS - 1:
                normed = out[5]
            if step == 1:
                normed, *cot = lax.optimization_barrier((normed, *cot))

        acted, grad, halt_table, halt_sums = halting(states, rows, cols, cot)
        acted_sent = send_back(acted)
        total = {}

        def add(name, value):
            total[name] = total[name] + value if name in total else value

        small_parts = ([], [], [], [])
        hidden_parts = []
        for step in reversed(range(STEPS)):
            (near_in, far_in, queries, keys_near, values_near, keys_far, values_far, mixed, lse,
             hidden, normed_two, act, slope) = kept[step]
            dz, du, dh, dy, grad_mixed, sums = unmix(
                step, grad, cols, slope, up_rows, down_rows, hidden, rows, out_weight
            )
            hidden_parts.append((act, dz, du, normed_two))
            small_parts[0].append(sums)
            add("out", dot(mixed, dy, TN))
            if step == 0:
                hidden_part = hidden_grads(*zip(*hidden_parts))
                grad_mixed = after(grad_mixed, hidden_part)
                hidden_sum = Scatter(hidden_part, [(core_bit,)])
                together([hidden_sum])
                names, wide = hidden_sum.names, normed_two.shape[1]
                hidden_sums = [
                    Scatter(hidden_sum.piece[..., :wide], y_order + [(side,)], names),
                    Scatter(hidden_sum.piece[..., wide:], [(side,)] + y_order, names),
                ]
            part_q, dk_far, dv_far, far_sums, *da_far = attend_back(
                queries, grad_mixed, mixed, lse, keys_far, values_far, far_feats, key_weight,
                value_weight, query_feats, None, None,
            )
            if step == STEPS - 1:
                *da_far, acted_own, acted_other = lax.optimization_barrier(
                    (*da_far, *acted_sent)
                )
                acted_sent = [acted_own, acted_other]
            crossed = [swap(part, 1, 0) for part in da_far[1::2]]
            add("key", dot(far_in, dk_far, TN))
            add("value", dot(far_in, dv_far, TN))
            total["key"], total["value"], *crossed = lax.optimization_barrier(
                (total["key"], total["value"], *crossed)
            )
            summed = [part + other for part, other in zip(da_far[0::2], crossed)]
            sent = [swap(part, 0, (at + 1) * 2) for at, part in enumerate(summed)]
            held = [part_q, total["out"], *summed]
            if step == 0:
                held += [item.piece for item in hidden_sums]
            part_q, total["out"], *pieces = lax.optimization_barrier(tuple(held))
            pieces = pieces[len(summed) :]
            if step == 0:
                for item, piece in zip(hidden_sums, pieces):
                    item.piece = piece
                hidden_sent = [item.start()[0] for item in hidden_sums]
            dq, dk_near, dv_near, near_sums, da_own, da_mate = attend_back(
                queries, grad_mixed, mixed, lse, keys_near, values_near, near_feats, key_weight,
                value_weight, query_feats, part_q, cols,
            )
            small_parts[1].append(near_sums)
            small_parts[2].append(far_sums)
            if step == 0:
                da_mate, dq, dk_near, dv_near, *hidden_sent = lax.optimization_barrier(
                    (da_mate, dq, dk_near, dv_near, *hidden_sent)
                )
            da_mate, *sent = lax.optimization_barrier((da_mate, *sent))
            arrived = swap(da_mate, 1, 0)
            add("key", dot(near_in, dk_near, TN))
            add("value", dot(near_in, dv_near, TN))
            add("query", dot(near_in[: 2 * seq_here], dq, TN))
            if step > 0:
                dq, total["query"], total["key"], total["value"] = lax.optimization_barrier(
                    (dq, total["query"], total["key"], total["value"])
                )
            grad, join_sums = join(
                step, dq, query_weight, da_own, states[step], rows, grad, cols, dh, halt_table,
                cot, sent + [arrived],
            )
            small_parts[3].append(join_sums)

        squares = [total["query"], total["key"], total["value"], total["out"]]
        by_kernel = width % (16 * 2 ** len(bit_names)) == 0
        if by_kernel:
            squares = pack(bit_names, squares)
        else:
            squares = [
                turn(jnp.concatenate(squares[place : place + 2], 1).astype(bf16))
                for place in (0, 2)
            ]
        names = (
            "query_bias", "value_bias", "out_bias", "gain_one", "shift_one", "gain_two",
            "shift_two", "down_bias", "halt",
        )
        small = small_sums(*small_parts, halt_sums).reshape(-1)
        for item, arrived in zip(hidden_sums, hidden_sent):
            item.finish([arrived])
        sums = [
            Scatter(squares[0], [(core_bit,)] + y_order + [(side,)]),
            Scatter(squares[1], [(core_bit,), (side,)] + y_order),
        ]
        small = Small(small, [(name,) for name in [item[0] for item in [(core_bit,)] + y_order] + [side]] + z_order[::-1])
        (grad,) = together(sums + hidden_sums, [grad])
        grad_sent = send_back(grad.astype(bf16))
        while hidden_sums[0].order:
            together(hidden_sums)
        hidden_all = Scatter(
            jnp.concatenate([item.piece for item in hidden_sums], -1), z_order[::-1], z_bits
        )
        grad_sent = together(sums + [hidden_all, small], grad_sent)
        grad_tokens = unspread(*grad_sent).astype(f32)
        while sums[0].order:
            together(sums + [hidden_all, small])
        while hidden_all.order:
            together([hidden_all, small])
        hidden_all = Gather(hidden_all.piece, y_order[::-1] + [(core_bit,)])
        both = Scatter(
            jnp.concatenate([item.piece for item in sums], -1), [z_bits], z_bits
        )
        together([both, hidden_all, small])
        both = Gather(both.piece, [z_bits])
        together([both, hidden_all, small])
        sums = [
            Gather(
                both.piece[..., place * 2 * width : (place + 1) * 2 * width],
                order[::-1] + [(core_bit,)],
                [z_bits],
            )
            for place, order in enumerate((y_order + [(side,)], [(side,)] + y_order))
        ]
        while sums[0].order:
            together(sums + [hidden_all, small])
        while hidden_all.order or small.order:
            together([hidden_all, small])
        small = small.piece
        up_out, up_bias_out, down_out = hidden_out(
            dp_bits, hidden_all.piece.reshape(-1, hidden_part.shape[1]), width
        )
        squares = [item.piece.reshape(width, 2 * width) for item in sums]
        if by_kernel:
            grad_q, grad_k, grad_v, grad_o = unpack(bit_names, squares)
        else:
            grad_q, grad_k, grad_v, grad_o = (
                turn(item)[:, place * width : (place + 1) * width].astype(f32)
                for item in squares
                for place in range(2)
            )
        vectors = {name: small[i * width : (i + 1) * width] for i, name in enumerate(names)}
        return (
            unspread(*acted_sent),
            grad_tokens,
            grad_q,
            vectors["query_bias"],
            grad_k,
            grad_v,
            vectors["value_bias"],
            grad_o,
            vectors["out_bias"],
            vectors["gain_one"],
            vectors["shift_one"],
            vectors["gain_two"],
            vectors["shift_two"],
            up_out,
            up_bias_out[0],
            down_out,
            vectors["down_bias"],
            vectors["halt"],
            small[len(names) * width : len(names) * width + 1],
        )

    return per_device


def solution(mesh):
    shared = P()
    rows = P("dp", "sq", None)
    return jax.shard_map(
        make_per_device(mesh.shape["dp"], mesh.shape["sq"]),
        mesh=mesh,
        in_specs=(rows, P("dp", None), P("dp", None), P("dp", "sq"))
        + (shared,) * 11
        + (P(None, "sq"), P("sq"), P("sq", None), shared, shared, shared, rows),
        out_specs=(rows, rows)
        + (shared,) * 11
        + (P(None, "sq"), P("sq"), P("sq", None), shared, shared, shared),
        check_vma=False,
    )
```

```python
import functools
import math

import jax
import jax.numpy as jnp
from jax import lax
from jax.experimental import pallas as pl
from jax.experimental.pallas import tpu as pltpu
from jax.sharding import PartitionSpec as P

HEAD = 64
STEPS = 3
LN_EPS = 1e-05
PONDER = 0.01
MASKED = -1e30
TOO_LARGE = 1e30
QUAD = 256
PAIR = 128
SHIFT_LANE = 16
BIAS_Q, BIAS_V, BIAS_O, BIAS_D, GAIN_1, SHIFT_1, GAIN_2, SHIFT_2, HALT_W, HALT_B = range(10)
HALTS, ALONE = 0, 1
AXES = ("dp", "sq")
VMEM_LIMIT = 20 * 2**20
HIGHEST = lax.Precision.HIGHEST
bf16 = jnp.bfloat16
f32 = jnp.float32

NN = (((1,), (0,)), ((), ()))
NT = (((1,), (1,)), ((), ()))
TN = (((0,), (0,)), ((), ()))


def dot(left, right, dims=NN):
    return lax.dot_general(left, right, dims, preferred_element_type=f32)


def split_two(values):
    high = values.astype(bf16)
    return high, (values - high.astype(f32)).astype(bf16)


def iota(shape, dim):
    return lax.broadcasted_iota(jnp.int32, shape, dim)


def head_lanes(groups):
    row, lane = iota((QUAD, PAIR), 0), iota((QUAD, PAIR), 1)
    place = lane - SHIFT_LANE
    hit = (place >= 0) & (place < 8 * groups) & (place % 8 == row // HEAD)
    return jnp.where(hit, 1.0, 0.0).astype(bf16)


def head_rows():
    hit = iota((8, QUAD), 0) == iota((8, QUAD), 1) // HEAD
    return jnp.where(hit, 1.0, 0.0).astype(bf16)


def head_block():
    hit = iota((QUAD, QUAD), 0) // HEAD == iota((QUAD, QUAD), 1) // HEAD
    return jnp.where(hit, 1.0, 0.0).astype(bf16)


def exact_three(values):
    group = (iota((1, PAIR), 1) - SHIFT_LANE) // 8
    high = values.astype(bf16).astype(f32)
    rest = values - high
    middle = rest.astype(bf16).astype(f32)
    low = rest - middle
    return jnp.where(group == 0, high, jnp.where(group == 1, middle, low)).astype(bf16)


def rows_to_lanes(rows, groups):
    count = rows.shape[1]
    parts = [jnp.zeros((SHIFT_LANE, count), f32)] + [rows] * groups
    parts.append(jnp.zeros((PAIR - SHIFT_LANE - 8 * groups, count), f32))
    return jnp.concatenate(parts, 0).T


def pair_of(values, head):
    start = head // 2 * PAIR
    return values[:, start : start + PAIR]


def only_head(values, head):
    return jnp.where(iota((1, PAIR), 1) // HEAD == head % 2, pair_of(values, head), bf16(0))


def shift_lanes(shift, features, head, groups=1):
    place = iota((1, PAIR), 1) - SHIFT_LANE
    hit = (place >= 0) & (place < 8 * groups) & (place % 8 == head)
    return jnp.where(hit, -shift, features)


def norm_stats(values):
    centered = values - jnp.mean(values, axis=-1, keepdims=True)
    inverse = lax.rsqrt(jnp.mean(centered * centered, axis=-1, keepdims=True) + LN_EPS)
    return centered * inverse, inverse


def norm_back(grad, normal, inverse, gain):
    scaled = grad * gain
    return inverse * (
        scaled
        - jnp.mean(scaled, axis=-1, keepdims=True)
        - normal * jnp.mean(scaled * normal, axis=-1, keepdims=True)
    )


def near_kernel(
    own_ref, mate_ref, wq_ref, wk_ref, wv_ref, rows_ref, qf_ref, kf_ref, alone_ref,
    q_ref, k_ref, v_ref, mixed_ref, lse_ref, rows_in_ref, vt_ref,
):
    count = own_ref.shape[0]
    own = own_ref[...]

    @pl.when(pl.program_id(0) == 0)
    def _():
        rows_in_ref[:count, :] = own
        rows_in_ref[count:, :] = mate_ref[...]

    bias_q, bias_v = rows_ref[BIAS_Q : BIAS_Q + 1, :], rows_ref[BIAS_V : BIAS_V + 1, :]
    q_ref[...] = (dot(own, wq_ref[...]) + bias_q).astype(bf16) * bf16(1.0 / math.sqrt(HEAD))
    for place, rows in ((0, own), (1, mate_ref[...])):
        here = pl.ds(place * count, count)
        k_ref[here, :] = dot(rows, wk_ref[...]).astype(bf16)
        v_ref[here, :] = (dot(rows, wv_ref[...]) + bias_v).astype(bf16)
    vt_ref[...] = v_ref[...].T
    high, low = split_two(q_ref[...].astype(f32) * k_ref[:count, :].astype(f32))
    shift = dot(high, head_lanes(1)).astype(bf16)
    self_score = dot(head_rows(), high, NT) + dot(head_rows(), low, NT)
    pick = jnp.where(iota((8, PAIR), 1) == iota((8, PAIR), 0) + SHIFT_LANE, 1.0, 0.0).astype(bf16)
    base = dot(pick, shift, NT)
    lse_ref[...] = jnp.zeros_like(lse_ref)

    def one_head(head, exact):
        query = jnp.concatenate(
            [only_head(q_ref[...], head), shift_lanes(shift, qf_ref[...], head)], 1
        )
        keys = jnp.concatenate([pair_of(k_ref, head), kf_ref[...]], 1)
        scores = dot(keys, query, NT)
        start = base[head : head + 1]
        if exact:
            top = jnp.maximum(jnp.max(scores, axis=0, keepdims=True), 0.0)
            scores = scores - top
            start = start + top
        probs = jnp.exp(scores).astype(bf16)
        lanes = pl.ds(head * HEAD, HEAD)
        ones = jnp.ones((16, probs.shape[0]), bf16)
        mixed = dot(jnp.concatenate([vt_ref[lanes, :], ones], 0), probs)
        mixed, total = mixed[:HEAD], mixed[HEAD : HEAD + 1]
        alone = jnp.exp(self_score[head : head + 1] - start) * alone_ref[0:1, :]
        total = total + alone
        mixed = mixed + vt_ref[lanes, :count].astype(f32) * alone
        mixed_ref[lanes, :] = mixed / total
        lse_ref[head : head + 1, :] = start + jnp.log(total)
        return total

    most = functools.reduce(jnp.maximum, [one_head(head, False) for head in range(4)])

    @pl.when(jnp.logical_not(jnp.max(most) < TOO_LARGE))
    def _():
        for head in range(4):
            one_head(head, True)


def far_kernel(blocks, *refs):
    block_refs, refs = refs[:blocks], refs[blocks:]
    wk_ref, wv_ref, rows_ref, qf_ref, kf_ref, q_ref, near_ref, near_lse_ref = refs[:8]
    k_ref, v_ref, mixed_ref, lse_ref, rows_in_ref, rest_ref, vt_ref, total_ref = refs[8:]
    count = q_ref.shape[0]

    @pl.when(pl.program_id(0) == 0)
    def _():
        for place, block_ref in enumerate(block_refs):
            rows_in_ref[pl.ds(place * count, count), :] = block_ref[...]

    bias_v = rows_ref[BIAS_V : BIAS_V + 1, :]
    for place, block_ref in enumerate(block_refs):
        here = pl.ds(place * count, count)
        rows = block_ref[...]
        k_ref[here, :] = dot(rows, wk_ref[...]).astype(bf16)
        v_ref[here, :] = (dot(rows, wv_ref[...]) + bias_v).astype(bf16)
    vt_ref[...] = v_ref[...].T
    near_lse = near_lse_ref[...]
    base = near_lse.astype(bf16).astype(f32)
    shift = rows_to_lanes(base, 1).astype(bf16)
    lse_ref[...] = jnp.zeros_like(lse_ref)

    def one_head(head, exact):
        query = jnp.concatenate(
            [only_head(q_ref[...], head), shift_lanes(shift, qf_ref[...], head)], 1
        )
        keys = jnp.concatenate([pair_of(k_ref, head), kf_ref[...]], 1)
        scores = dot(keys, query, NT)
        start = base[head : head + 1]
        if exact:
            top = jnp.maximum(jnp.max(scores, axis=0, keepdims=True), 0.0)
            scores = scores - top
            start = start + top
        probs = jnp.exp(scores).astype(bf16)
        lanes = pl.ds(head * HEAD, HEAD)
        ones = jnp.ones((16, probs.shape[0]), bf16)
        mixed = dot(jnp.concatenate([vt_ref[lanes, :], ones], 0), probs)
        mixed, total = mixed[:HEAD], mixed[HEAD : HEAD + 1]
        before = jnp.exp(near_lse[head : head + 1] - start)
        total = total + before
        total_ref[lanes, :] = (mixed + near_ref[lanes, :] * before) / total
        lse_ref[head : head + 1, :] = start + jnp.log(total)
        return total

    most = functools.reduce(jnp.maximum, [one_head(head, False) for head in range(4)])

    @pl.when(jnp.logical_not(jnp.max(most) < TOO_LARGE))
    def _():
        for head in range(4):
            one_head(head, True)

    mixed, rest = split_two(total_ref[...].T)
    mixed_ref[...] = mixed
    rest_ref[...] = rest


def back_kernel(
    with_self, blocks, q_ref, do_ref, o_ref, rest_ref, lse_ref, k_ref, v_ref, kf_ref, wk_ref, wv_ref, qf_ref,
    *refs,
):
    if with_self:
        part_q_ref, cols_ref = refs[:2]
        refs = refs[2:]
    dq_ref, dk_ref, dv_ref, sum_ref = refs[:4]
    da_refs = refs[4 : 4 + blocks]
    kt_ref, dqt_ref, dkf_ref, dvf_ref, daf_ref = refs[4 + blocks :]
    count = q_ref.shape[0]
    step = pl.program_id(0)
    kt_ref[...] = k_ref[...].T
    query_all, grad_all = q_ref[...], do_ref[...]
    lse_terms = exact_three(rows_to_lanes(lse_ref[...], 3))
    high, low = split_two(
        grad_all.astype(f32) * (o_ref[...].astype(f32) + rest_ref[...].astype(f32))
    )
    delta_terms = exact_three(dot(high, head_lanes(3)) + dot(low, head_lanes(3)))
    for head in range(4):
        query = only_head(query_all, head)
        grad = only_head(grad_all, head)
        keys = jnp.concatenate([pair_of(k_ref, head), kf_ref[...]], 1)
        values = jnp.concatenate([pair_of(v_ref, head), kf_ref[...]], 1)
        query_wide = jnp.concatenate([query, shift_lanes(lse_terms, qf_ref[...], head, 3)], 1)
        grad_wide = jnp.concatenate([grad, shift_lanes(delta_terms, bf16(0), head, 3)], 1)
        probs = jnp.exp(dot(keys, query_wide, NT))
        back = (probs * dot(values, grad_wide, NT)).astype(bf16)
        probs = probs.astype(bf16)
        pair = pl.ds(head // 2 * PAIR, PAIR)
        if head % 2 == 0:
            dvf_ref[:, pair] = dot(probs, grad)
            dkf_ref[:, pair] = dot(back, query)
        else:
            dvf_ref[:, pair] += dot(probs, grad)
            dkf_ref[:, pair] += dot(back, query)
        lanes = pl.ds(head * HEAD, HEAD)
        dqt_ref[lanes, :] = dot(kt_ref[lanes, :], back)
    dq = dqt_ref[...].T
    if with_self:
        block = head_block()
        own_k, own_v = k_ref[:count, :].astype(f32), v_ref[:count, :].astype(f32)
        query_f, grad_f = query_all.astype(f32), grad_all.astype(f32)

        def per_head(values):
            first, second = split_two(values)
            return dot(first, block) + dot(second, block)

        spread = jnp.where(
            (iota((PAIR, QUAD), 0) >= SHIFT_LANE)
            & (iota((PAIR, QUAD), 0) < SHIFT_LANE + 24)
            & (iota((PAIR, QUAD), 0) % 8 == iota((PAIR, QUAD), 1) // HEAD),
            1.0,
            0.0,
        ).astype(bf16)
        prob = jnp.exp(per_head(query_f * own_k) - dot(lse_terms, spread)) * cols_ref[:, ALONE : ALONE + 1]
        back = prob * (per_head(grad_f * own_v) - dot(delta_terms, spread))
        dq = dq + back * own_k
        dkf_ref[:count, :] += back * query_f
        dvf_ref[:count, :] += prob * grad_f
    dq = dq * (1.0 / math.sqrt(HEAD))
    if with_self:
        dq = (dq + part_q_ref[...]).astype(bf16)
        sum_ref[0:1, :] = jnp.sum(dq.astype(f32), axis=0, keepdims=True)
    else:
        sum_ref[0:1, :] = jnp.zeros((1, QUAD), f32)
    dq_ref[...] = dq
    dk, dv = dkf_ref[...].astype(bf16), dvf_ref[...].astype(bf16)
    dk_ref[...] = dk
    dv_ref[...] = dv
    sum_ref[1:2, :] = jnp.sum(dvf_ref[...], axis=0, keepdims=True)
    part = dot(dk, wk_ref[...], NT) + dot(dv, wv_ref[...], NT)

    @pl.when(step == 0)
    def _():
        daf_ref[...] = part

    @pl.when(step > 0)
    def _():
        daf_ref[...] += part

    @pl.when(step == pl.num_programs(0) - 1)
    def _():
        for place, da_ref in enumerate(da_refs):
            da_ref[...] = daf_ref[place * count : (place + 1) * count, :].astype(bf16)


def mix_kernel(
    step_no, last, x_ref, o_ref, wo_ref, rows_ref, up_a_ref, up_b_ref, down_a_ref, down_b_ref,
    cols_ref, hidden_ref, normed_ref, act_ref, slope_ref, new_ref, *refs,
):
    if last:
        (total_ref,) = refs
    else:
        next_ref, total_ref = refs
    step = pl.program_id(0)
    width = x_ref.shape[1]

    def row(place):
        return rows_ref[place : place + 1, :]

    @pl.when(step == 0)
    def _():
        hidden = x_ref[...] + (dot(o_ref[...], wo_ref[...]) + row(BIAS_O))
        hidden_ref[...] = hidden
        normal = norm_stats(hidden)[0]
        normed_ref[:, :width] = (normal * row(GAIN_2) + row(SHIFT_2)).astype(bf16)
        one = jnp.where(iota((x_ref.shape[0], PAIR), 1) == 0, 1.0, 0.0)
        normed_ref[:, width:] = one.astype(bf16)
        total_ref[...] = hidden + row(BIAS_D)

    in_first = step < pl.num_programs(0) // 2
    before = dot(normed_ref[...], jnp.where(in_first, up_a_ref[...], up_b_ref[...]), NT)
    root = math.sqrt(2.0 / math.pi)
    square = before * before
    bent = jnp.tanh(before * (root + root * 0.044715 * square))
    half = 0.5 + 0.5 * bent
    exact = before * half
    act = exact.astype(bf16)
    act_ref[...] = act
    slope_ref[...] = (
        half + exact * (1.0 - half) * (2.0 * root + 6.0 * root * 0.044715 * square)
    ).astype(bf16)
    total_ref[...] += dot(act, jnp.where(in_first, down_a_ref[...], down_b_ref[...]))

    @pl.when(step == pl.num_programs(0) - 1)
    def _():
        live = cols_ref[:, HALTS : HALTS + 1] >= step_no + 1
        new = jnp.where(live, total_ref[...], x_ref[...])
        new_ref[...] = new
        if not last:
            next_ref[...] = (norm_stats(new)[0] * row(GAIN_1) + row(SHIFT_1)).astype(bf16)


def unmix_kernel(
    step_no, grad_ref, cols_ref, slope_ref, up_a_ref, up_b_ref, down_a_ref, down_b_ref,
    hidden_ref, rows_ref, wo_ref, dz_ref, du_ref, dh_ref, dy_ref, do_ref, sum_ref, total_ref,
):
    in_first = pl.program_id(0) < pl.num_programs(0) // 2
    step = pl.program_id(0)
    width = grad_ref.shape[1]

    def live_grad():
        return jnp.where(cols_ref[:, HALTS : HALTS + 1] >= step_no + 1, grad_ref[...], 0.0)

    @pl.when(step == 0)
    def _():
        dz_ref[...] = live_grad().astype(bf16)

    down = jnp.where(in_first, down_a_ref[...], down_b_ref[...])
    du = (slope_ref[...].astype(f32) * dot(dz_ref[...], down, NT)).astype(bf16)
    du_ref[...] = du
    part = dot(du, jnp.where(in_first, up_a_ref[:, :width], up_b_ref[:, :width]))

    @pl.when(step == 0)
    def _():
        total_ref[...] = part

    @pl.when(step > 0)
    def _():
        total_ref[...] += part

    @pl.when(step == pl.num_programs(0) - 1)
    def _():
        normal, inverse = norm_stats(hidden_ref[...])
        back = total_ref[...]
        gain = rows_ref[GAIN_2 : GAIN_2 + 1, :]
        dh = live_grad() + norm_back(back, normal, inverse, gain)
        dh_ref[...] = dh
        dy = dh.astype(bf16)
        dy_ref[...] = dy
        do_ref[...] = dot(dy, wo_ref[...], NT).astype(bf16)
        sum_ref[0:1, :] = jnp.sum(dz_ref[...].astype(f32), axis=0, keepdims=True)
        sum_ref[1:2, :] = jnp.sum(dy.astype(f32), axis=0, keepdims=True)
        sum_ref[2:3, :] = jnp.sum(back * normal, axis=0, keepdims=True)
        sum_ref[3:4, :] = jnp.sum(back, axis=0, keepdims=True)


def half_of(first_ref, second_ref):
    in_first = pl.program_id(0) < pl.num_programs(0) // 2
    return jnp.where(in_first, first_ref[...], second_ref[...])


def join_kernel(
    step_no, received, dq_ref, wq_ref, near_ref, x_ref, rows_ref, grad_ref, cols_ref, dh_ref,
    halt_ref, cot_a_ref, cot_b_ref, *refs,
):
    parts, (new_ref, sum_ref) = refs[:received], refs[received:]
    back = dot(dq_ref[...], wq_ref[...], NT) + near_ref[...].astype(f32)
    for part in parts:
        back = back + part[...].astype(f32)
    values = x_ref[...]
    normal, inverse = norm_stats(values)
    slope = halt_ref[:, step_no : step_no + 1]
    passed = jnp.where(cols_ref[:, HALTS : HALTS + 1] >= step_no + 1, 0.0, grad_ref[...])
    new = (
        passed
        + dh_ref[...]
        + norm_back(back, normal, inverse, rows_ref[GAIN_1 : GAIN_1 + 1, :])
        + slope * rows_ref[HALT_W : HALT_W + 1, :]
    )
    if step_no > 0:
        weight = halt_ref[:, STEPS + step_no - 1 : STEPS + step_no]
        new = new + weight * half_of(cot_a_ref, cot_b_ref).astype(f32)
    new_ref[...] = new
    sums = [back * normal, back, slope * values]

    @pl.when(pl.program_id(0) == 0)
    def _():
        sum_ref[...] = jnp.zeros_like(sum_ref)

    for place, item in enumerate(sums):
        sum_ref[place : place + 1, :] += jnp.sum(item, axis=0, keepdims=True)


def halt_kernel(*refs):
    state_refs = refs[: STEPS + 1]
    rows_ref, cols_ref, cot_a_ref, cot_b_ref, acted_ref, grad_ref, halt_ref, sum_ref = refs[
        STEPS + 1 :
    ]
    states = [ref[...] for ref in state_refs]
    cot = half_of(cot_a_ref, cot_b_ref).astype(f32)
    halts = cols_ref[:, HALTS : HALTS + 1]
    halt_row = rows_ref[HALT_W : HALT_W + 1, :]
    halt_bias = rows_ref[HALT_B : HALT_B + 1, 0:1]
    final_dot = jnp.sum(cot * states[STEPS], axis=-1, keepdims=True)
    remainder = jnp.ones_like(halts)
    acted = jnp.zeros_like(states[0])
    slopes, weights = [], []
    for step in range(STEPS):
        logit = jnp.sum(states[step] * halt_row, axis=-1, keepdims=True) + halt_bias
        prob = (1.0 / (1.0 + jnp.exp(-logit))) / STEPS
        early = halts > step + 1
        weight = jnp.where(early, prob, 0.0)
        weights.append(weight)
        remainder = remainder - weight
        acted = acted + weight * states[step + 1]
        step_dot = jnp.sum(cot * states[step + 1], axis=-1, keepdims=True)
        slope = (step_dot - final_dot - PONDER) * prob * (1.0 - STEPS * prob)
        slopes.append(jnp.where(early, slope, 0.0))
    acted_ref[...] = (acted + remainder * states[STEPS]).astype(bf16)
    grad_ref[...] = (remainder + weights[STEPS - 1]) * cot
    lane = iota((halts.shape[0], PAIR), 1)
    table = jnp.zeros((halts.shape[0], PAIR), f32)
    for place, column in enumerate(slopes + weights):
        table = jnp.where(lane == place, column, table)
    halt_ref[...] = table

    @pl.when(pl.program_id(0) == 0)
    def _():
        sum_ref[...] = jnp.zeros_like(sum_ref)

    sum_ref[0:1, :] += jnp.sum(jnp.where(lane < STEPS, table, 0.0), axis=0, keepdims=True)


def outset_kernel(
    tokens_ref, mask_ref, halts_ref, cot_ref, lengths_ref, own_ref, other_ref, cot_own_ref,
    cot_other_ref,
):
    seq_here, width = tokens_ref.shape[1:]
    parity = lax.axis_index("sq") % 2
    lane = iota((1, width), 1)

    def row_of(ref, row):
        return jnp.where(row == 0, ref[0:1, :], ref[1:2, :]).astype(f32)

    for row, out_ref, cot_out_ref in (
        (parity, own_ref, cot_own_ref), (1 - parity, other_ref, cot_other_ref)
    ):
        cot_out_ref[...] = cot_ref[row]
        out_ref[:seq_here, :] = tokens_ref[row]
        mask = row_of(mask_ref, row)
        parts = [mask[:, at : at + width] for at in range(0, mask.shape[1], width)]
        halts = row_of(halts_ref, row)
        if seq_here < width:
            halts = jnp.concatenate([halts, jnp.zeros((1, width - seq_here), f32)], 1)
        parts.append(halts)
        for part in (lambda value: value // 16, lambda value: value % 16):
            entry = jnp.zeros((1, width), jnp.int32)
            for doc in range(lengths_ref.shape[1]):
                entry = jnp.where(lane == doc, part(lengths_ref[row, doc]), entry)
            parts.append(entry.astype(f32))
        parts.append(jnp.zeros((out_ref.shape[0] - seq_here - len(parts), width), f32))
        out_ref[seq_here:, :] = jnp.concatenate(parts, 0).astype(bf16)


def begin_kernel(
    middle, docs, row_len, a_ref, b_ref, rows_ref, x_ref, normed_ref, qf_ref, near_ref, far_ref,
    cols_ref, alone_ref, row_ref,
):
    count, width = x_ref.shape
    seq_here = count // 2
    d_at, s_at = lax.axis_index("dp"), lax.axis_index("sq")
    top = 2 * middle
    parity, core, chip = s_at % 2, d_at % 2, s_at % top // 2
    for place, ref in enumerate((a_ref, b_ref)):
        here = pl.ds(place * seq_here, seq_here)
        values = ref[:seq_here, :].astype(f32)
        x_ref[here, :] = values
        normed_ref[here, :] = (
            norm_stats(values)[0] * rows_ref[GAIN_1 : GAIN_1 + 1, :]
            + rows_ref[SHIFT_1 : SHIFT_1 + 1, :]
        ).astype(bf16)
    info = a_ref[seq_here:, :].astype(f32)
    mask_rows = row_len // width
    for at in range(mask_rows):
        row_ref[:, at * width : (at + 1) * width] = jnp.broadcast_to(
            info[at : at + 1, :], (row_ref.shape[0], width)
        )
    lengths = info[mask_rows + 1 : mask_rows + 2, :] * 16.0 + info[mask_rows + 2 : mask_rows + 3, :]
    lane = iota((1, width), 1)
    ends = [
        jnp.sum(jnp.where(lane <= doc, lengths, 0.0), axis=1, keepdims=True)
        for doc in range(docs)
    ]

    def at_block(core_at, chip_at):
        start = (core_at * middle + chip_at) * count
        block = row_ref[0:1, pl.ds(pl.multiple_of(start, count), count)]
        turned = jnp.concatenate([block[:, seq_here:], block[:, :seq_here]], 1)
        offset = iota((1, count), 1) + parity * seq_here
        place = (start + jnp.where(offset >= count, offset - count, offset)).astype(f32)
        doc_at = jnp.zeros((1, count), jnp.int32)
        for end in ends:
            doc_at = doc_at + jnp.where(place >= end, 1, 0)
        return doc_at, jnp.where(parity == 0, block, turned)

    kind = iota((PAIR, 1), 0)

    def key_features(core_at, chip_at):
        doc_at, open_at = at_block(core_at, chip_at)
        closed = (kind == doc_at) | ((kind == 8) & (open_at == 0))
        ones = jnp.where(kind >= SHIFT_LANE, 1.0, 0.0)
        return jnp.where(closed, MASKED, jnp.broadcast_to(ones, closed.shape)).T.astype(bf16)

    doc_at, open_at = at_block(core, chip)
    wanted = ((kind < docs) & (kind != doc_at)) | (kind == 8)
    qf_ref[...] = jnp.where(wanted, 1.0, 0.0).T.astype(bf16)
    for place, core_at in enumerate((core, 1 - core)):
        near_ref[pl.ds(place * count, count), :] = key_features(core_at, chip)
    place = 0
    for offset in range(1, middle):
        for core_at in (core, 1 - core):
            far_ref[pl.ds(place * count, count), :] = key_features(core_at, chip ^ offset)
            place += 1
    halts = jnp.concatenate(
        [
            ref[seq_here:, :].astype(f32)[mask_rows : mask_rows + 1, :seq_here]
            for ref in (a_ref, b_ref)
        ],
        1,
    )
    alone = jnp.where(open_at == 0, 1.0, 0.0)
    alone_ref[...] = jnp.broadcast_to(alone, alone_ref.shape)
    table = jnp.where(kind == HALTS, halts, jnp.where(kind == ALONE, alone, 0.0))
    cols_ref[...] = table.T


def small_kernel(unmix_refs, near_refs, far_refs, join_refs, halt_ref, out_ref):
    def row(refs, place):
        return sum(ref[place : place + 1, :] for ref in refs)

    out_ref[...] = jnp.zeros_like(out_ref)
    entries = (
        row(near_refs, 0), row(near_refs, 1) + row(far_refs, 1), row(unmix_refs, 1),
        row(join_refs, 0), row(join_refs, 1), row(unmix_refs, 2), row(unmix_refs, 3),
        row(unmix_refs, 0), row(join_refs, 2),
    )
    for place, entry in enumerate(entries):
        out_ref[place : place + 1, :] = entry
    bias = jnp.sum(halt_ref[0:1, :], axis=1, keepdims=True)
    out_ref[len(entries) : len(entries) + 1, :] = jnp.broadcast_to(bias, (1, out_ref.shape[1]))


def hidden_grads_kernel(steps, *refs):
    act_refs, dz_refs, du_refs, normed_refs = (refs[i * steps : (i + 1) * steps] for i in range(4))
    out_ref = refs[4 * steps]
    wide = normed_refs[0].shape[1]
    out_ref[:, :wide] = sum(
        dot(du[...], normed[...], TN) for du, normed in zip(du_refs, normed_refs)
    ).astype(bf16)
    out_ref[:, wide:] = sum(
        dot(act[...], dz[...], TN) for act, dz in zip(act_refs, dz_refs)
    ).astype(bf16)


def pack_kernel(bits, *refs):
    sources, results = refs[: len(refs) // 3 * 2], refs[len(refs) // 3 * 2 :]
    blocks = 2 ** len(bits)
    rows = sources[0].shape[0] // blocks
    width = sources[0].shape[1]
    own = own_block(bits)
    for block in range(blocks):
        start = pl.multiple_of((own ^ block) * rows, rows)
        for place, source in enumerate(sources):
            lanes = pl.ds(place % 2 * width, width)
            results[place // 2][pl.ds(block * rows, rows), lanes] = source[
                pl.ds(start, rows), :
            ].astype(bf16)


def unpack_kernel(bits, *refs):
    sources, results = refs[: len(refs) // 3], refs[len(refs) // 3 :]
    blocks = 2 ** len(bits)
    rows = sources[0].shape[0] // blocks
    width = sources[0].shape[1] // 2
    own = own_block(bits)
    for block in range(blocks):
        start = pl.multiple_of((own ^ block) * rows, rows)
        for place, result in enumerate(results):
            lanes = pl.ds(place % 2 * width, width)
            result[pl.ds(block * rows, rows), :] = sources[place // 2][
                pl.ds(start, rows), lanes
            ].astype(f32)


def hidden_out_kernel(dp_bits, source_ref, up_ref, bias_ref, down_ref, wide_ref, order_ref):
    width = down_ref.shape[1]
    blocks = 2 ** len(dp_bits)
    rows = source_ref.shape[0] // blocks
    own = own_block([(bit, 0) for bit in dp_bits])
    wide_ref[...] = source_ref[...].astype(f32)
    for block in range(blocks):
        place = sum(
            (1 << at) for at, bit in enumerate(dp_bits[::-1]) if block & bit
        )
        start = pl.multiple_of((own ^ place) * rows, rows)
        order_ref[pl.ds(block * rows, rows), :] = wide_ref[pl.ds(start, rows), :]
    up_ref[...] = order_ref[:, :width].T
    bias_ref[...] = jnp.broadcast_to(order_ref[:, width : width + PAIR].T[0:1, :], bias_ref.shape)
    down_ref[...] = order_ref[:, width + PAIR :]


def own_block(bits):
    own = jnp.int32(0)
    for d_bit, s_bit in bits:
        at = lax.axis_index("dp") & d_bit if d_bit else lax.axis_index("sq") & s_bit
        own = own * 2 + jnp.where(at != 0, 1, 0)
    return own


def whole(shape):
    return pl.BlockSpec(shape, lambda i: (0,) * len(shape))


def lanes_of(rows, width=QUAD):
    return pl.BlockSpec((rows, width), lambda i: (0, i))


def rows_of(rows, width):
    return pl.BlockSpec((rows, width), lambda i: (i, 0))


def shaped(shape, dtype):
    return jax.ShapeDtypeStruct(shape, dtype)


def in_hbm(value):
    return pltpu.with_memory_space_constraint(value, pltpu.HBM)


def params(flops, moved, exps=0):
    return dict(
        compiler_params=pltpu.CompilerParams(vmem_limit_bytes=VMEM_LIMIT),
        cost_estimate=pl.CostEstimate(
            flops=int(flops), bytes_accessed=int(moved), transcendentals=int(exps)
        ),
    )


def attend_near(own, mate, wq, wk, wv, rows, qf, kf, alone):
    count, width = own.shape
    quads = width // QUAD
    keys = 2 * count
    return pl.pallas_call(
        near_kernel,
        grid=(quads,),
        in_specs=[
            whole((count, width)), whole((count, width)),
            lanes_of(width), lanes_of(width), lanes_of(width), lanes_of(rows.shape[0]),
            whole((count, PAIR)), whole((keys, PAIR)), whole((8, count)),
        ],
        out_specs=[
            lanes_of(count), lanes_of(keys), lanes_of(keys), rows_of(QUAD, count),
            rows_of(8, count), whole((keys, width)),
        ],
        out_shape=[
            shaped((count, width), bf16), shaped((keys, width), bf16), shaped((keys, width), bf16),
            shaped((width, count), f32), shaped((8 * quads, count), f32),
            shaped((keys, width), bf16),
        ],
        scratch_shapes=[pltpu.VMEM((QUAD, keys), bf16)],
        name="attend_near",
        **params(8 * count * keys * width * 2, 10 * count * width * 2, count * keys * 8),
    )(own, mate, wq, wk, wv, rows, qf, kf, alone)


def attend_far(blocks, wk, wv, rows, qf, kf, queries, near_mixed, near_lse):
    count, width = queries.shape
    quads = width // QUAD
    keys = len(blocks) * count
    return pl.pallas_call(
        functools.partial(far_kernel, len(blocks)),
        grid=(quads,),
        in_specs=[whole((count, width))] * len(blocks)
        + [
            lanes_of(width), lanes_of(width), lanes_of(rows.shape[0]),
            whole((count, PAIR)), whole((keys, PAIR)), lanes_of(count), rows_of(QUAD, count),
            rows_of(8, count),
        ],
        out_specs=[
            lanes_of(keys), lanes_of(keys), lanes_of(count), rows_of(8, count), whole((keys, width)),
            lanes_of(count),
        ],
        out_shape=[
            shaped((keys, width), bf16), shaped((keys, width), bf16), shaped((count, width), bf16),
            shaped((8 * quads, count), f32), shaped((keys, width), bf16),
            shaped((count, width), bf16),
        ],
        scratch_shapes=[pltpu.VMEM((QUAD, keys), bf16), pltpu.VMEM((QUAD, count), f32)],
        name="attend_far",
        **params(8 * count * keys * width * 2, 10 * count * width * 2, count * keys * 8),
    )(*blocks, wk, wv, rows, qf, kf, queries, near_mixed, near_lse)


def attend_back(
    queries, grad_mixed, mixed, rest, lse, keys_in, values_in, kf, wk, wv, qf, partial, cols
):
    count, width = queries.shape
    quads = width // QUAD
    keys = keys_in.shape[0]
    blocks = keys // count
    with_self = cols is not None
    extra = [partial, cols] if with_self else []
    extra_specs = [lanes_of(count), whole((count, PAIR))] if with_self else []
    return pl.pallas_call(
        functools.partial(back_kernel, with_self, blocks),
        grid=(quads,),
        in_specs=[
            lanes_of(count), lanes_of(count), lanes_of(count), lanes_of(count), rows_of(8, count),
            lanes_of(keys), lanes_of(keys), whole((keys, PAIR)), lanes_of(width), lanes_of(width),
            whole((count, PAIR)),
        ]
        + extra_specs,
        out_specs=[lanes_of(count), lanes_of(keys), lanes_of(keys), lanes_of(8)]
        + [whole((count, width))] * blocks,
        out_shape=[
            shaped((count, width), bf16 if with_self else f32), shaped((keys, width), bf16),
            shaped((keys, width), bf16), shaped((8, width), f32),
        ]
        + [shaped((count, width), bf16)] * blocks,
        scratch_shapes=[
            pltpu.VMEM((QUAD, keys), bf16), pltpu.VMEM((QUAD, count), f32),
            pltpu.VMEM((keys, QUAD), f32), pltpu.VMEM((keys, QUAD), f32),
            pltpu.VMEM((keys, width), f32),
        ],
        name="back_near" if with_self else "back_far",
        **params(20 * count * keys * width * 2, 20 * count * width * 2, count * keys * 8),
    )(queries, grad_mixed, mixed, rest, lse, keys_in, values_in, kf, wk, wv, qf, *extra)


def halves_of(rows, width, steps):
    half = steps // 2
    return [
        pl.BlockSpec((rows, width), lambda i: (jnp.minimum(i, half - 1), 0)),
        pl.BlockSpec((rows, width), lambda i: (jnp.maximum(i - half, 0), 0)),
    ]


def mix(step_no, x, mixed, wo, rows, ups, downs, cols, last):
    count, width = x.shape
    hidden = 2 * ups[0].shape[0]
    chunk = min(1024, hidden // 2)
    steps = hidden // chunk
    square = whole((count, width))
    wide = width + PAIR
    out_specs = [
        square, whole((count, wide)), lanes_of(count, chunk), lanes_of(count, chunk), square,
    ]
    out_shape = [
        shaped((count, width), f32), shaped((count, wide), bf16), shaped((count, hidden), bf16),
        shaped((count, hidden), bf16), shaped((count, width), f32),
    ]
    if not last:
        out_specs.append(square)
        out_shape.append(shaped((count, width), bf16))
    return pl.pallas_call(
        functools.partial(mix_kernel, step_no, last),
        grid=(hidden // chunk,),
        in_specs=[
            square, square, whole((width, width)), whole(rows.shape),
            *halves_of(chunk, wide, steps), *halves_of(chunk, width, steps),
            whole((count, PAIR)),
        ],
        out_specs=out_specs,
        out_shape=out_shape,
        scratch_shapes=[pltpu.VMEM((count, width), f32)],
        name="mix",
        **params(4 * count * width * hidden, 16 * count * width + 8 * width * hidden),
    )(x, mixed, wo, rows, *ups, *downs, cols)


def unmix(step_no, grad, cols, slope, ups, downs, hidden_state, rows, wo):
    count, width = grad.shape
    hidden = 2 * ups[0].shape[0]
    chunk = min(1024, hidden // 2)
    steps = hidden // chunk
    square = whole((count, width))
    return pl.pallas_call(
        functools.partial(unmix_kernel, step_no),
        grid=(hidden // chunk,),
        in_specs=[
            square, whole((count, PAIR)), lanes_of(count, chunk),
            *halves_of(chunk, width + PAIR, steps), *halves_of(chunk, width, steps), square,
            whole(rows.shape), whole((width, width)),
        ],
        out_specs=[
            square, lanes_of(count, chunk), square, square, square, whole((8, width)),
        ],
        out_shape=[
            shaped((count, width), bf16), shaped((count, hidden), bf16), shaped((count, width), f32),
            shaped((count, width), bf16), shaped((count, width), bf16), shaped((8, width), f32),
        ],
        scratch_shapes=[pltpu.VMEM((count, width), f32)],
        name="unmix",
        **params(4 * count * width * hidden, 16 * count * width + 8 * width * hidden),
    )(grad, cols, slope, *ups, *downs, hidden_state, rows, wo)


def join(step_no, dq, wq, near, x, rows, grad, cols, dh, halt_table, cot, parts):
    count, width = x.shape
    piece = min(128, count // 2)
    part, table = rows_of(piece, width), rows_of(piece, PAIR)
    return pl.pallas_call(
        functools.partial(join_kernel, step_no, len(parts)),
        grid=(count // piece,),
        in_specs=[
            part, whole((width, width)), part, part, whole(rows.shape), part, table, part, table,
            *halves_of(piece, width, count // piece),
        ]
        + [part] * len(parts),
        out_specs=[part, whole((8, width))],
        out_shape=[shaped((count, width), f32), shaped((8, width), f32)],
        name="join",
        **params(2 * count * width * width, 24 * count * width),
    )(dq, wq, near, x, rows, grad, cols, dh, halt_table, *cot, *parts)


def halting(states, rows, cols, cot):
    count, width = states[0].shape
    piece = min(128, count // 2)
    part, table = rows_of(piece, width), rows_of(piece, PAIR)
    return pl.pallas_call(
        halt_kernel,
        grid=(count // piece,),
        in_specs=[part] * len(states) + [whole(rows.shape), table, *halves_of(piece, width, count // piece)],
        out_specs=[part, part, table, whole((8, PAIR))],
        out_shape=[
            shaped((count, width), bf16), shaped((count, width), f32), shaped((count, PAIR), f32),
            shaped((8, PAIR), f32),
        ],
        name="halting",
        **params(20 * count * width, 24 * count * width),
    )(*states, rows, cols, *cot)


def outset(tokens, mask, halts, cot, lengths):
    seq_here, width = tokens.shape[1:]
    here = pl.BlockSpec(memory_space=pltpu.VMEM)
    extra = -(-(mask.shape[1] // width + 3) // 16) * 16
    block = shaped((seq_here + extra, width), bf16)
    return pl.pallas_call(
        outset_kernel,
        in_specs=[here] * 4 + [pl.BlockSpec(memory_space=pltpu.SMEM)],
        out_specs=[here] * 4,
        out_shape=[block] * 2 + [shaped((seq_here, width), bf16)] * 2,
        name="outset",
        **params(0, 8 * seq_here * width),
    )(*map(in_hbm, (tokens, mask, halts, cot)), lengths)


def begin(middle, docs, row_len, blocks, rows, seq_here):
    width = blocks[0].shape[1]
    count = 2 * seq_here
    far = max(2 * (middle - 1), 1) * count
    here = pl.BlockSpec(memory_space=pltpu.VMEM)
    return pl.pallas_call(
        functools.partial(begin_kernel, middle, docs, row_len),
        in_specs=[here] * 3,
        out_specs=[here] * 7,
        out_shape=[
            shaped((count, width), f32), shaped((count, width), bf16),
            shaped((count, PAIR), bf16), shaped((2 * count, PAIR), bf16), shaped((far, PAIR), bf16),
            shaped((count, PAIR), f32), shaped((8, count), f32),
        ],
        scratch_shapes=[pltpu.VMEM((8, row_len), f32)],
        name="begin",
        **params(10 * count * width, 16 * count * width),
    )(*blocks, rows)


def small_sums(unmix_sums, near_sums, far_sums, join_sums, halt_sums):
    steps, width = len(unmix_sums), unmix_sums[0].shape[1]
    here = pl.BlockSpec(memory_space=pltpu.VMEM)

    def body(*refs):
        groups = [refs[at * steps : (at + 1) * steps] for at in range(4)]
        small_kernel(*groups, *refs[4 * steps :])

    return pl.pallas_call(
        body,
        in_specs=[here] * (4 * steps + 1),
        out_specs=here,
        out_shape=shaped((16, width), f32),
        name="small_sums",
        **params(0, 64 * width),
    )(*unmix_sums, *near_sums, *far_sums, *join_sums, halt_sums)


def hidden_grads(acts, dzs, dus, normeds):
    count, hidden = acts[0].shape
    width, wide = dzs[0].shape[1], normeds[0].shape[1]
    chunk = min(256, hidden)
    tall = lanes_of(count, chunk)
    steps = len(acts)
    return pl.pallas_call(
        functools.partial(hidden_grads_kernel, steps),
        grid=(hidden // chunk,),
        in_specs=[tall] * steps
        + [whole((count, width))] * steps
        + [tall] * steps
        + [whole((count, wide))] * steps,
        out_specs=rows_of(chunk, wide + width),
        out_shape=shaped((hidden, wide + width), bf16),
        name="hidden_grads",
        **params(4 * steps * count * width * hidden, 4 * steps * count * hidden),
    )(*map(in_hbm, acts), *dzs, *map(in_hbm, dus), *normeds)


def pack(bits, sources):
    rows, width = sources[0].shape
    here = pl.BlockSpec(memory_space=pltpu.VMEM)
    return pl.pallas_call(
        functools.partial(pack_kernel, bits),
        in_specs=[here] * len(sources),
        out_specs=[here] * (len(sources) // 2),
        out_shape=[shaped((rows, 2 * width), bf16)] * (len(sources) // 2),
        name="pack",
        **params(0, 6 * rows * width * len(sources)),
    )(*sources)


def unpack(bits, sources):
    rows, width = sources[0].shape
    here = pl.BlockSpec(memory_space=pltpu.VMEM)
    return pl.pallas_call(
        functools.partial(unpack_kernel, bits),
        in_specs=[here] * len(sources),
        out_specs=[here] * (2 * len(sources)),
        out_shape=[shaped((rows, width // 2), f32)] * (2 * len(sources)),
        name="unpack",
        **params(0, 6 * rows * width * len(sources)),
    )(*sources)


def hidden_out(dp_bits, source, width):
    rows = source.shape[0]
    here = pl.BlockSpec(memory_space=pltpu.VMEM)
    return pl.pallas_call(
        functools.partial(hidden_out_kernel, dp_bits),
        in_specs=[here],
        out_specs=[here] * 3,
        out_shape=[shaped((width, rows), f32), shaped((8, rows), f32), shaped((rows, width), f32)],
        scratch_shapes=[pltpu.VMEM(source.shape, f32), pltpu.VMEM(source.shape, f32)],
        name="hidden_out",
        **params(0, 6 * rows * source.shape[1]),
    )(source)


def make_per_device(dp_size, sq_size):
    middle = sq_size // 4
    top = sq_size // 2

    def permute(value, move):
        pairs = []
        for d in range(dp_size):
            for s in range(sq_size):
                to_d, to_s = move(d, s)
                pairs.append((d * sq_size + s, to_d * sq_size + to_s))
        return lax.ppermute(value, AXES, pairs)

    def swap(value, d_bits, s_bits):
        return permute(value, lambda d, s: (d ^ d_bits, s ^ s_bits))

    def regroup(flip):
        def move(d, s):
            upper, core = s // top, d % 2
            return d - core + upper, (core * top + s % top) ^ flip

        return move

    def bits_of(size):
        return [1 << place for place in range(size.bit_length() - 1)]

    dp_bits, sq_bits = bits_of(dp_size), bits_of(sq_size)
    bit_names = [(bit, 0) for bit in dp_bits] + [(0, bit) for bit in sq_bits[::-1]]

    def with_bits(value, names=bit_names):
        return value.reshape((2,) * len(names) + (-1,) + value.shape[len(value.shape) - 1 :])

    def offsets_of(group):
        result = []
        for code in range(1, 2 ** len(group)):
            digits = [code >> (len(group) - 1 - at) & 1 for at in range(len(group))]
            move = [0, 0]
            for digit, (d_bit, s_bit) in zip(digits, group):
                move[0] |= d_bit * digit
                move[1] |= s_bit * digit
            result.append((tuple(move), digits))
        return result

    class Gather:
        def __init__(self, piece, order, axes=()):
            self.piece, self.order, self.axes = piece, list(order), list(axes)

        def start(self):
            return [swap(self.piece, *move) for move, _ in offsets_of(self.order[0])]

        def finish(self, arrived):
            group = self.order.pop(0)
            first = bit_names.index(group[0])
            place = sum(bit_names.index(axis[0]) < first for axis in self.axes)
            self.axes.insert(place, group)
            self.piece = jnp.stack([self.piece] + list(arrived), place)

    class Scatter:
        def __init__(self, total, order, names=bit_names):
            self.piece, self.order, self.names = with_bits(total, names), list(order), list(names)

        def start(self):
            group = self.order[0]
            sent = []
            for move, digits in [(None, [0] * len(group))] + offsets_of(group):
                part = self.piece
                taken = sorted(zip(group, digits), key=lambda item: -self.names.index(item[0]))
                for name, digit in taken:
                    part = lax.index_in_dim(part, digit, self.names.index(name), False)
                if move is None:
                    self.kept = part
                else:
                    sent.append(swap(part, *move))
            return sent

        def finish(self, arrived):
            for name in self.order.pop(0):
                self.names.remove(name)
            self.piece = self.kept
            for item in arrived:
                self.piece = self.piece + item

    class Small:
        def __init__(self, total, order):
            self.piece, self.order = total, list(order)

        def start(self):
            return [swap(self.piece, *move) for move, _ in offsets_of(self.order[0])]

        def finish(self, arrived):
            self.order.pop(0)
            for item in arrived:
                self.piece = self.piece + item

    def together(chains, others=()):
        chains = [chain for chain in chains if chain.order]
        sent = [chain.start() for chain in chains]
        flat = [item for items in sent for item in items] + list(others)
        if flat:
            flat = list(lax.optimization_barrier(tuple(flat)))
        for chain, items in zip(chains, sent):
            chain.finish([flat.pop(0) for _ in items])
        return flat

    def own_part(shard):
        rows = shard.shape[0] // dp_size
        return lax.dynamic_slice_in_dim(shard, lax.axis_index("dp") * rows, rows, 0)

    def turn(total):
        shape = total.shape
        total = with_bits(total)
        for axis, (d_bit, s_bit) in enumerate(bit_names):
            own = ((lax.axis_index("dp") & d_bit) | (lax.axis_index("sq") & s_bit)) != 0
            total = jnp.where(own, jnp.flip(total, axis), total)
        return total.reshape(shape)

    def after(value, *others):
        return lax.optimization_barrier((value,) + others)[0]

    def per_device(
        tokens, lengths, key_mask, halt_steps, query_weight, query_bias, key_weight, value_weight,
        value_bias, out_weight, out_bias, first_gain, first_shift, second_gain, second_shift,
        up_weight, up_bias, down_weight, down_bias, halt_weight, halt_bias, cotangent,
    ):
        seq_here, width = tokens.shape[1:]
        parity = lax.axis_index("sq") % 2

        def send_back(value):
            return [
                permute(value[:seq_here], regroup(0)), permute(value[seq_here:], regroup(1))
            ]

        def unspread(own, other):
            first = jnp.where(parity == 0, own, other)
            second = jnp.where(parity == 0, other, own)
            return jnp.stack([first, second], 0)

        *leaving, cot_own, cot_other = outset(tokens, key_mask, halt_steps, cotangent, lengths)
        tokens_here = [permute(block, regroup(flip)) for flip, block in enumerate(leaving)]
        core_bit, side = (1, 0), (0, 1)
        z_bits = tuple((0, bit) for bit in sq_bits[::-1][:-1])
        y_order = [((bit, 0),) for bit in dp_bits[1:]]
        z_order = [(bit,) for bit in z_bits]
        up_wide = jnp.concatenate(
            [up_weight.T, jnp.pad(up_bias[:, None], ((0, 0), (0, PAIR - 1)))], 1
        )
        gathers = [
            Gather(own_part(up_wide), z_order + [(side,)] + y_order),
            Gather(own_part(down_weight), z_order + y_order + [(side,)]),
        ]

        def gather_step(*others):
            sent = [gather.start() for gather in gathers]
            for gather, items in zip(gathers, sent):
                gather.finish([after(item, *others) for item in items])

        def gathered():
            return [gather.piece for gather in gathers]

        rows = jnp.stack(
            [
                item.astype(f32)
                for item in (
                    query_bias, value_bias, out_bias, down_bias, first_gain, first_shift,
                    second_gain, second_shift, halt_weight, jnp.broadcast_to(halt_bias, (width,)),
                )
            ]
            + [jnp.zeros((width,), f32)] * 6
        )
        gather_step()
        tokens_here = [after(item, *gathered()) for item in tokens_here]
        x, normed, query_feats, near_feats, far_feats, cols, alone_row = begin(
            middle, lengths.shape[1], key_mask.shape[1], tokens_here, rows, seq_here
        )

        states, kept = [x], []
        for step in range(STEPS):
            x = states[-1]
            arrived = [swap(normed, 0, offset * 2) for offset in range(1, middle)]
            mate = swap(normed, 1, 0)
            if step == 0:
                gather_step(normed)
                mate = after(mate, *gathered())
            queries, keys_near, values_near, near_mixed, near_lse, near_in = attend_near(
                normed, mate, query_weight, key_weight, value_weight, rows, query_feats,
                near_feats, alone_row,
            )
            if step == 0:
                gather_step(near_lse)
                arrived = [after(block, *gathered()) for block in arrived]
            far = []
            for block in arrived:
                block = after(block, near_lse)
                far += [block, swap(block, 1, 0)]
            if step == 1:
                cot = [
                    permute(after(block, far[0]), regroup(flip))
                    for flip, block in enumerate((cot_own, cot_other))
                ]
            keys_far, values_far, mixed, lse, far_in, rest = attend_far(
                far, key_weight, value_weight, rows, query_feats, far_feats, queries, near_mixed,
                near_lse,
            )
            if step == 0:
                gather_step(lse)
                while gathers[0].order:
                    gather_step()
                halves = []
                for gather, weight in zip(gathers, (up_wide, down_weight)):
                    half = gather.piece.reshape(-1, weight.shape[1])
                    halves.append((half, swap(half, *core_bit)))
                up_rows, down_rows = halves
            out = mix(
                step, x, mixed, out_weight, rows, up_rows, down_rows, cols, step == STEPS - 1
            )
            hidden, normed_two, act, slope, new = out[:5]
            kept.append(
                (near_in, far_in, queries, keys_near, values_near, keys_far, values_far, mixed,
                 rest, lse, hidden, normed_two, act, slope)
            )
            states.append(new)
            if step < STEPS - 1:
                normed = out[5]
            if step == 1:
                normed, *cot = lax.optimization_barrier((normed, *cot))

        acted, grad, halt_table, halt_sums = halting(states, rows, cols, cot)
        acted_sent = send_back(acted)
        total = {}

        def add(name, value):
            total[name] = total[name] + value if name in total else value

        small_parts = ([], [], [], [])
        hidden_parts = []
        for step in reversed(range(STEPS)):
            (near_in, far_in, queries, keys_near, values_near, keys_far, values_far, mixed, rest,
             lse, hidden, normed_two, act, slope) = kept[step]
            dz, du, dh, dy, grad_mixed, sums = unmix(
                step, grad, cols, slope, up_rows, down_rows, hidden, rows, out_weight
            )
            hidden_parts.append((act, dz, du, normed_two))
            small_parts[0].append(sums)
            add("out", dot(mixed, dy, TN))
            if step == 0:
                hidden_part = hidden_grads(*zip(*hidden_parts))
                grad_mixed = after(grad_mixed, hidden_part)
                hidden_sum = Scatter(hidden_part, [(core_bit,)])
                together([hidden_sum])
                names, wide = hidden_sum.names, normed_two.shape[1]
                hidden_sums = [
                    Scatter(hidden_sum.piece[..., :wide], y_order + [(side,)], names),
                    Scatter(hidden_sum.piece[..., wide:], [(side,)] + y_order, names),
                ]
            part_q, dk_far, dv_far, far_sums, *da_far = attend_back(
                queries, grad_mixed, mixed, rest, lse, keys_far, values_far, far_feats, key_weight,
                value_weight, query_feats, None, None,
            )
            if step == STEPS - 1:
                *da_far, acted_own, acted_other = lax.optimization_barrier(
                    (*da_far, *acted_sent)
                )
                acted_sent = [acted_own, acted_other]
            crossed = [swap(part, 1, 0) for part in da_far[1::2]]
            add("key", dot(far_in, dk_far, TN))
            add("value", dot(far_in, dv_far, TN))
            total["key"], total["value"], *crossed = lax.optimization_barrier(
                (total["key"], total["value"], *crossed)
            )
            summed = [part + other for part, other in zip(da_far[0::2], crossed)]
            sent = [swap(part, 0, (at + 1) * 2) for at, part in enumerate(summed)]
            held = [part_q, total["out"], *summed]
            if step == 0:
                held += [item.piece for item in hidden_sums]
            part_q, total["out"], *pieces = lax.optimization_barrier(tuple(held))
            pieces = pieces[len(summed) :]
            if step == 0:
                for item, piece in zip(hidden_sums, pieces):
                    item.piece = piece
                hidden_sent = [item.start()[0] for item in hidden_sums]
            dq, dk_near, dv_near, near_sums, da_own, da_mate = attend_back(
                queries, grad_mixed, mixed, rest, lse, keys_near, values_near, near_feats, key_weight,
                value_weight, query_feats, part_q, cols,
            )
            small_parts[1].append(near_sums)
            small_parts[2].append(far_sums)
            if step == 0:
                da_mate, dq, dk_near, dv_near, *hidden_sent = lax.optimization_barrier(
                    (da_mate, dq, dk_near, dv_near, *hidden_sent)
                )
            da_mate, *sent = lax.optimization_barrier((da_mate, *sent))
            arrived = swap(da_mate, 1, 0)
            add("key", dot(near_in, dk_near, TN))
            add("value", dot(near_in, dv_near, TN))
            add("query", dot(near_in[: 2 * seq_here], dq, TN))
            if step > 0:
                dq, total["query"], total["key"], total["value"] = lax.optimization_barrier(
                    (dq, total["query"], total["key"], total["value"])
                )
            grad, join_sums = join(
                step, dq, query_weight, da_own, states[step], rows, grad, cols, dh, halt_table,
                cot, sent + [arrived],
            )
            small_parts[3].append(join_sums)

        squares = [total["query"], total["key"], total["value"], total["out"]]
        by_kernel = width % (16 * 2 ** len(bit_names)) == 0
        if by_kernel:
            squares = pack(bit_names, squares)
        else:
            squares = [
                turn(jnp.concatenate(squares[place : place + 2], 1).astype(bf16))
                for place in (0, 2)
            ]
        names = (
            "query_bias", "value_bias", "out_bias", "gain_one", "shift_one", "gain_two",
            "shift_two", "down_bias", "halt",
        )
        small = small_sums(*small_parts, halt_sums).reshape(-1)
        for item, arrived in zip(hidden_sums, hidden_sent):
            item.finish([arrived])
        sums = [
            Scatter(squares[0], [(core_bit,)] + y_order + [(side,)]),
            Scatter(squares[1], [(core_bit,), (side,)] + y_order),
        ]
        small = Small(small, [(core_bit,)] + y_order + [(side,)] + z_order[::-1])
        late = [item.start()[0] for item in hidden_sums]
        (grad,) = together(sums, [grad])
        tokens_back = send_back(grad.astype(bf16))
        late = together(sums + [small], late)
        for item, arrived in zip(hidden_sums, late):
            item.finish([arrived])
        while hidden_sums[0].order:
            together(hidden_sums)
        hidden_all = Scatter(
            jnp.concatenate([item.piece for item in hidden_sums], -1), z_order[::-1], z_bits
        )
        tokens_back = together(sums + [hidden_all, small], tokens_back)
        grad_tokens = unspread(*tokens_back).astype(f32)
        while sums[0].order:
            together(sums + [hidden_all, small])
        both = Scatter(
            jnp.concatenate([item.piece for item in sums], -1), [z_bits], z_bits
        )
        together([both, small])
        both = Gather(both.piece, [z_bits])
        together([both, small])
        sums = [
            Gather(
                both.piece[..., place * 2 * width : (place + 1) * 2 * width],
                order[::-1] + [(core_bit,)],
                [z_bits],
            )
            for place, order in enumerate((y_order + [(side,)], [(side,)] + y_order))
        ]
        together(sums + [hidden_all, small])
        while hidden_all.order:
            together([hidden_all])
        hidden_all = Gather(hidden_all.piece, y_order[::-1] + [(core_bit,)])
        while sums[0].order:
            together(sums + [hidden_all, small])
        while hidden_all.order or small.order:
            together([hidden_all, small])
        small = small.piece
        up_out, up_bias_out, down_out = hidden_out(
            dp_bits, hidden_all.piece.reshape(-1, hidden_part.shape[1]), width
        )
        squares = [item.piece.reshape(width, 2 * width) for item in sums]
        if by_kernel:
            grad_q, grad_k, grad_v, grad_o = unpack(bit_names, squares)
        else:
            grad_q, grad_k, grad_v, grad_o = (
                turn(item)[:, place * width : (place + 1) * width].astype(f32)
                for item in squares
                for place in range(2)
            )
        vectors = {name: small[i * width : (i + 1) * width] for i, name in enumerate(names)}
        return (
            unspread(*acted_sent),
            grad_tokens,
            grad_q,
            vectors["query_bias"],
            grad_k,
            grad_v,
            vectors["value_bias"],
            grad_o,
            vectors["out_bias"],
            vectors["gain_one"],
            vectors["shift_one"],
            vectors["gain_two"],
            vectors["shift_two"],
            up_out,
            up_bias_out[0],
            down_out,
            vectors["down_bias"],
            vectors["halt"],
            small[len(names) * width : len(names) * width + 1],
        )

    return per_device


def solution(mesh):
    shared = P()
    rows = P("dp", "sq", None)
    return jax.shard_map(
        make_per_device(mesh.shape["dp"], mesh.shape["sq"]),
        mesh=mesh,
        in_specs=(rows, P("dp", None), P("dp", None), P("dp", "sq"))
        + (shared,) * 11
        + (P(None, "sq"), P("sq"), P("sq", None), shared, shared, shared, rows),
        out_specs=(rows, rows)
        + (shared,) * 11
        + (P(None, "sq"), P("sq"), P("sq", None), shared, shared, shared),
        check_vma=False,
    )
```
